32 devices in a mesh: group: 4 (over z), sub: 8 (over y, x, core).
Axes of the slice: x: 2, y: 2, z: 4, core: 2. Of those that a mesh axis runs over, the one named last changes fastest.
Arguments:
- load: float32 [8, 512, 256], P(None, ('group', 'sub'))
- row_scale: float32 [512, 256], P(('group', 'sub'))
- diag_blocks: bfloat16 [512, 256, 256], P(('group', 'sub')), may hold values from -0.01184082 to 0.01184082
- off_blocks: bfloat16 [512, 256, 256], P(('group', 'sub')), may hold values from -0.01184082 to 0.01184082
- off_pattern: int32 [32, 16], P(('group', 'sub')), may hold values from 0 to 15, each once within a row
- partner: int32 [32, 16], P(('group', 'sub')), may hold values from 0 to 7, as said below
- corner_coupling: bfloat16 [256, 4096], P(('group', 'sub')), may hold values from -0.375 to 0.375
- corner_index: int32 [4, 64], P('group'), may hold values from 0 to 31
- coarse_inverse: float32 [128, 32], P('group'), as said below
Outputs:
- multipliers: float32 [8, 512, 256], P(None, ('group', 'sub'))
- residual: float32 [8, 512, 256], P(None, ('group', 'sub'))
The draws below stay inside these ranges and needn't reach their ends.
Inputs may be any that keep to these rules, and one draw needn't show every extreme that they name: partner[s, i] is t XOR m for the subdomain s = 8 * grp + t, with m nonzero and depending only on grp and i; so block i of s and block i of its partner share one multiplier. No subdomain shares more than 3 blocks with one other subdomain, and some share exactly 3. `coarse_inverse`: each cluster's block is symmetric and positive definite.
All inputs are finite; a program needn't handle non-finite values.
Results may differ from the reference program's by a relative error of at most 0.012.
The reference program's roundings to bfloat16 on the way (of `scaled` and `local`) count: a program that leaves them out, or rounds other values in their place, can miss the bound.
Values sent between devices are 32-bit elements; how exact they have to be, the bound alone decides.
No kernel may reach another device: no remote copies, remote signals or barrier semaphores. Data moves between devices by JAX's collectives and lax.ppermute only.
A program may use at most 64 MiB of HBM per device.

```python
import jax
import jax.numpy as jnp
from jax import lax

BS = 256
NB = 16
NC = 8
NRHS = 8
ITERS = 4
SUBS = 32
CG = 32
CAP = 3
N_GROUP = 4
N_SUB = 8


def draw_partner(key, part):
    key = jax.random.fold_in(key, 11)

    def one_group(index):
        group_key = jax.random.fold_in(key, index)
        order = jax.random.permutation(jax.random.fold_in(group_key, 1), N_SUB - 1).astype(jnp.int32) + 1
        tiled = jnp.tile(order, CAP)[:NB]
        place = jax.random.permutation(jax.random.fold_in(group_key, 2), NB)
        return tiled[place]
    masks = jax.vmap(one_group)(jnp.arange(N_GROUP, dtype=jnp.int32))
    local = jnp.arange(N_SUB, dtype=jnp.int32)
    mates = jnp.bitwise_xor(local[None, :, None], masks[:, None, :])
    return mates.reshape(N_GROUP * N_SUB, NB).astype(jnp.int32)


def place_in_cluster():
    within = jnp.arange(SUBS * NB, dtype=jnp.int32) // NB % N_SUB
    return within.astype(jnp.float32) / (N_SUB - 1) - 0.5


def draw_load(key, part):
    key = jax.random.fold_in(key, 12)
    place = place_in_cluster()
    base = jax.random.normal(key, (NRHS, SUBS * NB, BS), jnp.float32)
    grow = 3.0 ** place
    return base * grow[None, :, None]


def draw_row_scale(key, part):
    key = jax.random.fold_in(key, 14)
    place = place_in_cluster()
    base = jnp.exp(jax.random.uniform(key, (SUBS * NB, BS), jnp.float32, -0.5, 0.47))
    fall = 3.0 ** (-place)
    return base * fall[:, None]


def draw_coarse_inverse(key, part):
    key = jax.random.fold_in(key, 13)
    reach = 0.9 / CG
    raw = jax.random.uniform(key, (N_GROUP, CG, CG), jnp.float32, -reach, reach)
    mirrored = 0.5 * (raw + jnp.swapaxes(raw, 1, 2))
    eye = jnp.eye(CG, dtype=jnp.float32)[None]
    return (0.5 * (eye + mirrored)).reshape(N_GROUP * CG, CG)


def plant(drawn, rng, least, largest):
    index_at = [jax.random.randint(jax.random.fold_in(rng, axis), (), 0, length) for axis, length in enumerate(drawn.shape)]
    widest = drawn.shape.index(max(drawn.shape))
    beside = index_at[:widest] + [(index_at[widest] + 1) % drawn.shape[widest]] + index_at[widest + 1:]
    return drawn.at[tuple(index_at)].set(least).at[tuple(beside)].set(largest)


def block_scale(stream_key, dims, shards, low, high):
    def one(dim, shards_of):
        heights = jax.random.uniform(jax.random.fold_in(jax.random.fold_in(stream_key, 6), dim), (shards_of,), jnp.float32, low / len(shards), high / len(shards))
        return jnp.repeat(jnp.exp(heights), dims[dim] // shards_of).reshape((-1,) + (1,) * (len(dims) - dim - 1))

    gain = one(*shards[0])
    for cut in shards[1:]:
        gain = gain * one(*cut)
    return gain


def centred(rng, shape, width, most, cuts=(), kind=jnp.bfloat16):
    entries = width * jax.random.normal(rng, shape, jnp.float32)
    if cuts:
        entries = entries * block_scale(rng, shape, cuts, -0.22, 0.18)
    return jnp.clip(entries, -most, most).astype(kind)


def setup_inputs(seed: int = 0) -> dict:
    seeds = jax.random.split(jax.random.key(seed), 10)
    return {
        "load": draw_load(jax.random.fold_in(seeds[9], 71), 0),
        "row_scale": draw_row_scale(jax.random.fold_in(seeds[9], 71), 0),
        "diag_blocks": jnp.clip(jax.random.uniform(seeds[2], (SUBS * NB, BS, BS), jnp.float32, -0.01184082, 0.01184082) * block_scale(seeds[2], (SUBS * NB, BS, BS), ((0, 32),), -0.4, 0.0), -0.01184082, 0.01184082).astype(jnp.bfloat16),
        "off_blocks": jnp.clip(jax.random.uniform(seeds[3], (SUBS * NB, BS, BS), jnp.float32, -0.01184082, 0.01184082) * block_scale(seeds[3], (SUBS * NB, BS, BS), ((0, 32),), -0.4, 0.0), -0.01184082, 0.01184082).astype(jnp.bfloat16),
        "off_pattern": jax.vmap(lambda own: jax.random.permutation(own, NB))(jax.random.split(seeds[4], SUBS)).reshape((SUBS, NB)).astype(jnp.int32),
        "partner": draw_partner(jax.random.fold_in(seeds[9], 71), 0),
        "corner_coupling": centred(seeds[6], (SUBS * NC, NB * BS), BS ** -0.5, 0.375, ((0, 32),)),
        "corner_index": plant(jax.random.randint(seeds[7], (N_GROUP, N_SUB * NC), 0, CG), jax.random.fold_in(seeds[7], 1), 0, CG - 1).astype(jnp.int32),
        "coarse_inverse": draw_coarse_inverse(jax.random.fold_in(seeds[9], 71), 0),
    }


HIGH = lax.Precision.HIGHEST


def couple(args):
    diag, off, sigma, vals = args
    kd = diag.astype(jnp.float32)
    ko = off.astype(jnp.float32)
    values = vals.astype(jnp.float32)
    select = (sigma[:, None] == jnp.arange(NB, dtype=jnp.int32)[None, :]).astype(jnp.float32)
    moved = jnp.einsum("ij,njl->nil", select, values, precision=HIGH)
    total = jnp.einsum("ikl,nil->nik", kd, values, precision=HIGH)
    total = total + jnp.einsum("ilk,nil->nik", kd, values, precision=HIGH)
    total = total + jnp.einsum("ikl,nil->nik", ko, moved, precision=HIGH)
    back = jnp.einsum("ilk,nil->nik", ko, values, precision=HIGH)
    return total + jnp.einsum("ij,nik->njk", select, back, precision=HIGH)


def reference(load, row_scale, diag_blocks, off_blocks, off_pattern, partner, corner_coupling, corner_index, coarse_inverse):
    scale = row_scale.reshape(SUBS, NB, BS)
    diag = diag_blocks.reshape(SUBS, NB, BS, BS)
    off = off_blocks.reshape(SUBS, NB, BS, BS)
    coupling = corner_coupling.reshape(SUBS, NC, NB * BS).astype(jnp.float32)
    base = (jnp.arange(SUBS, dtype=jnp.int32) // N_SUB) * N_SUB
    mate = base[:, None] + partner
    slot = jnp.broadcast_to(jnp.arange(NB, dtype=jnp.int32)[None, :], (SUBS, NB))
    onehot = (corner_index[:, :, None] == jnp.arange(CG, dtype=jnp.int32)[None, None, :]).astype(jnp.float32)
    inverse = coarse_inverse.reshape(N_GROUP, CG, CG)

    def jump(field):
        return field - field[:, mate, slot, :]

    def apply(field):
        scaled = (scale[None] * field).astype(jnp.bfloat16)
        coupled = lax.map(couple, (diag, off, off_pattern, jnp.transpose(scaled, (1, 0, 2, 3))))
        coupled = jnp.transpose(coupled, (1, 0, 2, 3))
        flat = scaled.astype(jnp.float32).reshape(NRHS, SUBS, NB * BS)
        partial_terms = jnp.einsum("scr,nsr->nsc", coupling, flat, precision=HIGH)
        grouped = partial_terms.reshape(NRHS, N_GROUP, N_SUB * NC)
        gathered = jnp.einsum("gjc,ngj->ngc", onehot, grouped, precision=HIGH)
        solved = jnp.einsum("gcd,ngd->ngc", inverse, gathered, precision=HIGH)
        local = jnp.einsum("gjc,ngc->ngj", onehot, solved, precision=HIGH).astype(jnp.bfloat16)
        local = local.reshape(NRHS, SUBS, NC).astype(jnp.float32)
        lifted = jnp.einsum("scr,nsc->nsr", coupling, local, precision=HIGH).reshape(NRHS, SUBS, NB, BS)
        return jump(scale[None] * (scaled.astype(jnp.float32) + coupled + lifted))

    def column(first, second):
        return jnp.sum(first * second, axis=(1, 2, 3))

    field = load.reshape(NRHS, SUBS, NB, BS)
    residual = jump(field)
    multipliers = jnp.zeros_like(residual)
    direction = residual
    norm_now = column(residual, residual)
    for step in range(ITERS):
        product = apply(direction)
        alpha = norm_now / column(direction, product)
        multipliers = multipliers + alpha[:, None, None, None] * direction
        residual = residual - alpha[:, None, None, None] * product
        norm_next = column(residual, residual)
        direction = residual + (norm_next / norm_now)[:, None, None, None] * direction
        norm_now = norm_next
    return multipliers.reshape(NRHS, SUBS * NB, BS), residual.reshape(NRHS, SUBS * NB, BS)
```

```python
import functools

import jax
import jax.numpy as jnp
from jax import lax
from jax.experimental import pallas as pl
from jax.experimental.pallas import tpu as pltpu
from jax.sharding import PartitionSpec as P

ITERS = 4
HIGH = lax.Precision.HIGHEST
F32 = jnp.float32
BF16 = jnp.bfloat16
VMEM = pl.BlockSpec(memory_space=pltpu.VMEM)
SMEM = pl.BlockSpec(memory_space=pltpu.SMEM)
LIMIT = 24 * 1024 * 1024
PAIRS = [(i, j) for j in range(ITERS) for i in range(j + 1)]
ENTRIES = len(PAIRS) + ITERS
NN = (((1,), (0,)), ((), ()))
NT = (((1,), (1,)), ((), ()))
TN = (((0,), (0,)), ((), ()))


def dot(a, b, dims):
    return lax.dot_general(a, b, dims, preferred_element_type=F32)


def dot_high(a, b, dims):
    return lax.dot_general(a, b, dims, precision=HIGH, preferred_element_type=F32)


def split(a):
    high = a.astype(BF16).astype(F32)
    return jnp.concatenate([high, a - high], axis=0).astype(BF16)


def fold(a):
    half = a.shape[0] // 2
    return a[:half] + a[half:]


def lane_ids(shape):
    return lax.broadcasted_iota(jnp.int32, shape, 1)


class Sizes:
    def __init__(self, load, corner_coupling, coarse_inverse, mesh):
        self.columns = load.shape[0]
        self.blocks = load.shape[1]
        self.width = load.shape[2]
        self.corners = corner_coupling.shape[0]
        self.coarse = coarse_inverse.shape[1]
        self.peers = mesh["sub"]
        self.groups = mesh["group"]
        self.capacity = (self.blocks + self.peers - 2) // (self.peers - 1)
        self.all_corners = self.peers * self.corners
        self.max_lane = self.all_corners
        self.gram_lane = self.max_lane + self.peers
        self.extra_chunks = -(-(self.gram_lane + ENTRIES) // self.width)
        self.extra = self.extra_chunks * self.width
        self.masks = range(1, self.peers)
        self.slots = self.peers * self.capacity


def fill_slots(z, partner, slots, counts):
    me = lax.axis_index("sub")
    for entry in range(z.slots):
        slots[entry] = z.blocks
    for m in range(z.peers):
        counts[m] = 0
    for i in range(z.blocks):
        m = partner[0, i] ^ me
        rank = counts[m]
        slots[m * z.capacity + rank] = i
        counts[m] = rank + 1


def send_slots(z, slots, source, outs):
    for m, out in zip(z.masks, outs):
        for r in range(z.capacity):
            block = jnp.minimum(slots[m * z.capacity + r], z.blocks - 1)
            out[r] = source[block]


def place_slots(z, slots, incs, target):
    for m, inc in zip(z.masks, incs):
        for r in range(z.capacity):
            target[slots[m * z.capacity + r]] = inc[r]


def pack_load(z, partner, load, field, *rest):
    outs, (slots, counts) = rest[:-2], rest[-2:]
    fill_slots(z, partner, slots, counts)
    for i in range(z.blocks):
        field[i] = load[:, i, :]
    send_slots(z, slots, field, outs)


def pack_lift(z, partner, scale, coupling, lift, *rest):
    outs, (slots, counts) = rest[:-2], rest[-2:]
    fill_slots(z, partner, slots, counts)
    for i in range(z.blocks):
        part = coupling[:, i * z.width : (i + 1) * z.width].astype(F32)
        lift[i] = scale[i : i + 1, :] * part
    send_slots(z, slots, lift, outs)


def build_coarse(z, partner, index, inverse, lift, *rest):
    count = len(z.masks)
    incs, (operator, jump_lift), (slots, counts, other) = rest[:count], rest[count : count + 2], rest[count + 2 :]
    fill_slots(z, partner, slots, counts)
    place_slots(z, slots, incs, other)
    me = lax.axis_index("sub")
    rows = lax.broadcasted_iota(jnp.int32, (z.coarse, z.all_corners), 0)
    select = (rows == index[...]).astype(F32)
    operator[...] = dot_high(select, dot_high(inverse[...], select, NN), TN)
    own = operator[pl.ds(me * z.corners, z.corners), :]
    for i in range(z.blocks):
        theirs = operator[pl.ds(partner[0, i] * z.corners, z.corners), :]
        left = jnp.concatenate([own, -theirs], axis=0)
        right = jnp.concatenate([lift[i], other[i]], axis=0)
        jump_lift[i] = split(dot_high(left, right, TN))


def extra_sum(z, own, incs):
    total = own[...]
    for inc in incs:
        total = total + jnp.concatenate(
            [inc[z.capacity + j] for j in range(z.extra_chunks)], axis=1
        )
    return total


def cluster_max(z, total):
    lanes = lane_ids(total.shape)
    own = (lanes >= z.max_lane) & (lanes < z.gram_lane)
    return jnp.max(jnp.where(own, total, 0.0), axis=1, keepdims=True)


def corner_rows(z, total):
    rows = split(total[:, : z.all_corners])
    return jnp.concatenate([rows, rows], axis=1)


def lane_sum(a):
    return jnp.sum(a, axis=1, keepdims=True)


def apply_round(z, step, partner, pattern, *rest):
    count = len(z.masks)
    first, last = step == 1, step == ITERS
    rest = list(rest)
    take = lambda n: [rest.pop(0) for _ in range(n)]
    incs = take(count)
    (before,) = take(1)
    if not first:
        own_extra, jump_lift = take(2)
    scale, diag, off, coupling = take(4)
    older = take(ITERS - 1) if last else []
    field, image = take(2)
    if not first:
        (total_out,) = take(1)
    (extra,) = take(1)
    outs = take(count)
    slots, counts, inverse, other, parts = rest
    fill_slots(z, partner, slots, counts)
    for j in range(z.blocks):
        inverse[pattern[0, j]] = j
    place_slots(z, slots, incs, other)
    if not first:
        total = extra_sum(z, own_extra, incs)
        total_out[...] = total
        rows = corner_rows(z, total)
        shrink = 1.0 / cluster_max(z, total)
    for i in range(z.blocks):
        value = before[i] - other[i]
        if not first:
            value = (value + fold(dot(rows, jump_lift[i], NN))) * shrink
        field[i] = value
        parts[i] = split(scale[i : i + 1, :] * value)
    partial = jnp.zeros((2 * z.columns, z.corners), F32)
    top = jnp.zeros((z.columns, z.width), F32)
    for i in range(z.blocks):
        mine = parts[i]
        partial = partial + dot(mine, coupling[:, i * z.width : (i + 1) * z.width], NT)
        source = inverse[i]
        coupled = dot(mine, diag[i], NT) + dot(mine, diag[i], NN)
        coupled = coupled + dot(parts[pattern[0, i]], off[i], NT)
        coupled = coupled + dot(parts[source], off[source], NN)
        row = scale[i : i + 1, :]
        result = row * (row * field[i] + fold(coupled))
        image[i] = result
        top = jnp.maximum(top, jnp.abs(result))
    send_slots(z, slots, image, outs)
    me = lax.axis_index("sub")
    lanes = lane_ids((z.columns, z.extra))
    sums = fold(partial)
    padded = jnp.concatenate(
        [sums, jnp.zeros((z.columns, z.extra - z.corners), F32)], axis=1
    )
    tile = pltpu.roll(padded, me * z.corners, 1)
    tile = jnp.where(lanes == z.max_lane + me, jnp.max(top, axis=1, keepdims=True), tile)
    if last:
        fields = older + [field]
        products = [(fields[i], fields[j]) for i, j in PAIRS] + [(f, image) for f in fields]
        for entry, (a, b) in enumerate(products):
            acc = a[0] * b[0]
            for i in range(1, z.blocks):
                acc = acc + a[i] * b[i]
            tile = jnp.where(lanes == z.gram_lane + entry, lane_sum(acc), tile)
    extra[...] = tile
    for out in outs:
        for j in range(z.extra_chunks):
            out[z.capacity + j] = tile[:, j * z.width : (j + 1) * z.width]


def cluster_gram(z, operator, own_extra, *rest):
    count = len(z.masks)
    incs, totals, (gram,) = rest[:count], rest[count:-1], rest[-1:]
    total = extra_sum(z, own_extra, incs)
    totals = [t[...] for t in totals]
    partials = [t[:, : z.all_corners] for t in totals + [total]]
    lifted = dot_high(partials[-1], operator[...], NT)
    lanes = lane_ids(gram.shape)
    tile = jnp.zeros(gram.shape, F32)
    for entry in range(ENTRIES):
        lane = z.gram_lane + entry
        value = total[:, lane : lane + 1]
        if entry >= len(PAIRS):
            value = 2.0 * (value + lane_sum(partials[entry - len(PAIRS)] * lifted))
        tile = jnp.where(lanes == entry, value, tile)
    for step, t in enumerate(totals):
        tile = jnp.where(lanes == ENTRIES + step, cluster_max(z, t), tile)
    gram[...] = tile


def finish(z, partner, *rest):
    count = len(z.masks)
    rest = list(rest)
    take = lambda n: [rest.pop(0) for _ in range(n)]
    grams = take(z.groups)
    incs = take(count)
    before, own_extra, jump_lift = take(3)
    fields = take(ITERS)
    multipliers, residual = take(2)
    slots, counts, other, tiles = rest
    here = lax.axis_index("group")
    for k, gram in enumerate(grams):
        tiles[lax.rem(here + z.groups - k, z.groups)] = gram[...]
    total = extra_sum(z, own_extra, incs)
    rows = corner_rows(z, total)
    fill_slots(z, partner, slots, counts)
    place_slots(z, slots, incs, other)

    tables = [tiles[g] for g in range(z.groups)]
    mine = grams[0][...]
    one = jnp.ones((z.columns, 1), F32)
    ratio = [[one] * z.groups]
    own_ratio = [one]
    growth = [None]
    for step in range(1, ITERS + 1):
        if step < ITERS:
            lane = ENTRIES + step - 1
            grown = [q * t[:, lane : lane + 1] for q, t in zip(ratio[-1], tables)]
            own = own_ratio[-1] * mine[:, lane : lane + 1]
        else:
            grown, own = ratio[-1], own_ratio[-1]
        top = functools.reduce(jnp.maximum, grown)
        ratio.append([q / top for q in grown])
        own_ratio.append(own / top)
        growth.append(top)
    gram = {}
    pairs = PAIRS + [(i, ITERS) for i in range(ITERS)]
    for entry, (i, j) in enumerate(pairs):
        value = 0.0
        for g in range(z.groups):
            value = value + ratio[i][g] * ratio[j][g] * tables[g][:, entry : entry + 1]
        gram[i, j] = gram[j, i] = value

    def inner(a, b):
        return sum(a[i] * sum(gram[i, j] * b[j] for j in b) for i in a)

    def add(a, weight, b):
        out = dict(a)
        for i, value in b.items():
            out[i] = out[i] + weight * value if i in out else weight * value
        return out

    rest_of, way, found = {0: one}, {0: one}, {}
    norm = gram[0, 0]
    for step in range(ITERS):
        product = {i + 1: growth[i + 1] * value for i, value in way.items()}
        alpha = norm / inner(way, product)
        found = add(found, alpha, way)
        rest_of = add(rest_of, -alpha, product)
        if step < ITERS - 1:
            following = inner(rest_of, rest_of)
            way = add(rest_of, following / norm, way)
            norm = following
    found = {i: value * own_ratio[i] for i, value in found.items()}
    rest_of = {i: value * own_ratio[i] for i, value in rest_of.items()}
    for i in range(z.blocks):
        newest = before[i] - other[i] + fold(dot(rows, jump_lift[i], NN))
        values = [f[i] for f in fields] + [newest]
        multipliers[:, i, :] = sum(c * values[j] for j, c in found.items())
        residual[:, i, :] = sum(c * values[j] for j, c in rest_of.items())


def call(body, outs, scratch, cost, args, scalars=1):
    specs = [SMEM] * scalars + [VMEM] * (len(args) - scalars)
    return pl.pallas_call(
        body,
        out_shape=[jax.ShapeDtypeStruct(s, t) for s, t in outs],
        in_specs=specs,
        out_specs=[VMEM] * len(outs),
        scratch_shapes=scratch,
        compiler_params=pltpu.CompilerParams(vmem_limit_bytes=LIMIT),
        cost_estimate=pl.CostEstimate(flops=cost, bytes_accessed=cost // 16, transcendentals=0),
    )(*args)


def on_device(
    load,
    row_scale,
    diag_blocks,
    off_blocks,
    off_pattern,
    partner,
    corner_coupling,
    corner_index,
    coarse_inverse,
    *,
    mesh,
):
    z = Sizes(load, corner_coupling, coarse_inverse, mesh)
    cols, blocks, width = z.columns, z.blocks, z.width
    count = len(z.masks)
    field = ((blocks, cols, width), F32)
    tables = [pltpu.SMEM((z.slots,), jnp.int32), pltpu.SMEM((z.peers,), jnp.int32)]
    inverse = pltpu.SMEM((blocks,), jnp.int32)
    other = pltpu.VMEM((blocks + 1, cols, width), F32)
    parts = pltpu.VMEM((blocks, 2 * cols, width), BF16)
    plain = ((z.capacity, cols, width), F32)
    lift_piece = ((z.capacity, z.corners, width), F32)
    full = ((z.capacity + z.extra_chunks, cols, width), F32)
    extra = ((cols, z.extra), F32)
    gram = ((cols, 128), F32)
    light, heavy = 4_000_000, 600_000_000

    def swap(pieces):
        return [
            lax.ppermute(piece, "sub", [(t, t ^ m) for t in range(z.peers)])
            for m, piece in zip(z.masks, pieces)
        ]

    def kernel(body, *extra_args):
        return functools.partial(body, z, *extra_args)

    loaded, *pieces = call(
        kernel(pack_load), [field] + [plain] * count, tables, light,
        [partner, load],
    )
    incs = swap(pieces)
    lift, *pieces = call(
        kernel(pack_lift),
        [((blocks, z.corners, width), F32)] + [lift_piece] * count,
        tables, light, [partner, row_scale, corner_coupling],
    )
    lifts = swap(pieces)

    weights = [row_scale, diag_blocks, off_blocks, corner_coupling]
    scratch = tables + [inverse, other, parts]
    newest, image, own_extra, *pieces = call(
        kernel(apply_round, 1), [field, field, extra] + [full] * count, scratch, heavy,
        [partner, off_pattern, *incs, loaded, *weights], 2,
    )
    incs = swap(pieces)
    operator, jump_lift = call(
        kernel(build_coarse),
        [
            ((z.all_corners, z.all_corners), F32),
            ((blocks, 2 * z.all_corners, width), BF16),
        ],
        tables + [pltpu.VMEM((blocks + 1, z.corners, width), F32)],
        heavy,
        [partner, corner_index, coarse_inverse, lift, *lifts],
    )
    fields, totals = [newest], []
    for step in range(2, ITERS + 1):
        older = fields if step == ITERS else []
        newest, image, total, own_extra, *pieces = call(
            kernel(apply_round, step),
            [field, field, extra, extra] + [full] * count, scratch, heavy,
            [partner, off_pattern, *incs, image, own_extra, jump_lift, *weights, *older], 2,
        )
        fields.append(newest)
        totals.append(total)
        incs = swap(pieces)
    (own_gram,) = call(
        kernel(cluster_gram), [gram], [], light, [operator, own_extra, *incs, *totals], 0
    )
    grams = [own_gram] + [
        lax.ppermute(own_gram, "group", [(a, (a + k) % z.groups) for a in range(z.groups)])
        for k in range(1, z.groups)
    ]
    flat = (load.shape, F32)
    multipliers, residual = call(
        kernel(finish), [flat, flat],
        tables + [other, pltpu.VMEM((z.groups, cols, 128), F32)], light,
        [partner, *grams, *incs, image, own_extra, jump_lift, *fields],
    )
    return multipliers, residual


def solution(mesh):
    return jax.shard_map(
        functools.partial(on_device, mesh=dict(mesh.shape)),
        mesh=mesh,
        in_specs=(
            P(None, ("group", "sub"), None),
            P(("group", "sub"), None),
            P(("group", "sub"), None, None),
            P(("group", "sub"), None, None),
            P(("group", "sub"), None),
            P(("group", "sub"), None),
            P(("group", "sub"), None),
            P("group", None),
            P("group", None),
        ),
        out_specs=(P(None, ("group", "sub"), None), P(None, ("group", "sub"), None)),
        check_vma=False,
    )
```

```python
import functools

import jax
import jax.numpy as jnp
from jax import lax
from jax.experimental import pallas as pl
from jax.experimental.pallas import tpu as pltpu
from jax.sharding import PartitionSpec as P

ITERS = 4
HIGH = lax.Precision.HIGHEST
F32 = jnp.float32
BF16 = jnp.bfloat16
VMEM = pl.BlockSpec(memory_space=pltpu.VMEM)
SMEM = pl.BlockSpec(memory_space=pltpu.SMEM)
HBM = pl.BlockSpec(memory_space=pltpu.HBM)
LIMIT = 24 * 1024 * 1024
PAIRS = [(i, j) for j in range(ITERS) for i in range(j + 1)]
ENTRIES = len(PAIRS) + ITERS
NN = (((1,), (0,)), ((), ()))
NT = (((1,), (1,)), ((), ()))
TN = (((0,), (0,)), ((), ()))


def dot(a, b, dims):
    return lax.dot_general(a, b, dims, preferred_element_type=F32)


def dot_high(a, b, dims):
    return lax.dot_general(a, b, dims, precision=HIGH, preferred_element_type=F32)


def split(a):
    high = a.astype(BF16).astype(F32)
    return jnp.concatenate([high, a - high], axis=0).astype(BF16)


def fold(a):
    half = a.shape[0] // 2
    return a[:half] + a[half:]


def lane_ids(shape):
    return lax.broadcasted_iota(jnp.int32, shape, 1)


class Sizes:
    def __init__(self, load, corner_coupling, coarse_inverse, mesh):
        self.columns = load.shape[0]
        self.blocks = load.shape[1]
        self.width = load.shape[2]
        self.corners = corner_coupling.shape[0]
        assert self.corners == self.columns
        self.coarse = coarse_inverse.shape[1]
        self.peers = mesh["sub"]
        self.groups = mesh["group"]
        self.capacity = (self.blocks + self.peers - 2) // (self.peers - 1)
        self.all_corners = self.peers * self.corners
        self.max_lane = self.all_corners
        self.gram_lane = self.max_lane + self.peers
        self.extra_chunks = -(-(self.gram_lane + ENTRIES) // self.width)
        self.extra = self.extra_chunks * self.width
        self.far = range(2, self.peers, 2)
        self.odd = range(1, self.peers, 2)
        self.slots = self.peers * self.capacity
        self.inverse = self.slots
        self.pattern = self.inverse + self.blocks
        self.partner = self.pattern + self.blocks
        self.table = self.partner + self.blocks

    def near_rows(self, kinds):
        return len(self.odd) * kinds * self.capacity

    def far_rows(self, kinds):
        return 2 * kinds * self.capacity


def fill_table(z, partner, pattern, table, counts):
    me = lax.axis_index("sub")
    for entry in range(z.slots):
        table[entry] = z.blocks
    for m in range(z.peers):
        counts[m] = 0
    for i in range(z.blocks):
        mate = partner[0, i]
        source = pattern[0, i]
        m = mate ^ me
        rank = counts[m]
        table[m * z.capacity + rank] = i
        counts[m] = rank + 1
        table[z.inverse + source] = i
        table[z.pattern + i] = source
        table[z.partner + i] = mate


def block_of(z, table, m, r):
    return jnp.minimum(table[m * z.capacity + r], z.blocks - 1)


def fill_near(z, table, sources, near):
    row = 0
    for m in z.odd:
        for source in sources:
            for r in range(z.capacity):
                near[row] = source[block_of(z, table, m, r)]
                row += 1


def place(z, table, near, fars, kind, kinds, target):
    for r in range(z.capacity):
        target[table[z.capacity + r]] = near[kind * z.capacity + r]
    for m, far in zip(z.far, fars):
        for r in range(z.capacity):
            row = 2 * kind * z.capacity + r
            target[table[m * z.capacity + r]] = far[row]
            target[table[(m + 1) * z.capacity + r]] = far[row + z.capacity]


def begin(z, partner, pattern, load, scale, coupling, table, field, lift, scale_out, coupling_out, near, *scratch):
    here, partner_here, pattern_here, counts, sems = scratch
    copies = [
        pltpu.make_async_copy(a, b, sems.at[k])
        for k, (a, b) in enumerate(
            [
                (partner, partner_here),
                (pattern, pattern_here),
                (load, here),
                (scale, scale_out),
                (coupling, coupling_out),
            ]
        )
    ]
    for copy in copies:
        copy.start()
    copies[0].wait()
    copies[1].wait()
    fill_table(z, partner_here, pattern_here, table, counts)
    for copy in copies[2:]:
        copy.wait()
    for i in range(z.blocks):
        field[i] = here[:, i, :]
        part = coupling_out[:, i * z.width : (i + 1) * z.width].astype(F32)
        lift[i] = scale_out[i : i + 1, :] * part
    fill_near(z, table, [field, lift], near)


def relay(z, kinds, table, *rest):
    sources, rest = rest[:kinds], rest[kinds:]
    extras = z.extra_chunks if kinds == 1 else 0
    if extras:
        own_extra, rest = rest[0], rest[1:]
    near, fars = rest[0], rest[1:]
    for m, far in zip(z.far, fars):
        for kind, source in enumerate(sources):
            row = 2 * kind * z.capacity
            base = (m // 2 * kinds + kind) * z.capacity
            for r in range(z.capacity):
                far[row + r] = source[block_of(z, table, m, r)]
                far[row + z.capacity + r] = near[base + r]
    for j in range(extras):
        chunk = own_extra[:, j * z.width : (j + 1) * z.width] + near[z.near_rows(1) + j]
        for far in fars:
            far[z.far_rows(1) + j] = chunk


def split3(a):
    high = a.astype(BF16).astype(F32)
    middle = (a - high).astype(BF16).astype(F32)
    return [high, middle, a - high - middle]


def build_operator(z, index, inverse, operator):
    rows = lax.broadcasted_iota(jnp.int32, (z.coarse, z.all_corners), 0)
    select = (rows == index[...]).astype(BF16)
    parts = jnp.concatenate(split3(inverse[...]), axis=0).astype(BF16)
    half = dot(parts, select, NN)
    half = sum(half[k * z.coarse : (k + 1) * z.coarse] for k in range(3))
    parts = jnp.concatenate(split3(half), axis=1).astype(BF16)
    full = dot(select, parts, TN)
    operator[...] = sum(full[:, k * z.all_corners : (k + 1) * z.all_corners] for k in range(3))


def build_lift(z, table, operator, lift, near, *rest):
    fars, (jump_lift, other) = rest[:-2], rest[-2:]
    place(z, table, near, fars, 1, 2, other)
    me = lax.axis_index("sub")
    own = operator[pl.ds(pl.multiple_of(me * z.corners, z.corners), z.corners), :]
    for i in range(z.blocks):
        at = pl.multiple_of(table[z.partner + i] * z.corners, z.corners)
        left = split(jnp.concatenate([own, -operator[pl.ds(at, z.corners), :]], axis=0))
        right = split(jnp.concatenate([lift[i], other[i]], axis=0))
        count = 2 * z.corners
        left = jnp.concatenate([left, left[:count]], axis=0)
        right = jnp.concatenate([right[:count], right[:count], right[count:]], axis=0)
        jump_lift[i] = split(dot(left, right, TN))


def extra_sum(z, own, near, fars):
    def read(ref, row):
        return jnp.concatenate([ref[row + j] for j in range(z.extra_chunks)], axis=1)

    total = own[...] + read(near, z.near_rows(1))
    for far in fars:
        total = total + read(far, z.far_rows(1))
    return total


def cluster_max(z, total):
    lanes = lane_ids(total.shape)
    own = (lanes >= z.max_lane) & (lanes < z.gram_lane)
    return jnp.max(jnp.where(own, total, 0.0), axis=1, keepdims=True)


def corner_rows(z, total):
    rows = split(total[:, : z.all_corners])
    return jnp.concatenate([rows, rows], axis=1)


def lane_sum(a):
    return jnp.sum(a, axis=1, keepdims=True)


def apply_round(z, step, table, *rest):
    count = len(z.far)
    first, last = step == 1, step == ITERS
    rest = list(rest)
    take = lambda n: [rest.pop(0) for _ in range(n)]
    near, *fars = take(1 + count)
    (before,) = take(1)
    if not first:
        own_extra, jump_lift = take(2)
    scale, diag, off, coupling = take(4)
    older = take(ITERS - 1) if last else []
    field, image = take(2)
    if first:
        sources, (diag, off) = (diag, off), take(2)
    else:
        (total_out,) = take(1)
    extra, near_out = take(2)
    other, parts = take(2)
    if first:
        (sems,) = rest
        copies = [
            [
                pltpu.make_async_copy(a.at[i], b.at[i], sems.at[k, i])
                for k, (a, b) in enumerate(zip(sources, (diag, off)))
            ]
            for i in range(z.blocks)
        ]
        for pair in copies:
            for copy in pair:
                copy.start()
    place(z, table, near, fars, 0, 2 if first else 1, other)
    if not first:
        total = extra_sum(z, own_extra, near, fars)
        total_out[...] = total
        rows = corner_rows(z, total)
        shrink = 1.0 / cluster_max(z, total)
    for i in range(z.blocks):
        value = before[i] - other[i]
        if not first:
            value = (value + fold(dot(rows, jump_lift[i], NN))) * shrink
        field[i] = value
        parts[i] = split(scale[i : i + 1, :] * value)
    if first:
        for pair in copies:
            for copy in pair:
                copy.wait()
    partial = jnp.zeros((2 * z.columns, z.corners), F32)
    top = jnp.zeros((z.columns, z.width), F32)
    for i in range(z.blocks):
        mine = parts[i]
        partial = partial + dot(mine, coupling[:, i * z.width : (i + 1) * z.width], NT)
        source = table[z.inverse + i]
        coupled = dot(mine, diag[i], NT) + dot(mine, diag[i], NN)
        coupled = coupled + dot(parts[table[z.pattern + i]], off[i], NT)
        coupled = coupled + dot(parts[source], off[source], NN)
        row = scale[i : i + 1, :]
        result = row * (row * field[i] + fold(coupled))
        image[i] = result
        top = jnp.maximum(top, jnp.abs(result))
    fill_near(z, table, [image], near_out)
    me = lax.axis_index("sub")
    lanes = lane_ids((z.columns, z.extra))
    sums = fold(partial)
    padded = jnp.concatenate(
        [sums, jnp.zeros((z.columns, z.extra - z.corners), F32)], axis=1
    )
    tile = pltpu.roll(padded, me * z.corners, 1)
    tile = jnp.where(lanes == z.max_lane + me, jnp.max(top, axis=1, keepdims=True), tile)
    if last:
        fields = older + [field]
        products = [(fields[i], fields[j]) for i, j in PAIRS] + [(f, image) for f in fields]
        for entry, (a, b) in enumerate(products):
            acc = a[0] * b[0]
            for i in range(1, z.blocks):
                acc = acc + a[i] * b[i]
            tile = jnp.where(lanes == z.gram_lane + entry, lane_sum(acc), tile)
    extra[...] = tile
    for j in range(z.extra_chunks):
        near_out[z.near_rows(1) + j] = tile[:, j * z.width : (j + 1) * z.width]


def cluster_gram(z, operator, own_extra, near, *rest):
    count = len(z.far)
    fars, totals, (gram,) = rest[:count], rest[count:-1], rest[-1:]
    total = extra_sum(z, own_extra, near, fars)
    totals = [t[...] for t in totals]
    partials = [t[:, : z.all_corners] for t in totals + [total]]
    lifted = dot_high(partials[-1], operator[...], NT)
    lanes = lane_ids(gram.shape)
    tile = jnp.zeros(gram.shape, F32)
    for entry in range(ENTRIES):
        lane = z.gram_lane + entry
        value = total[:, lane : lane + 1]
        if entry >= len(PAIRS):
            value = 2.0 * (value + lane_sum(partials[entry - len(PAIRS)] * lifted))
        tile = jnp.where(lanes == entry, value, tile)
    for step, t in enumerate(totals):
        tile = jnp.where(lanes == ENTRIES + step, cluster_max(z, t), tile)
    gram[...] = tile


def last_vector(z, table, before, own_extra, jump_lift, near, *rest):
    fars, (field, other) = rest[:-2], rest[-2:]
    place(z, table, near, fars, 0, 1, other)
    rows = corner_rows(z, extra_sum(z, own_extra, near, fars))
    for i in range(z.blocks):
        field[i] = before[i] - other[i] + fold(dot(rows, jump_lift[i], NN))


def finish(z, *rest):
    grams, rest = rest[: z.groups], rest[z.groups :]
    fields, (multipliers, residual) = rest[:-2], rest[-2:]
    tables = [gram[...] for gram in grams]
    mine = tables[0]
    one = jnp.ones((z.columns, 1), F32)
    ratio = [[one] * z.groups]
    own_ratio = [one]
    growth = [None]
    for step in range(1, ITERS + 1):
        if step < ITERS:
            lane = ENTRIES + step - 1
            grown = [q * t[:, lane : lane + 1] for q, t in zip(ratio[-1], tables)]
            own = own_ratio[-1] * mine[:, lane : lane + 1]
        else:
            grown, own = ratio[-1], own_ratio[-1]
        top = functools.reduce(jnp.maximum, grown)
        ratio.append([q / top for q in grown])
        own_ratio.append(own / top)
        growth.append(top)
    gram = {}
    pairs = PAIRS + [(i, ITERS) for i in range(ITERS)]
    for entry, (i, j) in enumerate(pairs):
        value = 0.0
        for g in range(z.groups):
            value = value + ratio[i][g] * ratio[j][g] * tables[g][:, entry : entry + 1]
        gram[i, j] = gram[j, i] = value

    def inner(a, b):
        return sum(a[i] * sum(gram[i, j] * b[j] for j in b) for i in a)

    def add(a, weight, b):
        out = dict(a)
        for i, value in b.items():
            out[i] = out[i] + weight * value if i in out else weight * value
        return out

    rest_of, way, found = {0: one}, {0: one}, {}
    norm = gram[0, 0]
    for step in range(ITERS):
        product = {i + 1: growth[i + 1] * value for i, value in way.items()}
        alpha = norm / inner(way, product)
        found = add(found, alpha, way)
        rest_of = add(rest_of, -alpha, product)
        if step < ITERS - 1:
            following = inner(rest_of, rest_of)
            way = add(rest_of, following / norm, way)
            norm = following
    found = {i: value * own_ratio[i] for i, value in found.items()}
    rest_of = {i: value * own_ratio[i] for i, value in rest_of.items()}
    for i in range(z.blocks):
        values = [f[i] for f in fields]
        multipliers[:, i, :] = sum(c * values[j] for j, c in found.items())
        residual[:, i, :] = sum(c * values[j] for j, c in rest_of.items())


def call(body, outs, scratch, cost, args, table=True, away=(), table_out=False):
    specs = [HBM if k in away else VMEM for k in range(len(args))]
    if table:
        specs[0] = SMEM
    out_specs = [VMEM] * len(outs)
    if table_out:
        out_specs[0] = SMEM
    return pl.pallas_call(
        body,
        out_shape=[jax.ShapeDtypeStruct(s, t) for s, t in outs],
        in_specs=specs,
        out_specs=out_specs,
        scratch_shapes=scratch,
        compiler_params=pltpu.CompilerParams(vmem_limit_bytes=LIMIT),
        cost_estimate=pl.CostEstimate(flops=cost, bytes_accessed=cost // 16, transcendentals=0),
    )(*args)


def on_device(
    load,
    row_scale,
    diag_blocks,
    off_blocks,
    off_pattern,
    partner,
    corner_coupling,
    corner_index,
    coarse_inverse,
    *,
    mesh,
):
    z = Sizes(load, corner_coupling, coarse_inverse, mesh)
    cols, blocks, width = z.columns, z.blocks, z.width
    field = ((blocks, cols, width), F32)
    other = pltpu.VMEM((blocks + 1, cols, width), F32)
    parts = pltpu.VMEM((blocks, 2 * cols, width), BF16)
    extra = ((cols, z.extra), F32)
    gram = ((cols, 128), F32)
    light, heavy = 4_000_000, 600_000_000

    def near_shape(kinds):
        return ((z.near_rows(kinds) + (z.extra_chunks if kinds == 1 else 0), cols, width), F32)

    def far_shape(kinds):
        return ((z.far_rows(kinds) + (z.extra_chunks if kinds == 1 else 0), cols, width), F32)

    def kernel(body, *extra_args):
        return functools.partial(body, z, *extra_args)

    def across(piece, m):
        return lax.ppermute(piece, "sub", [(t, t ^ m) for t in range(z.peers)])

    def exchange(near, sources):
        kinds = 1 if len(sources) == 1 else 2
        near = across(near, 1)
        own = [own_extra] if kinds == 1 else []
        pieces = call(
            kernel(relay, kinds), [far_shape(kinds)] * len(z.far), [], light,
            [table, *sources, *own, near],
        )
        return [near] + [across(piece, m) for m, piece in zip(z.far, pieces)]

    table, loaded, lift, scale, coupling, near = call(
        kernel(begin),
        [
            ((z.table,), jnp.int32),
            field,
            field,
            (row_scale.shape, F32),
            (corner_coupling.shape, BF16),
            near_shape(2),
        ],
        [
            pltpu.VMEM(load.shape, F32),
            pltpu.SMEM(partner.shape, jnp.int32),
            pltpu.SMEM(off_pattern.shape, jnp.int32),
            pltpu.SMEM((z.peers,), jnp.int32),
            pltpu.SemaphoreType.DMA((5,)),
        ],
        light,
        [partner, off_pattern, load, row_scale, corner_coupling],
        False, range(5), True,
    )
    arrived = exchange(near, [loaded, lift])
    (operator,) = call(
        kernel(build_operator), [((z.all_corners, z.all_corners), F32)], [], light,
        [corner_index, coarse_inverse], False,
    )
    weight = (diag_blocks.shape, BF16)
    newest, image, diag, off, own_extra, near = call(
        kernel(apply_round, 1),
        [field, field, weight, weight, extra, near_shape(1)],
        [other, parts, pltpu.SemaphoreType.DMA((2, blocks))], heavy,
        [table, *arrived, loaded, scale, diag_blocks, off_blocks, coupling],
        True, (len(arrived) + 3, len(arrived) + 4),
    )
    (jump_lift,) = call(
        kernel(build_lift), [((blocks, 2 * z.all_corners, width), BF16)], [other], heavy,
        [table, operator, lift, *arrived],
    )
    arrived = exchange(near, [image])
    fields, totals = [newest], []
    for step in range(2, ITERS + 1):
        older = fields if step == ITERS else []
        newest, image, total, own_extra, near = call(
            kernel(apply_round, step),
            [field, field, extra, extra, near_shape(1)], [other, parts], heavy,
            [table, *arrived, image, own_extra, jump_lift, scale, diag, off, coupling, *older],
        )
        fields.append(newest)
        totals.append(total)
        arrived = exchange(near, [image])
    (own_gram,) = call(
        kernel(cluster_gram), [gram], [], light, [operator, own_extra, *arrived, *totals], False
    )
    power = z.groups & (z.groups - 1) == 0
    grams = [own_gram] + [
        lax.ppermute(
            own_gram, "group",
            [(a, a ^ k if power else (a + k) % z.groups) for a in range(z.groups)],
        )
        for k in range(1, z.groups)
    ]
    (newest,) = call(
        kernel(last_vector), [field], [other], light,
        [table, image, own_extra, jump_lift, *arrived],
    )
    multipliers, residual = call(
        kernel(finish), [(load.shape, F32)] * 2, [], light, [*grams, *fields, newest], False
    )
    return multipliers, residual


def solution(mesh):
    return jax.shard_map(
        functools.partial(on_device, mesh=dict(mesh.shape)),
        mesh=mesh,
        in_specs=(
            P(None, ("group", "sub"), None),
            P(("group", "sub"), None),
            P(("group", "sub"), None, None),
            P(("group", "sub"), None, None),
            P(("group", "sub"), None),
            P(("group", "sub"), None),
            P(("group", "sub"), None),
            P("group", None),
            P("group", None),
        ),
        out_specs=(P(None, ("group", "sub"), None), P(None, ("group", "sub"), None)),
        check_vma=False,
    )
```

```python
import functools

import jax
import jax.numpy as jnp
from jax import lax
from jax.experimental import pallas as pl
from jax.experimental.pallas import tpu as pltpu
from jax.sharding import PartitionSpec as P

ITERS = 4
HIGH = lax.Precision.HIGHEST
F32 = jnp.float32
BF16 = jnp.bfloat16
VMEM = pl.BlockSpec(memory_space=pltpu.VMEM)
SMEM = pl.BlockSpec(memory_space=pltpu.SMEM)
HBM = pl.BlockSpec(memory_space=pltpu.HBM)
LIMIT = 24 * 1024 * 1024
LANES = 128
PAIRS = [(i, j) for j in range(ITERS) for i in range(j + 1)]
ENTRIES = len(PAIRS) + ITERS
NN = (((1,), (0,)), ((), ()))
NT = (((1,), (1,)), ((), ()))
TN = (((0,), (0,)), ((), ()))


def dot(a, b, dims):
    return lax.dot_general(a, b, dims, preferred_element_type=F32)


def dot_high(a, b, dims):
    return lax.dot_general(a, b, dims, precision=HIGH, preferred_element_type=F32)


def split(a):
    high = a.astype(BF16).astype(F32)
    return jnp.concatenate([high, a - high], axis=0).astype(BF16)


def fold(a):
    half = a.shape[0] // 2
    return a[:half] + a[half:]


def lane_ids(shape):
    return lax.broadcasted_iota(jnp.int32, shape, 1)


class Sizes:
    def __init__(self, load, corner_coupling, coarse_inverse, mesh):
        self.columns = load.shape[0]
        self.blocks = load.shape[1]
        self.width = load.shape[2]
        self.corners = corner_coupling.shape[0]
        assert self.corners == self.columns
        self.coarse = coarse_inverse.shape[1]
        self.peers = mesh["sub"]
        self.groups = mesh["group"]
        self.capacity = (self.blocks + self.peers - 2) // (self.peers - 1)
        self.all_corners = self.peers * self.corners
        self.max_lane = self.all_corners
        self.gram_lane = self.max_lane + self.peers
        self.extra_chunks = -(-(self.gram_lane + ENTRIES) // LANES)
        self.extra = self.extra_chunks * LANES
        self.halves = self.width // LANES
        self.masks = range(self.peers - 1, 0, -1)
        self.slots = self.peers * self.capacity
        self.inverse = self.slots
        self.pattern = self.inverse + self.blocks
        self.partner = self.pattern + self.blocks
        self.table = self.partner + self.blocks

    def rows(self, kinds):
        return kinds * self.capacity * self.halves


def fill_table(z, partner, pattern, table, counts):
    me = lax.axis_index("sub")
    for entry in range(z.slots):
        table[entry] = z.blocks
    for m in range(z.peers):
        counts[m] = 0
    for i in range(z.blocks):
        mate = partner[0, i]
        source = pattern[0, i]
        m = mate ^ me
        rank = counts[m]
        table[m * z.capacity + rank] = i
        counts[m] = rank + 1
        table[z.inverse + source] = i
        table[z.pattern + i] = source
        table[z.partner + i] = mate


def fill_pieces(z, table, sources, pieces):
    for m, piece in zip(z.masks, pieces):
        row = 0
        for source in sources:
            for r in range(z.capacity):
                block = jnp.minimum(table[m * z.capacity + r], z.blocks - 1)
                value = source[block]
                for h in range(z.halves):
                    piece[row] = value[:, h * LANES : (h + 1) * LANES]
                    row += 1


def place(z, table, pieces, kind, target):
    for m, piece in zip(z.masks, pieces):
        row = z.rows(kind)
        for r in range(z.capacity):
            block = table[m * z.capacity + r]
            for h in range(z.halves):
                target[block, :, h * LANES : (h + 1) * LANES] = piece[row]
                row += 1


def begin(z, partner, pattern, load, scale, coupling, table, field, lift, scale_out, coupling_out, *rest):
    pieces, (here, partner_here, pattern_here, counts, sems) = rest[:-5], rest[-5:]
    copies = [
        pltpu.make_async_copy(a, b, sems.at[k])
        for k, (a, b) in enumerate(
            [
                (partner, partner_here),
                (pattern, pattern_here),
                (load, here),
                (scale, scale_out),
                (coupling, coupling_out),
            ]
        )
    ]
    for copy in copies:
        copy.start()
    copies[0].wait()
    copies[1].wait()
    fill_table(z, partner_here, pattern_here, table, counts)
    for copy in copies[2:]:
        copy.wait()
    for i in range(z.blocks):
        field[i] = here[:, i, :]
        part = coupling_out[:, i * z.width : (i + 1) * z.width].astype(F32)
        lift[i] = scale_out[i : i + 1, :] * part
    fill_pieces(z, table, [field, lift], pieces)


def split3(a):
    high = a.astype(BF16).astype(F32)
    middle = (a - high).astype(BF16).astype(F32)
    return [high, middle, a - high - middle]


def build_operator(z, index, inverse, operator):
    rows = lax.broadcasted_iota(jnp.int32, (z.coarse, z.all_corners), 0)
    select = (rows == index[...]).astype(BF16)
    parts = jnp.concatenate(split3(inverse[...]), axis=0).astype(BF16)
    half = dot(parts, select, NN)
    half = sum(half[k * z.coarse : (k + 1) * z.coarse] for k in range(3))
    parts = jnp.concatenate(split3(half), axis=1).astype(BF16)
    full = dot(select, parts, TN)
    operator[...] = sum(full[:, k * z.all_corners : (k + 1) * z.all_corners] for k in range(3))


def build_lift(z, table, operator, lift, *rest):
    pieces, (jump_lift, other) = rest[:-2], rest[-2:]
    place(z, table, pieces, 1, other)
    me = lax.axis_index("sub")
    own = operator[pl.ds(pl.multiple_of(me * z.corners, z.corners), z.corners), :]
    for i in range(z.blocks):
        at = pl.multiple_of(table[z.partner + i] * z.corners, z.corners)
        left = split(jnp.concatenate([own, -operator[pl.ds(at, z.corners), :]], axis=0))
        right = split(jnp.concatenate([lift[i], other[i]], axis=0))
        count = 2 * z.corners
        left = jnp.concatenate([left, left[:count]], axis=0)
        right = jnp.concatenate([right[:count], right[:count], right[count:]], axis=0)
        jump_lift[i] = split(dot(left, right, TN))


def extra_sum(z, own, pieces):
    total = own[...]
    for piece in pieces:
        total = total + jnp.concatenate(
            [piece[z.rows(1) + j] for j in range(z.extra_chunks)], axis=1
        )
    return total


def cluster_max(z, total):
    lanes = lane_ids(total.shape)
    own = (lanes >= z.max_lane) & (lanes < z.gram_lane)
    return jnp.max(jnp.where(own, total, 0.0), axis=1, keepdims=True)


def corner_rows(z, total):
    rows = split(total[:, : z.all_corners])
    return jnp.concatenate([rows, rows], axis=1)


def lane_sum(a):
    return jnp.sum(a, axis=1, keepdims=True)


def apply_round(z, step, table, *rest):
    count = len(z.masks)
    first, last = step == 1, step == ITERS
    rest = list(rest)
    take = lambda n: [rest.pop(0) for _ in range(n)]
    arrived = take(count)
    (before,) = take(1)
    if not first:
        own_extra, jump_lift = take(2)
    scale, diag, off, coupling = take(4)
    older = take(ITERS - 1) if last else []
    if first:
        take(1)
    field, image = take(2)
    if first:
        sources, (diag, off) = (diag, off), take(2)
    else:
        (total_out,) = take(1)
    (extra,) = take(1)
    pieces = take(count)
    other, parts = take(2)
    if first:
        (sems,) = rest
        copies = [
            [
                pltpu.make_async_copy(a.at[i], b.at[i], sems.at[k, i])
                for k, (a, b) in enumerate(zip(sources, (diag, off)))
            ]
            for i in range(z.blocks)
        ]
        for pair in copies:
            for copy in pair:
                copy.start()
    place(z, table, arrived, 0, other)
    if not first:
        total = extra_sum(z, own_extra, arrived)
        total_out[...] = total
        rows = corner_rows(z, total)
        shrink = 1.0 / cluster_max(z, total)
    for i in range(z.blocks):
        value = before[i] - other[i]
        if not first:
            value = (value + fold(dot(rows, jump_lift[i], NN))) * shrink
        field[i] = value
        parts[i] = split(scale[i : i + 1, :] * value)
    if first:
        for pair in copies:
            for copy in pair:
                copy.wait()
    partial = jnp.zeros((2 * z.columns, z.corners), F32)
    top = jnp.zeros((z.columns, z.width), F32)
    for i in range(z.blocks):
        mine = parts[i]
        partial = partial + dot(mine, coupling[:, i * z.width : (i + 1) * z.width], NT)
        source = table[z.inverse + i]
        coupled = dot(mine, diag[i], NT) + dot(mine, diag[i], NN)
        coupled = coupled + dot(parts[table[z.pattern + i]], off[i], NT)
        coupled = coupled + dot(parts[source], off[source], NN)
        row = scale[i : i + 1, :]
        result = row * (row * field[i] + fold(coupled))
        image[i] = result
        top = jnp.maximum(top, jnp.abs(result))
    fill_pieces(z, table, [image], pieces)
    me = lax.axis_index("sub")
    lanes = lane_ids((z.columns, z.extra))
    sums = fold(partial)
    padded = jnp.concatenate(
        [sums, jnp.zeros((z.columns, z.extra - z.corners), F32)], axis=1
    )
    tile = pltpu.roll(padded, me * z.corners, 1)
    tile = jnp.where(lanes == z.max_lane + me, jnp.max(top, axis=1, keepdims=True), tile)
    if last:
        fields = older + [field]
        products = [(fields[i], fields[j]) for i, j in PAIRS] + [(f, image) for f in fields]
        for entry, (a, b) in enumerate(products):
            acc = a[0] * b[0]
            for i in range(1, z.blocks):
                acc = acc + a[i] * b[i]
            tile = jnp.where(lanes == z.gram_lane + entry, lane_sum(acc), tile)
    extra[...] = tile
    for piece in pieces:
        for j in range(z.extra_chunks):
            piece[z.rows(1) + j] = tile[:, j * LANES : (j + 1) * LANES]


def cluster_gram(z, operator, own_extra, *rest):
    count = len(z.masks)
    arrived, totals, (gram,) = rest[:count], rest[count:-1], rest[-1:]
    total = extra_sum(z, own_extra, arrived)
    totals = [t[...] for t in totals]
    partials = [t[:, : z.all_corners] for t in totals + [total]]
    lifted = dot_high(partials[-1], operator[...], NT)
    lanes = lane_ids(gram.shape)
    tile = jnp.zeros(gram.shape, F32)
    for entry in range(ENTRIES):
        lane = z.gram_lane + entry
        value = total[:, lane : lane + 1]
        if entry >= len(PAIRS):
            value = 2.0 * (value + lane_sum(partials[entry - len(PAIRS)] * lifted))
        tile = jnp.where(lanes == entry, value, tile)
    for step, t in enumerate(totals):
        tile = jnp.where(lanes == ENTRIES + step, cluster_max(z, t), tile)
    gram[...] = tile


def last_vector(z, table, before, own_extra, jump_lift, *rest):
    arrived, (field, other) = rest[:-2], rest[-2:]
    place(z, table, arrived, 0, other)
    rows = corner_rows(z, extra_sum(z, own_extra, arrived))
    for i in range(z.blocks):
        field[i] = before[i] - other[i] + fold(dot(rows, jump_lift[i], NN))


def finish(z, *rest):
    grams, rest = rest[: z.groups], rest[z.groups :]
    fields, (multipliers, residual) = rest[:-2], rest[-2:]
    tables = [gram[...] for gram in grams]
    mine = tables[0]
    one = jnp.ones((z.columns, 1), F32)
    ratio = [[one] * z.groups]
    own_ratio = [one]
    growth = [None]
    for step in range(1, ITERS + 1):
        if step < ITERS:
            lane = ENTRIES + step - 1
            grown = [q * t[:, lane : lane + 1] for q, t in zip(ratio[-1], tables)]
            own = own_ratio[-1] * mine[:, lane : lane + 1]
        else:
            grown, own = ratio[-1], own_ratio[-1]
        top = functools.reduce(jnp.maximum, grown)
        ratio.append([q / top for q in grown])
        own_ratio.append(own / top)
        growth.append(top)
    gram = {}
    pairs = PAIRS + [(i, ITERS) for i in range(ITERS)]
    for entry, (i, j) in enumerate(pairs):
        value = 0.0
        for g in range(z.groups):
            value = value + ratio[i][g] * ratio[j][g] * tables[g][:, entry : entry + 1]
        gram[i, j] = gram[j, i] = value

    def inner(a, b):
        return sum(a[i] * sum(gram[i, j] * b[j] for j in b) for i in a)

    def add(a, weight, b):
        out = dict(a)
        for i, value in b.items():
            out[i] = out[i] + weight * value if i in out else weight * value
        return out

    rest_of, way, found = {0: one}, {0: one}, {}
    norm = gram[0, 0]
    for step in range(ITERS):
        product = {i + 1: growth[i + 1] * value for i, value in way.items()}
        alpha = norm / inner(way, product)
        found = add(found, alpha, way)
        rest_of = add(rest_of, -alpha, product)
        if step < ITERS - 1:
            following = inner(rest_of, rest_of)
            way = add(rest_of, following / norm, way)
            norm = following
    found = {i: value * own_ratio[i] for i, value in found.items()}
    rest_of = {i: value * own_ratio[i] for i, value in rest_of.items()}
    for i in range(z.blocks):
        values = [f[i] for f in fields]
        multipliers[:, i, :] = sum(c * values[j] for j, c in found.items())
        residual[:, i, :] = sum(c * values[j] for j, c in rest_of.items())


def call(body, outs, scratch, cost, args, table=True, away=()):
    args = [
        pltpu.with_memory_space_constraint(a, pltpu.HBM) if k in away else a
        for k, a in enumerate(args)
    ]
    specs = [HBM if k in away else VMEM for k in range(len(args))]
    if table:
        specs[0] = SMEM
    shapes = [
        pltpu.SMEM(s, t) if t == jnp.int32 else jax.ShapeDtypeStruct(s, t) for s, t in outs
    ]
    return pl.pallas_call(
        body,
        out_shape=shapes,
        in_specs=specs,
        out_specs=[SMEM if t == jnp.int32 else VMEM for _, t in outs],
        scratch_shapes=scratch,
        compiler_params=pltpu.CompilerParams(vmem_limit_bytes=LIMIT),
        cost_estimate=pl.CostEstimate(flops=cost, bytes_accessed=cost // 16, transcendentals=0),
    )(*args)


def on_device(
    load,
    row_scale,
    diag_blocks,
    off_blocks,
    off_pattern,
    partner,
    corner_coupling,
    corner_index,
    coarse_inverse,
    *,
    mesh,
):
    z = Sizes(load, corner_coupling, coarse_inverse, mesh)
    cols, blocks, width = z.columns, z.blocks, z.width
    field = ((blocks, cols, width), F32)
    other = pltpu.VMEM((blocks + 1, cols, width), F32)
    parts = pltpu.VMEM((blocks, 2 * cols, width), BF16)
    extra = ((cols, z.extra), F32)
    gram = ((cols, 128), F32)
    light, heavy = 4_000_000, 600_000_000

    def piece_shapes(kinds):
        rows = z.rows(kinds) + (z.extra_chunks if kinds == 1 else 0)
        return [((rows, cols, LANES), F32)] * len(z.masks)

    def kernel(body, *extra_args):
        return functools.partial(body, z, *extra_args)

    def exchange(pieces):
        return [
            lax.ppermute(piece, "sub", [(t, t ^ m) for t in range(z.peers)])
            for m, piece in zip(z.masks, pieces)
        ]

    table, loaded, lift, scale, coupling, *pieces = call(
        kernel(begin),
        [
            ((z.table,), jnp.int32),
            field,
            field,
            (row_scale.shape, F32),
            (corner_coupling.shape, BF16),
        ]
        + piece_shapes(2),
        [
            pltpu.VMEM(load.shape, F32),
            pltpu.SMEM(partner.shape, jnp.int32),
            pltpu.SMEM(off_pattern.shape, jnp.int32),
            pltpu.SMEM((z.peers,), jnp.int32),
            pltpu.SemaphoreType.DMA((5,)),
        ],
        light,
        [partner, off_pattern, load, row_scale, corner_coupling],
        False, range(5),
    )
    arrived = exchange(pieces)
    (operator,) = call(
        kernel(build_operator), [((z.all_corners, z.all_corners), F32)], [], light,
        [corner_index, coarse_inverse], False,
    )
    weight = (diag_blocks.shape, BF16)
    newest, image, diag, off, own_extra, *pieces = call(
        kernel(apply_round, 1),
        [field, field, weight, weight, extra] + piece_shapes(1),
        [other, parts, pltpu.SemaphoreType.DMA((2, blocks))], heavy,
        [table, *arrived, loaded, scale, diag_blocks, off_blocks, coupling, operator],
        True, (len(arrived) + 3, len(arrived) + 4),
    )
    (jump_lift,) = call(
        kernel(build_lift), [((blocks, 2 * z.all_corners, width), BF16)], [other], heavy,
        [table, operator, lift, *arrived],
    )
    arrived = exchange(pieces)
    fields, totals = [newest], []
    for step in range(2, ITERS + 1):
        older = fields if step == ITERS else []
        newest, image, total, own_extra, *pieces = call(
            kernel(apply_round, step),
            [field, field, extra, extra] + piece_shapes(1), [other, parts], heavy,
            [table, *arrived, image, own_extra, jump_lift, scale, diag, off, coupling, *older],
        )
        fields.append(newest)
        totals.append(total)
        arrived = exchange(pieces)
    (own_gram,) = call(
        kernel(cluster_gram), [gram], [], light, [operator, own_extra, *arrived, *totals], False
    )
    power = z.groups & (z.groups - 1) == 0
    grams = [own_gram] + [
        lax.ppermute(
            own_gram, "group",
            [(a, a ^ k if power else (a + k) % z.groups) for a in range(z.groups)],
        )
        for k in range(1, z.groups)
    ]
    (newest,) = call(
        kernel(last_vector), [field], [other], light,
        [table, image, own_extra, jump_lift, *arrived],
    )
    multipliers, residual = call(
        kernel(finish), [(load.shape, F32)] * 2, [], light, [*grams, *fields, newest], False
    )
    return multipliers, residual


def solution(mesh):
    return jax.shard_map(
        functools.partial(on_device, mesh=dict(mesh.shape)),
        mesh=mesh,
        in_specs=(
            P(None, ("group", "sub"), None),
            P(("group", "sub"), None),
            P(("group", "sub"), None, None),
            P(("group", "sub"), None, None),
            P(("group", "sub"), None),
            P(("group", "sub"), None),
            P(("group", "sub"), None),
            P("group", None),
            P("group", None),
        ),
        out_specs=(P(None, ("group", "sub"), None), P(None, ("group", "sub"), None)),
        check_vma=False,
    )
```

```python
import functools

import jax
import jax.numpy as jnp
from jax import lax
from jax.experimental import pallas as pl
from jax.experimental.pallas import tpu as pltpu
from jax.sharding import PartitionSpec as P

ITERS = 4
HIGH = lax.Precision.HIGHEST
F32 = jnp.float32
BF16 = jnp.bfloat16
VMEM = pl.BlockSpec(memory_space=pltpu.VMEM)
SMEM = pl.BlockSpec(memory_space=pltpu.SMEM)
HBM = pl.BlockSpec(memory_space=pltpu.HBM)
LIMIT = 24 * 1024 * 1024
LANES = 128
PAIRS = [(i, j) for j in range(ITERS) for i in range(j + 1)]
ENTRIES = len(PAIRS) + ITERS
NN = (((1,), (0,)), ((), ()))
NT = (((1,), (1,)), ((), ()))
TN = (((0,), (0,)), ((), ()))


def dot(a, b, dims):
    return lax.dot_general(a, b, dims, preferred_element_type=F32)


def dot_high(a, b, dims):
    return lax.dot_general(a, b, dims, precision=HIGH, preferred_element_type=F32)


def split(a):
    high = a.astype(BF16).astype(F32)
    return jnp.concatenate([high, a - high], axis=0).astype(BF16)


def fold(a):
    half = a.shape[0] // 2
    return a[:half] + a[half:]


def lane_ids(shape):
    return lax.broadcasted_iota(jnp.int32, shape, 1)


class Sizes:
    def __init__(self, load, corner_coupling, coarse_inverse, mesh):
        self.columns = load.shape[0]
        self.blocks = load.shape[1]
        self.width = load.shape[2]
        self.corners = corner_coupling.shape[0]
        assert self.corners == self.columns
        self.coarse = coarse_inverse.shape[1]
        self.peers = mesh["sub"]
        self.groups = mesh["group"]
        self.capacity = (self.blocks + self.peers - 2) // (self.peers - 1)
        self.all_corners = self.peers * self.corners
        self.max_lane = self.all_corners
        self.gram_lane = self.max_lane + self.peers
        self.extra_chunks = -(-(self.gram_lane + ENTRIES) // LANES)
        self.extra = self.extra_chunks * LANES
        self.halves = self.width // LANES
        self.pairs = self.peers // 2
        self.masks = range(1, self.peers)
        self.slots = self.peers * self.capacity
        self.inverse = self.slots
        self.pattern = self.inverse + self.blocks
        self.partner = self.pattern + self.blocks
        self.table = self.partner + self.blocks

    def rows(self, kinds):
        return kinds * self.capacity * self.halves


def fill_table(z, partner, pattern, table, counts):
    me = lax.axis_index("sub")
    for entry in range(z.slots):
        table[entry] = z.blocks
    for m in range(z.peers):
        counts[m] = 0
    for i in range(z.blocks):
        mate = partner[0, i]
        source = pattern[0, i]
        m = mate ^ me
        rank = counts[m]
        table[m * z.capacity + rank] = i
        counts[m] = rank + 1
        table[z.inverse + source] = i
        table[z.pattern + i] = source
        table[z.partner + i] = mate


def pair_of(m):
    return (lax.axis_index("sub") ^ m) >> 1


def fill_pieces(z, table, sources, pieces):
    for m in z.masks:
        pair = pair_of(m)
        row = 0
        for source in sources:
            for r in range(z.capacity):
                block = jnp.minimum(table[m * z.capacity + r], z.blocks - 1)
                value = source[block]
                for h in range(z.halves):
                    pieces[pair, m % 2, row] = value[:, h * LANES : (h + 1) * LANES]
                    row += 1


def place(z, table, arrived, kind, target):
    for m in z.masks:
        pair = pair_of(m)
        row = z.rows(kind)
        for r in range(z.capacity):
            block = table[m * z.capacity + r]
            for h in range(z.halves):
                target[block, :, h * LANES : (h + 1) * LANES] = arrived[m % 2][pair, m % 2, row]
                row += 1


def begin(z, partner, pattern, load, scale, coupling, table, field, lift, scale_out, coupling_out, pieces, *scratch):
    here, partner_here, pattern_here, counts, sems = scratch
    copies = [
        pltpu.make_async_copy(a, b, sems.at[k])
        for k, (a, b) in enumerate(
            [
                (partner, partner_here),
                (pattern, pattern_here),
                (load, here),
                (scale, scale_out),
                (coupling, coupling_out),
            ]
        )
    ]
    for copy in copies:
        copy.start()
    copies[0].wait()
    copies[1].wait()
    fill_table(z, partner_here, pattern_here, table, counts)
    for copy in copies[2:]:
        copy.wait()
    for i in range(z.blocks):
        field[i] = here[:, i, :]
        part = coupling_out[:, i * z.width : (i + 1) * z.width].astype(F32)
        lift[i] = scale_out[i : i + 1, :] * part
    fill_pieces(z, table, [field, lift], pieces)


def split3(a):
    high = a.astype(BF16).astype(F32)
    middle = (a - high).astype(BF16).astype(F32)
    return [high, middle, a - high - middle]


def prepare(z, index_in, inverse_in, diag, off, operator, diag_out, off_out, index, inverse, sems):
    copies = [
        pltpu.make_async_copy(a, b, sems.at[k])
        for k, (a, b) in enumerate(
            [(index_in, index), (inverse_in, inverse), (diag, diag_out), (off, off_out)]
        )
    ]
    for copy in copies:
        copy.start()
    copies[0].wait()
    copies[1].wait()
    rows = lax.broadcasted_iota(jnp.int32, (z.coarse, z.all_corners), 0)
    select = (rows == index[...]).astype(BF16)
    parts = jnp.concatenate(split3(inverse[...]), axis=0).astype(BF16)
    half = dot(parts, select, NN)
    half = sum(half[k * z.coarse : (k + 1) * z.coarse] for k in range(3))
    parts = jnp.concatenate(split3(half), axis=1).astype(BF16)
    full = dot(select, parts, TN)
    operator[...] = sum(full[:, k * z.all_corners : (k + 1) * z.all_corners] for k in range(3))
    copies[2].wait()
    copies[3].wait()


def build_lift(z, table, operator, lift, same, across, jump_lift, other):
    place(z, table, (same, across), 1, other)
    me = lax.axis_index("sub")
    own = operator[pl.ds(pl.multiple_of(me * z.corners, z.corners), z.corners), :]
    for i in range(z.blocks):
        at = pl.multiple_of(table[z.partner + i] * z.corners, z.corners)
        left = split(jnp.concatenate([own, -operator[pl.ds(at, z.corners), :]], axis=0))
        right = split(jnp.concatenate([lift[i], other[i]], axis=0))
        count = 2 * z.corners
        left = jnp.concatenate([left, left[:count]], axis=0)
        right = jnp.concatenate([right[:count], right[:count], right[count:]], axis=0)
        jump_lift[i] = split(dot(left, right, TN))


def extra_sum(z, own, arrived):
    total = own[...]
    for m in z.masks:
        pair = pair_of(m)
        total = total + jnp.concatenate(
            [arrived[m % 2][pair, m % 2, z.rows(1) + j] for j in range(z.extra_chunks)], axis=1
        )
    return total


def cluster_max(z, total):
    lanes = lane_ids(total.shape)
    own = (lanes >= z.max_lane) & (lanes < z.gram_lane)
    return jnp.max(jnp.where(own, total, 0.0), axis=1, keepdims=True)


def corner_rows(z, total):
    rows = split(total[:, : z.all_corners])
    return jnp.concatenate([rows, rows], axis=1)


def lane_sum(a):
    return jnp.sum(a, axis=1, keepdims=True)


def apply_round(z, step, table, *rest):
    first, last = step == 1, step == ITERS
    rest = list(rest)
    take = lambda n: [rest.pop(0) for _ in range(n)]
    arrived = take(2)
    (before,) = take(1)
    if not first:
        own_extra, jump_lift = take(2)
    scale, diag, off, coupling = take(4)
    older = take(ITERS - 1) if last else []
    field, image = take(2)
    if not first:
        (total_out,) = take(1)
    extra, pieces, other, parts = rest
    place(z, table, arrived, 0, other)
    if not first:
        total = extra_sum(z, own_extra, arrived)
        total_out[...] = total
        rows = corner_rows(z, total)
        shrink = 1.0 / cluster_max(z, total)
    for i in range(z.blocks):
        value = before[i] - other[i]
        if not first:
            value = (value + fold(dot(rows, jump_lift[i], NN))) * shrink
        field[i] = value
        parts[i] = split(scale[i : i + 1, :] * value)
    partial = jnp.zeros((2 * z.columns, z.corners), F32)
    top = jnp.zeros((z.columns, z.width), F32)
    for i in range(z.blocks):
        mine = parts[i]
        partial = partial + dot(mine, coupling[:, i * z.width : (i + 1) * z.width], NT)
        source = table[z.inverse + i]
        coupled = dot(mine, diag[i], NT) + dot(mine, diag[i], NN)
        coupled = coupled + dot(parts[table[z.pattern + i]], off[i], NT)
        coupled = coupled + dot(parts[source], off[source], NN)
        row = scale[i : i + 1, :]
        result = row * (row * field[i] + fold(coupled))
        image[i] = result
        top = jnp.maximum(top, jnp.abs(result))
    fill_pieces(z, table, [image], pieces)
    me = lax.axis_index("sub")
    lanes = lane_ids((z.columns, z.extra))
    sums = fold(partial)
    padded = jnp.concatenate(
        [sums, jnp.zeros((z.columns, z.extra - z.corners), F32)], axis=1
    )
    tile = pltpu.roll(padded, me * z.corners, 1)
    tile = jnp.where(lanes == z.max_lane + me, jnp.max(top, axis=1, keepdims=True), tile)
    if last:
        fields = older + [field]
        products = [(fields[i], fields[j]) for i, j in PAIRS] + [(f, image) for f in fields]
        for entry, (a, b) in enumerate(products):
            acc = a[0] * b[0]
            for i in range(1, z.blocks):
                acc = acc + a[i] * b[i]
            tile = jnp.where(lanes == z.gram_lane + entry, lane_sum(acc), tile)
    extra[...] = tile
    for m in z.masks:
        pair = pair_of(m)
        for j in range(z.extra_chunks):
            pieces[pair, m % 2, z.rows(1) + j] = tile[:, j * LANES : (j + 1) * LANES]


def cluster_gram(z, operator, own_extra, *rest):
    arrived, totals, (gram,) = rest[:2], rest[2:-1], rest[-1:]
    total = extra_sum(z, own_extra, arrived)
    totals = [t[...] for t in totals]
    partials = [t[:, : z.all_corners] for t in totals + [total]]
    lifted = dot_high(partials[-1], operator[...], NT)
    lanes = lane_ids(gram.shape)
    tile = jnp.zeros(gram.shape, F32)
    for entry in range(ENTRIES):
        lane = z.gram_lane + entry
        value = total[:, lane : lane + 1]
        if entry >= len(PAIRS):
            value = 2.0 * (value + lane_sum(partials[entry - len(PAIRS)] * lifted))
        tile = jnp.where(lanes == entry, value, tile)
    for step, t in enumerate(totals):
        tile = jnp.where(lanes == ENTRIES + step, cluster_max(z, t), tile)
    gram[...] = tile


def last_vector(z, table, before, own_extra, jump_lift, *rest):
    arrived, (field, other) = rest[:-2], rest[-2:]
    place(z, table, arrived, 0, other)
    rows = corner_rows(z, extra_sum(z, own_extra, arrived))
    for i in range(z.blocks):
        field[i] = before[i] - other[i] + fold(dot(rows, jump_lift[i], NN))


def finish(z, *rest):
    grams, rest = rest[: z.groups], rest[z.groups :]
    fields, (multipliers, residual) = rest[:-2], rest[-2:]
    tables = [gram[...] for gram in grams]
    mine = tables[0]
    one = jnp.ones((z.columns, 1), F32)
    ratio = [[one] * z.groups]
    own_ratio = [one]
    growth = [None]
    for step in range(1, ITERS + 1):
        if step < ITERS:
            lane = ENTRIES + step - 1
            grown = [q * t[:, lane : lane + 1] for q, t in zip(ratio[-1], tables)]
            own = own_ratio[-1] * mine[:, lane : lane + 1]
        else:
            grown, own = ratio[-1], own_ratio[-1]
        top = functools.reduce(jnp.maximum, grown)
        ratio.append([q / top for q in grown])
        own_ratio.append(own / top)
        growth.append(top)
    gram = {}
    pairs = PAIRS + [(i, ITERS) for i in range(ITERS)]
    for entry, (i, j) in enumerate(pairs):
        value = 0.0
        for g in range(z.groups):
            value = value + ratio[i][g] * ratio[j][g] * tables[g][:, entry : entry + 1]
        gram[i, j] = gram[j, i] = value

    def inner(a, b):
        return sum(a[i] * sum(gram[i, j] * b[j] for j in b) for i in a)

    def add(a, weight, b):
        out = dict(a)
        for i, value in b.items():
            out[i] = out[i] + weight * value if i in out else weight * value
        return out

    rest_of, way, found = {0: one}, {0: one}, {}
    norm = gram[0, 0]
    for step in range(ITERS):
        product = {i + 1: growth[i + 1] * value for i, value in way.items()}
        alpha = norm / inner(way, product)
        found = add(found, alpha, way)
        rest_of = add(rest_of, -alpha, product)
        if step < ITERS - 1:
            following = inner(rest_of, rest_of)
            way = add(rest_of, following / norm, way)
            norm = following
    found = {i: value * own_ratio[i] for i, value in found.items()}
    rest_of = {i: value * own_ratio[i] for i, value in rest_of.items()}
    for i in range(z.blocks):
        values = [f[i] for f in fields]
        multipliers[:, i, :] = sum(c * values[j] for j, c in found.items())
        residual[:, i, :] = sum(c * values[j] for j, c in rest_of.items())


def call(body, outs, scratch, cost, args, table=True, away=()):
    args = [
        pltpu.with_memory_space_constraint(a, pltpu.HBM) if k in away else a
        for k, a in enumerate(args)
    ]
    specs = [HBM if k in away else VMEM for k in range(len(args))]
    if table:
        specs[0] = SMEM
    shapes = [
        pltpu.SMEM(s, t) if t == jnp.int32 else jax.ShapeDtypeStruct(s, t) for s, t in outs
    ]
    return pl.pallas_call(
        body,
        out_shape=shapes,
        in_specs=specs,
        out_specs=[SMEM if t == jnp.int32 else VMEM for _, t in outs],
        scratch_shapes=scratch,
        compiler_params=pltpu.CompilerParams(vmem_limit_bytes=LIMIT),
        cost_estimate=pl.CostEstimate(flops=cost, bytes_accessed=cost // 16, transcendentals=0),
    )(*args)


def on_device(
    load,
    row_scale,
    diag_blocks,
    off_blocks,
    off_pattern,
    partner,
    corner_coupling,
    corner_index,
    coarse_inverse,
    *,
    mesh,
):
    z = Sizes(load, corner_coupling, coarse_inverse, mesh)
    cols, blocks, width = z.columns, z.blocks, z.width
    field = ((blocks, cols, width), F32)
    other = pltpu.VMEM((blocks + 1, cols, width), F32)
    parts = pltpu.VMEM((blocks, 2 * cols, width), BF16)
    extra = ((cols, z.extra), F32)
    gram = ((cols, 128), F32)
    light, heavy = 4_000_000, 600_000_000

    def piece_shape(kinds):
        rows = z.rows(kinds) + (z.extra_chunks if kinds == 1 else 0)
        return ((z.pairs, 2, rows, cols, LANES), F32)

    def kernel(body, *extra_args):
        return functools.partial(body, z, *extra_args)

    def exchange(pieces):
        sides = [list(range(side, z.peers, 2)) for side in range(2)]
        same = lax.all_to_all(pieces, "sub", 0, 0, axis_index_groups=sides, tiled=True)
        return same, lax.ppermute(same, "sub", [(t, t ^ 1) for t in range(z.peers)])

    table, loaded, lift, scale, coupling, pieces = call(
        kernel(begin),
        [
            ((z.table,), jnp.int32),
            field,
            field,
            (row_scale.shape, F32),
            (corner_coupling.shape, BF16),
            piece_shape(2),
        ],
        [
            pltpu.VMEM(load.shape, F32),
            pltpu.SMEM(partner.shape, jnp.int32),
            pltpu.SMEM(off_pattern.shape, jnp.int32),
            pltpu.SMEM((z.peers,), jnp.int32),
            pltpu.SemaphoreType.DMA((5,)),
        ],
        light,
        [partner, off_pattern, load, row_scale, corner_coupling],
        False, range(5),
    )
    arrived = exchange(pieces)
    weight = (diag_blocks.shape, BF16)
    operator, diag, off = call(
        kernel(prepare), [((z.all_corners, z.all_corners), F32), weight, weight],
        [
            pltpu.VMEM(corner_index.shape, jnp.int32),
            pltpu.VMEM(coarse_inverse.shape, F32),
            pltpu.SemaphoreType.DMA((4,)),
        ],
        heavy, [corner_index, coarse_inverse, diag_blocks, off_blocks], False, range(4),
    )
    newest, image, own_extra, pieces = call(
        kernel(apply_round, 1),
        [field, field, extra, piece_shape(1)], [other, parts], heavy,
        [table, *arrived, loaded, scale, diag, off, coupling],
    )
    (jump_lift,) = call(
        kernel(build_lift), [((blocks, 2 * z.all_corners, width), BF16)], [other], heavy,
        [table, operator, lift, *arrived],
    )
    arrived = exchange(pieces)
    fields, totals = [newest], []
    for step in range(2, ITERS + 1):
        older = fields if step == ITERS else []
        newest, image, total, own_extra, pieces = call(
            kernel(apply_round, step),
            [field, field, extra, extra, piece_shape(1)], [other, parts], heavy,
            [table, *arrived, image, own_extra, jump_lift, scale, diag, off, coupling, *older],
        )
        fields.append(newest)
        totals.append(total)
        arrived = exchange(pieces)
    (own_gram,) = call(
        kernel(cluster_gram), [gram], [], light, [operator, own_extra, *arrived, *totals], False
    )
    power = z.groups & (z.groups - 1) == 0
    grams = [own_gram] + [
        lax.ppermute(
            own_gram, "group",
            [(a, a ^ k if power else (a + k) % z.groups) for a in range(z.groups)],
        )
        for k in range(1, z.groups)
    ]
    (newest,) = call(
        kernel(last_vector), [field], [other], light,
        [table, image, own_extra, jump_lift, *arrived],
    )
    multipliers, residual = call(
        kernel(finish), [(load.shape, F32)] * 2, [], light, [*grams, *fields, newest], False
    )
    return multipliers, residual


def solution(mesh):
    return jax.shard_map(
        functools.partial(on_device, mesh=dict(mesh.shape)),
        mesh=mesh,
        in_specs=(
            P(None, ("group", "sub"), None),
            P(("group", "sub"), None),
            P(("group", "sub"), None, None),
            P(("group", "sub"), None, None),
            P(("group", "sub"), None),
            P(("group", "sub"), None),
            P(("group", "sub"), None),
            P("group", None),
            P("group", None),
        ),
        out_specs=(P(None, ("group", "sub"), None), P(None, ("group", "sub"), None)),
        check_vma=False,
    )
```

```python
import functools

import jax
import jax.numpy as jnp
from jax import lax
from jax.experimental import pallas as pl
from jax.experimental.pallas import tpu as pltpu
from jax.sharding import PartitionSpec as P

ITERS = 4
HIGH = lax.Precision.HIGHEST
F32 = jnp.float32
BF16 = jnp.bfloat16
VMEM = pl.BlockSpec(memory_space=pltpu.VMEM)
SMEM = pl.BlockSpec(memory_space=pltpu.SMEM)
HBM = pl.BlockSpec(memory_space=pltpu.HBM)
LIMIT = 24 * 1024 * 1024
LANES = 128
PAIRS = [(i, j) for j in range(ITERS) for i in range(j + 1)]
ENTRIES = len(PAIRS) + ITERS
NN = (((1,), (0,)), ((), ()))
NT = (((1,), (1,)), ((), ()))
TN = (((0,), (0,)), ((), ()))


def dot(a, b, dims):
    return lax.dot_general(a, b, dims, preferred_element_type=F32)


def dot_high(a, b, dims):
    return lax.dot_general(a, b, dims, precision=HIGH, preferred_element_type=F32)


def split(a):
    high = a.astype(BF16).astype(F32)
    return jnp.concatenate([high, a - high], axis=0).astype(BF16)


def fold(a):
    half = a.shape[0] // 2
    return a[:half] + a[half:]


def lane_ids(shape):
    return lax.broadcasted_iota(jnp.int32, shape, 1)


class Sizes:
    def __init__(self, load, corner_coupling, coarse_inverse, mesh):
        self.columns = load.shape[0]
        self.blocks = load.shape[1]
        self.width = load.shape[2]
        self.corners = corner_coupling.shape[0]
        assert self.corners == self.columns
        self.coarse = coarse_inverse.shape[1]
        self.peers = mesh["sub"]
        self.groups = mesh["group"]
        self.capacity = (self.blocks + self.peers - 2) // (self.peers - 1)
        self.all_corners = self.peers * self.corners
        self.max_lane = self.all_corners
        self.gram_lane = self.max_lane + self.peers
        self.extra_chunks = -(-(self.gram_lane + ENTRIES) // LANES)
        self.extra = self.extra_chunks * LANES
        self.halves = self.width // LANES
        distances = range(2, self.peers, 2)
        self.paired = [m for m in distances if m & (m - 1) == 0]
        self.direct = [n for m in distances if m & (m - 1) for n in (m + 1, m)]
        self.handed = [1] + [m + 1 for m in self.paired]
        self.slots = self.peers * self.capacity
        self.inverse = self.slots
        self.pattern = self.inverse + self.blocks
        self.partner = self.pattern + self.blocks
        self.table = self.partner + self.blocks

    def rows(self, kinds):
        return kinds * self.capacity * self.halves

    def sent(self, kinds):
        rows = self.rows(kinds)
        near = len(self.handed) * rows
        return [near] + [rows] * len(self.direct) + [2 * rows] * len(self.paired)

    def first(self):
        return 1 + len(self.direct)

    def sources(self):
        found = [(1, 0, 0)]
        found += [(m, 1 + k, 0) for k, m in enumerate(self.direct)]
        for k, m in enumerate(self.paired):
            found += [(m + side, self.first() + k, side) for side in range(2)]
        return found


def fill_table(z, partner, pattern, table, counts):
    me = lax.axis_index("sub")
    for entry in range(z.slots):
        table[entry] = z.blocks
    for m in range(z.peers):
        counts[m] = 0
    for i in range(z.blocks):
        mate = partner[0, i]
        source = pattern[0, i]
        m = mate ^ me
        rank = counts[m]
        table[m * z.capacity + rank] = i
        counts[m] = rank + 1
        table[z.inverse + source] = i
        table[z.pattern + i] = source
        table[z.partner + i] = mate


def fill_piece(z, table, sources, m, piece, row):
    for source in sources:
        for r in range(z.capacity):
            value = source[jnp.minimum(table[m * z.capacity + r], z.blocks - 1)]
            for h in range(z.halves):
                piece[row] = value[:, h * LANES : (h + 1) * LANES]
                row += 1


def fill_first(z, table, sources, pieces):
    rows = z.rows(len(sources))
    for k, m in enumerate(z.handed):
        fill_piece(z, table, sources, m, pieces[0], k * rows)
    for m, piece in zip(z.direct, pieces[1:]):
        fill_piece(z, table, sources, m, piece, 0)


def relay(z, kinds, table, *rest):
    sources, rest = rest[:kinds], rest[kinds:]
    chunks = z.extra_chunks if kinds == 1 else 0
    if chunks:
        own_extra, rest = rest[0], rest[1:]
    near, pieces = rest[0], rest[1:]
    rows = z.rows(kinds)
    for k, (m, piece) in enumerate(zip(z.paired, pieces)):
        fill_piece(z, table, sources, m, piece, 0)
        for row in range(rows):
            piece[rows + row] = near[(k + 1) * rows + row]
        for j in range(chunks):
            mine = own_extra[:, j * LANES : (j + 1) * LANES]
            piece[2 * rows + j] = mine + near[z.sent(1)[0] + j]


def place(z, table, arrived, kind, kinds, target):
    for m, transfer, piece in z.sources():
        row = piece * z.rows(kinds) + z.rows(kind)
        for r in range(z.capacity):
            block = table[m * z.capacity + r]
            for h in range(z.halves):
                target[block, :, h * LANES : (h + 1) * LANES] = arrived[transfer][row]
                row += 1


def begin(z, partner, pattern, load, scale, coupling, table, field, lift, scale_out, coupling_out, *rest):
    pieces, (here, partner_here, pattern_here, counts, sems) = rest[:-5], rest[-5:]
    copies = [
        pltpu.make_async_copy(a, b, sems.at[k])
        for k, (a, b) in enumerate(
            [
                (partner, partner_here),
                (pattern, pattern_here),
                (load, here),
                (scale, scale_out),
                (coupling, coupling_out),
            ]
        )
    ]
    for copy in copies:
        copy.start()
    copies[0].wait()
    copies[1].wait()
    fill_table(z, partner_here, pattern_here, table, counts)
    for copy in copies[2:]:
        copy.wait()
    for i in range(z.blocks):
        field[i] = here[:, i, :]
        part = coupling_out[:, i * z.width : (i + 1) * z.width].astype(F32)
        lift[i] = scale_out[i : i + 1, :] * part
    fill_first(z, table, [field, lift], pieces)


def split3(a):
    high = a.astype(BF16).astype(F32)
    middle = (a - high).astype(BF16).astype(F32)
    return [high, middle, a - high - middle]


def prepare(z, index_in, inverse_in, diag, off, operator, diag_out, off_out, index, inverse, sems):
    copies = [
        pltpu.make_async_copy(a, b, sems.at[k])
        for k, (a, b) in enumerate(
            [(index_in, index), (inverse_in, inverse), (diag, diag_out), (off, off_out)]
        )
    ]
    for copy in copies:
        copy.start()
    copies[0].wait()
    copies[1].wait()
    rows = lax.broadcasted_iota(jnp.int32, (z.coarse, z.all_corners), 0)
    select = (rows == index[...]).astype(BF16)
    parts = jnp.concatenate(split3(inverse[...]), axis=0).astype(BF16)
    half = dot(parts, select, NN)
    half = sum(half[k * z.coarse : (k + 1) * z.coarse] for k in range(3))
    parts = jnp.concatenate(split3(half), axis=1).astype(BF16)
    full = dot(select, parts, TN)
    operator[...] = sum(full[:, k * z.all_corners : (k + 1) * z.all_corners] for k in range(3))
    copies[2].wait()
    copies[3].wait()


def build_lift(z, table, operator, lift, *rest):
    pieces, (jump_lift, other) = rest[:-2], rest[-2:]
    place(z, table, pieces, 1, 2, other)
    me = lax.axis_index("sub")
    own = operator[pl.ds(pl.multiple_of(me * z.corners, z.corners), z.corners), :]
    for i in range(z.blocks):
        at = pl.multiple_of(table[z.partner + i] * z.corners, z.corners)
        left = split(jnp.concatenate([own, -operator[pl.ds(at, z.corners), :]], axis=0))
        right = split(jnp.concatenate([lift[i], other[i]], axis=0))
        count = 2 * z.corners
        left = jnp.concatenate([left, left[:count]], axis=0)
        right = jnp.concatenate([right[:count], right[:count], right[count:]], axis=0)
        jump_lift[i] = split(dot(left, right, TN))


def extra_sum(z, own, arrived):
    total = own[...]
    for rows, piece in zip(z.sent(1), arrived):
        total = total + jnp.concatenate([piece[rows + j] for j in range(z.extra_chunks)], axis=1)
    return total


def cluster_max(z, total):
    lanes = lane_ids(total.shape)
    own = (lanes >= z.max_lane) & (lanes < z.gram_lane)
    return jnp.max(jnp.where(own, total, 0.0), axis=1, keepdims=True)


def corner_rows(z, total):
    rows = split(total[:, : z.all_corners])
    return jnp.concatenate([rows, rows], axis=1)


def lane_sum(a):
    return jnp.sum(a, axis=1, keepdims=True)


def apply_round(z, step, table, *rest):
    count = len(z.sent(1))
    first, last = step == 1, step == ITERS
    rest = list(rest)
    take = lambda n: [rest.pop(0) for _ in range(n)]
    arrived = take(count)
    (before,) = take(1)
    if not first:
        own_extra, jump_lift = take(2)
    scale, diag, off, coupling = take(4)
    older = take(ITERS - 1) if last else []
    field, image = take(2)
    if not first:
        (total_out,) = take(1)
    (extra,) = take(1)
    pieces = take(z.first())
    other, parts = rest
    place(z, table, arrived, 0, 2 if first else 1, other)
    if not first:
        total = extra_sum(z, own_extra, arrived)
        total_out[...] = total
        rows = corner_rows(z, total)
        shrink = 1.0 / cluster_max(z, total)
    for i in range(z.blocks):
        value = before[i] - other[i]
        if not first:
            value = (value + fold(dot(rows, jump_lift[i], NN))) * shrink
        field[i] = value
        parts[i] = split(scale[i : i + 1, :] * value)
    partial = jnp.zeros((2 * z.columns, z.corners), F32)
    top = jnp.zeros((z.columns, z.width), F32)
    for i in range(z.blocks):
        mine = parts[i]
        partial = partial + dot(mine, coupling[:, i * z.width : (i + 1) * z.width], NT)
        source = table[z.inverse + i]
        coupled = dot(mine, diag[i], NT) + dot(mine, diag[i], NN)
        coupled = coupled + dot(parts[table[z.pattern + i]], off[i], NT)
        coupled = coupled + dot(parts[source], off[source], NN)
        row = scale[i : i + 1, :]
        result = row * (row * field[i] + fold(coupled))
        image[i] = result
        top = jnp.maximum(top, jnp.abs(result))
    fill_first(z, table, [image], pieces)
    me = lax.axis_index("sub")
    lanes = lane_ids((z.columns, z.extra))
    sums = fold(partial)
    padded = jnp.concatenate(
        [sums, jnp.zeros((z.columns, z.extra - z.corners), F32)], axis=1
    )
    tile = pltpu.roll(padded, me * z.corners, 1)
    tile = jnp.where(lanes == z.max_lane + me, jnp.max(top, axis=1, keepdims=True), tile)
    if last:
        fields = older + [field]
        products = [(fields[i], fields[j]) for i, j in PAIRS] + [(f, image) for f in fields]
        for entry, (a, b) in enumerate(products):
            acc = a[0] * b[0]
            for i in range(1, z.blocks):
                acc = acc + a[i] * b[i]
            tile = jnp.where(lanes == z.gram_lane + entry, lane_sum(acc), tile)
    extra[...] = tile
    for rows, piece in zip(z.sent(1), pieces):
        for j in range(z.extra_chunks):
            piece[rows + j] = tile[:, j * LANES : (j + 1) * LANES]


def cluster_gram(z, operator, own_extra, *rest):
    count = len(z.sent(1))
    arrived, totals, (gram,) = rest[:count], rest[count:-1], rest[-1:]
    total = extra_sum(z, own_extra, arrived)
    totals = [t[...] for t in totals]
    partials = [t[:, : z.all_corners] for t in totals + [total]]
    lifted = dot_high(partials[-1], operator[...], NT)
    lanes = lane_ids(gram.shape)
    tile = jnp.zeros(gram.shape, F32)
    for entry in range(ENTRIES):
        lane = z.gram_lane + entry
        value = total[:, lane : lane + 1]
        if entry >= len(PAIRS):
            value = 2.0 * (value + lane_sum(partials[entry - len(PAIRS)] * lifted))
        tile = jnp.where(lanes == entry, value, tile)
    for step, t in enumerate(totals):
        tile = jnp.where(lanes == ENTRIES + step, cluster_max(z, t), tile)
    gram[...] = tile


def last_vector(z, table, before, own_extra, jump_lift, *rest):
    arrived, (field, other) = rest[:-2], rest[-2:]
    place(z, table, arrived, 0, 1, other)
    rows = corner_rows(z, extra_sum(z, own_extra, arrived))
    for i in range(z.blocks):
        field[i] = before[i] - other[i] + fold(dot(rows, jump_lift[i], NN))


def finish(z, *rest):
    grams, rest = rest[: z.groups], rest[z.groups :]
    fields, (multipliers, residual) = rest[:-2], rest[-2:]
    tables = [gram[...] for gram in grams]
    shape = (z.columns, LANES)
    lanes = lane_ids(shape)

    def column(table, lane):
        return jnp.broadcast_to(table[:, lane : lane + 1], shape)

    one = jnp.ones(shape, F32)
    ratio = [[one] * z.groups]
    growth = [None]
    for step in range(1, ITERS + 1):
        grown = ratio[-1]
        if step < ITERS:
            grown = [q * column(t, ENTRIES + step - 1) for q, t in zip(grown, tables)]
        top = functools.reduce(jnp.maximum, grown)
        inverse = 1.0 / top
        ratio.append([q * inverse for q in grown])
        growth.append(top)
    pairs = PAIRS + [(i, ITERS) for i in range(ITERS)]

    def lanes_of(side, level):
        chosen = [e for e, pair in enumerate(pairs) if pair[side] == level]
        return functools.reduce(jnp.logical_or, [lanes == e for e in chosen])

    where = [[lanes_of(side, level) for level in range(side, ITERS + side)] for side in range(2)]
    total = jnp.zeros(shape, F32)
    for g, table in enumerate(tables):
        for side in range(2):
            weight = one
            for level in range(1, ITERS + side):
                weight = jnp.where(where[side][level - side], ratio[level][g], weight)
            table = table * weight
        total = total + table
    gram = {}
    for entry, (i, j) in enumerate(pairs):
        gram[i, j] = gram[j, i] = column(total, entry)

    def inner(a, b):
        return sum(a[i] * sum(gram[i, j] * b[j] for j in b) for i in a)

    def add(a, weight, b):
        out = dict(a)
        for i, value in b.items():
            out[i] = out[i] + weight * value if i in out else weight * value
        return out

    rest_of, way, found = {0: one}, {0: one}, {}
    norm = gram[0, 0]
    for step in range(ITERS):
        product = {i + 1: growth[i + 1] * value for i, value in way.items()}
        alpha = norm / inner(way, product)
        found = add(found, alpha, way)
        rest_of = add(rest_of, -alpha, product)
        if step < ITERS - 1:
            following = inner(rest_of, rest_of)
            way = add(rest_of, following / norm, way)
            norm = following
    found = {i: value * ratio[i][0] for i, value in found.items()}
    rest_of = {i: value * ratio[i][0] for i, value in rest_of.items()}
    for i in range(z.blocks):
        for h in range(z.halves):
            part = slice(h * LANES, (h + 1) * LANES)
            values = [f[i, :, part] for f in fields]
            multipliers[:, i, part] = sum(c * values[j] for j, c in found.items())
            residual[:, i, part] = sum(c * values[j] for j, c in rest_of.items())


def call(body, outs, scratch, cost, args, table=True, away=()):
    args = [
        pltpu.with_memory_space_constraint(a, pltpu.HBM) if k in away else a
        for k, a in enumerate(args)
    ]
    specs = [HBM if k in away else VMEM for k in range(len(args))]
    if table:
        specs[0] = SMEM
    shapes = [
        pltpu.SMEM(s, t) if t == jnp.int32 else jax.ShapeDtypeStruct(s, t) for s, t in outs
    ]
    return pl.pallas_call(
        body,
        out_shape=shapes,
        in_specs=specs,
        out_specs=[SMEM if t == jnp.int32 else VMEM for _, t in outs],
        scratch_shapes=scratch,
        compiler_params=pltpu.CompilerParams(vmem_limit_bytes=LIMIT),
        cost_estimate=pl.CostEstimate(flops=cost, bytes_accessed=cost // 16, transcendentals=0),
    )(*args)


def on_device(
    load,
    row_scale,
    diag_blocks,
    off_blocks,
    off_pattern,
    partner,
    corner_coupling,
    corner_index,
    coarse_inverse,
    *,
    mesh,
):
    z = Sizes(load, corner_coupling, coarse_inverse, mesh)
    cols, blocks, width = z.columns, z.blocks, z.width
    field = ((blocks, cols, width), F32)
    other = pltpu.VMEM((blocks + 1, cols, width), F32)
    parts = pltpu.VMEM((blocks, 2 * cols, width), BF16)
    extra = ((cols, z.extra), F32)
    gram = ((cols, 128), F32)
    light, heavy = 4_000_000, 600_000_000

    def piece_shapes(kinds):
        chunks = z.extra_chunks if kinds == 1 else 0
        return [((rows + chunks, cols, LANES), F32) for rows in z.sent(kinds)]

    def kernel(body, *extra_args):
        return functools.partial(body, z, *extra_args)

    def across(piece, m):
        return lax.ppermute(piece, "sub", [(t, t ^ m) for t in range(z.peers)])

    def exchange(kinds, pieces, *sources):
        arrived = [across(piece, m) for m, piece in zip([1] + z.direct, pieces)]
        more = call(
            kernel(relay, kinds), piece_shapes(kinds)[z.first() :], [], light,
            [table, *sources, arrived[0]],
        )
        return arrived + [across(piece, m) for m, piece in zip(z.paired, more)]

    table, loaded, lift, scale, coupling, *pieces = call(
        kernel(begin),
        [
            ((z.table,), jnp.int32),
            field,
            field,
            (row_scale.shape, F32),
            (corner_coupling.shape, BF16),
        ]
        + piece_shapes(2)[: z.first()],
        [
            pltpu.VMEM(load.shape, F32),
            pltpu.SMEM(partner.shape, jnp.int32),
            pltpu.SMEM(off_pattern.shape, jnp.int32),
            pltpu.SMEM((z.peers,), jnp.int32),
            pltpu.SemaphoreType.DMA((5,)),
        ],
        light,
        [partner, off_pattern, load, row_scale, corner_coupling],
        False, range(5),
    )
    arrived = exchange(2, pieces, loaded, lift)
    weight = (diag_blocks.shape, BF16)
    operator, diag, off = call(
        kernel(prepare), [((z.all_corners, z.all_corners), F32), weight, weight],
        [
            pltpu.VMEM(corner_index.shape, jnp.int32),
            pltpu.VMEM(coarse_inverse.shape, F32),
            pltpu.SemaphoreType.DMA((4,)),
        ],
        heavy, [corner_index, coarse_inverse, diag_blocks, off_blocks], False, range(4),
    )
    newest, image, own_extra, *pieces = call(
        kernel(apply_round, 1),
        [field, field, extra] + piece_shapes(1)[: z.first()], [other, parts], heavy,
        [table, *arrived, loaded, scale, diag, off, coupling],
    )
    (jump_lift,) = call(
        kernel(build_lift), [((blocks, 2 * z.all_corners, width), BF16)], [other], heavy,
        [table, operator, lift, *arrived],
    )
    arrived = exchange(1, pieces, image, own_extra)
    fields, totals = [newest], []
    for step in range(2, ITERS + 1):
        older = fields if step == ITERS else []
        newest, image, total, own_extra, *pieces = call(
            kernel(apply_round, step),
            [field, field, extra, extra] + piece_shapes(1)[: z.first()], [other, parts], heavy,
            [table, *arrived, image, own_extra, jump_lift, scale, diag, off, coupling, *older],
        )
        fields.append(newest)
        totals.append(total)
        arrived = exchange(1, pieces, image, own_extra)
    (own_gram,) = call(
        kernel(cluster_gram), [gram], [], light, [operator, own_extra, *arrived, *totals], False
    )
    power = z.groups & (z.groups - 1) == 0
    grams = [own_gram] + [
        lax.ppermute(
            own_gram, "group",
            [(a, a ^ k if power else (a + k) % z.groups) for a in range(z.groups)],
        )
        for k in range(1, z.groups)
    ]
    (newest,) = call(
        kernel(last_vector), [field], [other], light,
        [table, image, own_extra, jump_lift, *arrived],
    )
    multipliers, residual = call(
        kernel(finish), [(load.shape, F32)] * 2, [], light, [*grams, *fields, newest], False
    )
    return multipliers, residual


def solution(mesh):
    return jax.shard_map(
        functools.partial(on_device, mesh=dict(mesh.shape)),
        mesh=mesh,
        in_specs=(
            P(None, ("group", "sub"), None),
            P(("group", "sub"), None),
            P(("group", "sub"), None, None),
            P(("group", "sub"), None, None),
            P(("group", "sub"), None),
            P(("group", "sub"), None),
            P(("group", "sub"), None),
            P("group", None),
            P("group", None),
        ),
        out_specs=(P(None, ("group", "sub"), None), P(None, ("group", "sub"), None)),
        check_vma=False,
    )
```

```python
import functools

import jax
import jax.numpy as jnp
from jax import lax
from jax.experimental import pallas as pl
from jax.experimental.pallas import tpu as pltpu
from jax.sharding import PartitionSpec as P

ITERS = 4
HIGH = lax.Precision.HIGHEST
F32 = jnp.float32
BF16 = jnp.bfloat16
VMEM = pl.BlockSpec(memory_space=pltpu.VMEM)
SMEM = pl.BlockSpec(memory_space=pltpu.SMEM)
HBM = pl.BlockSpec(memory_space=pltpu.HBM)
LIMIT = 24 * 1024 * 1024
LANES = 128
PAIRS = [(i, j) for j in range(ITERS) for i in range(j + 1)]
ENTRIES = len(PAIRS) + ITERS
NN = (((1,), (0,)), ((), ()))
NT = (((1,), (1,)), ((), ()))
TN = (((0,), (0,)), ((), ()))


def dot(a, b, dims):
    return lax.dot_general(a, b, dims, preferred_element_type=F32)


def dot_high(a, b, dims):
    return lax.dot_general(a, b, dims, precision=HIGH, preferred_element_type=F32)


def split(a):
    high = a.astype(BF16).astype(F32)
    return jnp.concatenate([high, a - high], axis=0).astype(BF16)


def fold(a):
    half = a.shape[0] // 2
    return a[:half] + a[half:]


def lane_ids(shape):
    return lax.broadcasted_iota(jnp.int32, shape, 1)


class Sizes:
    def __init__(self, load, corner_coupling, coarse_inverse, mesh):
        self.columns = load.shape[0]
        self.blocks = load.shape[1]
        self.width = load.shape[2]
        self.corners = corner_coupling.shape[0]
        assert self.corners == self.columns
        self.coarse = coarse_inverse.shape[1]
        self.peers = mesh["sub"]
        self.groups = mesh["group"]
        self.capacity = (self.blocks + self.peers - 2) // (self.peers - 1)
        self.all_corners = self.peers * self.corners
        self.max_lane = self.all_corners
        self.gram_lane = self.max_lane + self.peers
        self.extra_chunks = -(-(self.gram_lane + ENTRIES) // LANES)
        self.extra = self.extra_chunks * LANES
        self.halves = self.width // LANES
        evens = range(2, self.peers, 2)
        self.far = sorted(evens, key=lambda m: -m.bit_count())
        self.handed = [m + 1 for m in self.far]
        self.slots = self.peers * self.capacity
        self.inverse = self.slots
        self.pattern = self.inverse + self.blocks
        self.partner = self.pattern + self.blocks
        self.order = self.partner + self.blocks
        self.count = self.order + self.blocks + 1
        self.table = self.count + 1
        most = len(self.far) * self.capacity
        self.early = min(-(-most * 3 // 4), self.blocks)
        self.middle = max(self.early, min(most, self.blocks))

    def rows(self, kinds):
        return kinds * self.capacity * self.halves

    def near_rows(self, kinds):
        return len(self.handed) * self.rows(kinds)

    def sources(self):
        found = [(1, 0, 0)]
        for k, m in enumerate(self.far):
            found += [(m + side, 1 + k, side) for side in range(2)]
        return found


def fill_table(z, partner, pattern, table, counts):
    me = lax.axis_index("sub")
    for entry in range(z.slots):
        table[entry] = z.blocks
    for m in range(z.peers):
        counts[m] = 0
    for i in range(z.blocks):
        mate = partner[0, i]
        source = pattern[0, i]
        m = mate ^ me
        rank = counts[m]
        table[m * z.capacity + rank] = i
        counts[m] = rank + 1
        table[z.inverse + source] = i
        table[z.pattern + i] = source
        table[z.partner + i] = mate
    place = jnp.int32(0)
    for m in z.handed + z.far + [1]:
        for r in range(z.capacity):
            block = table[m * z.capacity + r]
            table[z.order + place] = block
            place = place + (block < z.blocks).astype(jnp.int32)
        if m == z.handed[-1]:
            table[z.count] = place


def fill_piece(z, table, sources, m, piece, row):
    for source in sources:
        for r in range(z.capacity):
            value = source[jnp.minimum(table[m * z.capacity + r], z.blocks - 1)]
            for h in range(z.halves):
                piece[row] = value[:, h * LANES : (h + 1) * LANES]
                row += 1


def fill_near(z, table, sources, near):
    for k, m in enumerate(z.handed):
        fill_piece(z, table, sources, m, near, k * z.rows(len(sources)))


def store_extra(z, tile, piece, row):
    for j in range(z.extra_chunks):
        piece[row + j] = tile[:, j * LANES : (j + 1) * LANES]


def load_extra(z, piece, row):
    return jnp.concatenate([piece[row + j] for j in range(z.extra_chunks)], axis=1)


def relay(z, kinds, late, table, *rest):
    sources, rest = rest[:kinds], rest[kinds:]
    if kinds == 1:
        extra, rest = rest[0], rest[1:]
    near, rest = rest[0], rest[1:]
    if late:
        beside, rest = rest[0], rest[1:]
    rows = z.rows(kinds)
    if kinds == 1:
        tile = extra[...] + load_extra(z, near, z.near_rows(1))
        if late:
            tile = tile + load_extra(z, beside, rows)
    for k, (m, piece) in enumerate(zip(z.far, rest)):
        fill_piece(z, table, sources, m, piece, 0)
        for row in range(rows):
            piece[rows + row] = near[k * rows + row]
        if kinds == 1:
            store_extra(z, tile, piece, 2 * rows)


def place(z, table, arrived, kind, kinds, target):
    for m, transfer, piece in z.sources():
        row = piece * z.rows(kinds) + z.rows(kind)
        for r in range(z.capacity):
            block = table[m * z.capacity + r]
            for h in range(z.halves):
                target[block, :, h * LANES : (h + 1) * LANES] = arrived[transfer][row]
                row += 1


def begin(z, partner, pattern, load, scale, coupling, table, field, lift, wide, coupling_out, near, beside, *scratch):
    here, scale_here, partner_here, pattern_here, counts, sems = scratch
    copies = [
        pltpu.make_async_copy(a, b, sems.at[k])
        for k, (a, b) in enumerate(
            [
                (partner, partner_here),
                (pattern, pattern_here),
                (load, here),
                (scale, scale_here),
                (coupling, coupling_out),
            ]
        )
    ]
    for copy in copies:
        copy.start()
    copies[0].wait()
    copies[1].wait()
    fill_table(z, partner_here, pattern_here, table, counts)
    for copy in copies[2:]:
        copy.wait()
    for i in range(z.blocks):
        field[i] = here[:, i, :]
        row = jnp.broadcast_to(scale_here[i : i + 1, :], (z.columns, z.width))
        wide[i] = row
        lift[i] = row * coupling_out[:, i * z.width : (i + 1) * z.width].astype(F32)
    fill_near(z, table, [field, lift], near)
    fill_piece(z, table, [field, lift], 1, beside, 0)


def split3(a):
    high = a.astype(BF16).astype(F32)
    middle = (a - high).astype(BF16).astype(F32)
    return [high, middle, a - high - middle]


def prepare(z, index_in, inverse_in, diag, off, operator, diag_out, off_out, index, inverse, sems):
    copies = [
        pltpu.make_async_copy(a, b, sems.at[k])
        for k, (a, b) in enumerate(
            [(index_in, index), (inverse_in, inverse), (diag, diag_out), (off, off_out)]
        )
    ]
    for copy in copies:
        copy.start()
    copies[0].wait()
    copies[1].wait()
    rows = lax.broadcasted_iota(jnp.int32, (z.coarse, z.all_corners), 0)
    select = (rows == index[...]).astype(BF16)
    parts = jnp.concatenate(split3(inverse[...]), axis=0).astype(BF16)
    half = dot(parts, select, NN)
    half = sum(half[k * z.coarse : (k + 1) * z.coarse] for k in range(3))
    parts = jnp.concatenate(split3(half), axis=1).astype(BF16)
    full = dot(select, parts, TN)
    operator[...] = sum(full[:, k * z.all_corners : (k + 1) * z.all_corners] for k in range(3))
    copies[2].wait()
    copies[3].wait()


def build_lift(z, table, operator, lift, *rest):
    pieces, (jump_lift, other) = rest[:-2], rest[-2:]
    place(z, table, pieces, 1, 2, other)
    me = lax.axis_index("sub")
    own = operator[pl.ds(pl.multiple_of(me * z.corners, z.corners), z.corners), :]
    for i in range(z.blocks):
        at = pl.multiple_of(table[z.partner + i] * z.corners, z.corners)
        left = split(jnp.concatenate([own, -operator[pl.ds(at, z.corners), :]], axis=0))
        right = split(jnp.concatenate([lift[i], other[i]], axis=0))
        count = 2 * z.corners
        left = jnp.concatenate([left, left[:count]], axis=0)
        right = jnp.concatenate([right[:count], right[:count], right[count:]], axis=0)
        jump_lift[i] = split(dot(left, right, TN))


def extra_sum(z, own, near, beside, *far):
    total = own[...] + load_extra(z, near, z.near_rows(1))
    if beside is not None:
        total = total + load_extra(z, beside, z.rows(1))
    for piece in far:
        total = total + load_extra(z, piece, 2 * z.rows(1))
    return total


def cluster_max(z, total):
    lanes = lane_ids(total.shape)
    own = (lanes >= z.max_lane) & (lanes < z.gram_lane)
    return jnp.max(jnp.where(own, total, 0.0), axis=1, keepdims=True)


def corner_rows(z, total):
    rows = split(total[:, : z.all_corners])
    return jnp.concatenate([rows, rows], axis=1)


def lane_sum(a):
    return jnp.sum(a, axis=1, keepdims=True)


def couple(z, table, position, wide, diag, off, parts, field, image):
    i = table[z.order + position]
    source = table[z.inverse + i]
    mine = parts[i]
    coupled = dot(mine, diag[i], NT) + dot(mine, diag[i], NN)
    coupled = coupled + dot(parts[table[z.pattern + i]], off[i], NT)
    coupled = coupled + dot(parts[source], off[source], NN)
    row = wide[i]
    image[i] = row * (row * field[i] + fold(coupled))


def first_half(z, step, table, *rest):
    rest = list(rest)
    take = lambda n: [rest.pop(0) for _ in range(n)]
    beside, *far = take(1 + len(z.far))
    (before,) = take(1)
    if step > 1:
        near, own_extra, jump_lift = take(3)
    wide, diag, off, coupling = take(4)
    field, image, parts = take(3)
    if step > 1:
        (total_out,) = take(1)
    extra, near_out, other = rest
    place(z, table, [beside, *far], 0, 2 if step == 1 else 1, other)
    if step > 1:
        total = extra_sum(z, own_extra, near, None, *far)
        total_out[...] = total
        rows = corner_rows(z, total)
        shrink = 1.0 / cluster_max(z, total)
    partial = jnp.zeros((2 * z.columns, z.corners), F32)
    top = jnp.zeros((z.columns, z.width), F32)
    for i in range(z.blocks):
        value = before[i] - other[i]
        if step > 1:
            value = (value + fold(dot(rows, jump_lift[i], NN))) * shrink
        field[i] = value
        scaled = wide[i] * value
        top = jnp.maximum(top, jnp.abs(wide[i] * scaled))
        mine = split(scaled)
        parts[i] = mine
        partial = partial + dot(mine, coupling[:, i * z.width : (i + 1) * z.width], NT)
    work = functools.partial(couple, z, table)
    refs = (wide, diag, off, parts, field, image)
    for position in range(z.early):
        work(position, *refs)

    @pl.when(table[z.count] > z.early)
    def _():
        for position in range(z.early, z.middle):
            work(position, *refs)

    fill_near(z, table, [image], near_out)
    me = lax.axis_index("sub")
    lanes = lane_ids((z.columns, z.extra))
    sums = fold(partial)
    padded = jnp.concatenate(
        [sums, jnp.zeros((z.columns, z.extra - z.corners), F32)], axis=1
    )
    tile = pltpu.roll(padded, me * z.corners, 1)
    tile = jnp.where(lanes == z.max_lane + me, jnp.max(top, axis=1, keepdims=True), tile)
    extra[...] = tile
    store_extra(z, tile, near_out, z.near_rows(1))


def second_half(z, last, table, wide, diag, off, parts, field, image_in, *rest):
    rest = list(rest)
    take = lambda n: [rest.pop(0) for _ in range(n)]
    extra, *older = take(ITERS) if last else (None,)
    image, beside = take(2)
    work = functools.partial(couple, z, table)
    refs = (wide, diag, off, parts, field, image)
    for i in range(z.blocks):
        image[i] = image_in[i]

    @pl.when(table[z.count] <= z.early)
    def _():
        for position in range(z.early, z.middle):
            work(position, *refs)

    for position in range(z.middle, z.blocks):
        work(position, *refs)
    fill_piece(z, table, [image], 1, beside, 0)
    if last:
        (extra_out,) = rest
        lanes = lane_ids((z.columns, z.extra))
        tile = jnp.zeros((z.columns, z.extra), F32)
        fields = older + [field]
        products = [(fields[i], fields[j]) for i, j in PAIRS] + [(f, image) for f in fields]
        for entry, (a, b) in enumerate(products):
            acc = a[0] * b[0]
            for i in range(1, z.blocks):
                acc = acc + a[i] * b[i]
            tile = jnp.where(lanes == z.gram_lane + entry, lane_sum(acc), tile)
        extra_out[...] = extra[...] + tile
        store_extra(z, tile, beside, z.rows(1))


def cluster_gram(z, operator, own_extra, near, beside, *rest):
    count = len(z.far)
    far, totals, (gram,) = rest[:count], rest[count:-1], rest[-1:]
    total = extra_sum(z, own_extra, near, beside, *far)
    totals = [t[...] for t in totals]
    partials = [t[:, : z.all_corners] for t in totals + [total]]
    lifted = dot_high(partials[-1], operator[...], NT)
    lanes = lane_ids(gram.shape)
    tile = jnp.zeros(gram.shape, F32)
    for entry in range(ENTRIES):
        lane = z.gram_lane + entry
        value = total[:, lane : lane + 1]
        if entry >= len(PAIRS):
            value = 2.0 * (value + lane_sum(partials[entry - len(PAIRS)] * lifted))
        tile = jnp.where(lanes == entry, value, tile)
    for step, t in enumerate(totals):
        tile = jnp.where(lanes == ENTRIES + step, cluster_max(z, t), tile)
    gram[...] = tile


def last_vector(z, table, before, own_extra, jump_lift, near, beside, *rest):
    far, (field, other) = rest[:-2], rest[-2:]
    place(z, table, [beside, *far], 0, 1, other)
    rows = corner_rows(z, extra_sum(z, own_extra, near, beside, *far))
    for i in range(z.blocks):
        field[i] = before[i] - other[i] + fold(dot(rows, jump_lift[i], NN))


def finish(z, *rest):
    grams, rest = rest[: z.groups], rest[z.groups :]
    fields, (multipliers, residual) = rest[:-2], rest[-2:]
    tables = [gram[...] for gram in grams]
    shape = (z.columns, LANES)
    lanes = lane_ids(shape)

    def column(table, lane):
        return jnp.broadcast_to(table[:, lane : lane + 1], shape)

    one = jnp.ones(shape, F32)
    ratio = [[one] * z.groups]
    growth = [None]
    for step in range(1, ITERS + 1):
        grown = ratio[-1]
        if step < ITERS:
            grown = [q * column(t, ENTRIES + step - 1) for q, t in zip(grown, tables)]
        top = functools.reduce(jnp.maximum, grown)
        inverse = 1.0 / top
        ratio.append([q * inverse for q in grown])
        growth.append(top)
    pairs = PAIRS + [(i, ITERS) for i in range(ITERS)]

    def lanes_of(side, level):
        chosen = [e for e, pair in enumerate(pairs) if pair[side] == level]
        return functools.reduce(jnp.logical_or, [lanes == e for e in chosen])

    where = [[lanes_of(side, level) for level in range(side, ITERS + side)] for side in range(2)]
    total = jnp.zeros(shape, F32)
    for g, table in enumerate(tables):
        for side in range(2):
            weight = one
            for level in range(1, ITERS + side):
                weight = jnp.where(where[side][level - side], ratio[level][g], weight)
            table = table * weight
        total = total + table
    gram = {}
    for entry, (i, j) in enumerate(pairs):
        gram[i, j] = gram[j, i] = column(total, entry)

    def inner(a, b):
        return sum(a[i] * sum(gram[i, j] * b[j] for j in b) for i in a)

    def add(a, weight, b):
        out = dict(a)
        for i, value in b.items():
            out[i] = out[i] + weight * value if i in out else weight * value
        return out

    rest_of, way, found = {0: one}, {0: one}, {}
    norm = gram[0, 0]
    for step in range(ITERS):
        product = {i + 1: growth[i + 1] * value for i, value in way.items()}
        alpha = norm / inner(way, product)
        found = add(found, alpha, way)
        rest_of = add(rest_of, -alpha, product)
        if step < ITERS - 1:
            following = inner(rest_of, rest_of)
            way = add(rest_of, following / norm, way)
            norm = following
    found = {i: value * ratio[i][0] for i, value in found.items()}
    rest_of = {i: value * ratio[i][0] for i, value in rest_of.items()}
    for i in range(z.blocks):
        for h in range(z.halves):
            part = slice(h * LANES, (h + 1) * LANES)
            values = [f[i, :, part] for f in fields]
            multipliers[:, i, part] = sum(c * values[j] for j, c in found.items())
            residual[:, i, part] = sum(c * values[j] for j, c in rest_of.items())


def call(body, outs, scratch, cost, args, table=True, away=()):
    args = [
        pltpu.with_memory_space_constraint(a, pltpu.HBM) if k in away else a
        for k, a in enumerate(args)
    ]
    specs = [HBM if k in away else VMEM for k in range(len(args))]
    if table:
        specs[0] = SMEM
    shapes = [
        pltpu.SMEM(s, t) if t == jnp.int32 else jax.ShapeDtypeStruct(s, t) for s, t in outs
    ]
    return pl.pallas_call(
        body,
        out_shape=shapes,
        in_specs=specs,
        out_specs=[SMEM if t == jnp.int32 else VMEM for _, t in outs],
        scratch_shapes=scratch,
        compiler_params=pltpu.CompilerParams(vmem_limit_bytes=LIMIT),
        cost_estimate=pl.CostEstimate(flops=cost, bytes_accessed=cost // 16, transcendentals=0),
    )(*args)


def on_device(
    load,
    row_scale,
    diag_blocks,
    off_blocks,
    off_pattern,
    partner,
    corner_coupling,
    corner_index,
    coarse_inverse,
    *,
    mesh,
):
    z = Sizes(load, corner_coupling, coarse_inverse, mesh)
    cols, blocks, width = z.columns, z.blocks, z.width
    field = ((blocks, cols, width), F32)
    other = pltpu.VMEM((blocks + 1, cols, width), F32)
    extra = ((cols, z.extra), F32)
    gram = ((cols, 128), F32)
    light, heavy = 4_000_000, 600_000_000

    def shape(rows, kinds):
        return ((rows + (z.extra_chunks if kinds == 1 else 0), cols, LANES), F32)

    def near_shapes(kinds):
        return [shape(z.near_rows(kinds), kinds), shape(z.rows(kinds), kinds)]

    def kernel(body, *extra_args):
        return functools.partial(body, z, *extra_args)

    def across(piece, m):
        return lax.ppermute(piece, "sub", [(t, t ^ m) for t in range(z.peers)])

    def far_exchange(kinds, sources, near, late=()):
        pieces = call(
            kernel(relay, kinds, len(late) > 0),
            [shape(2 * z.rows(kinds), kinds)] * len(z.far), [], light,
            [table, *sources, near, *late],
        )
        return [across(piece, m) for m, piece in zip(z.far, pieces)]

    table, loaded, lift, wide, coupling, near, beside = call(
        kernel(begin),
        [((z.table,), jnp.int32), field, field, field, (corner_coupling.shape, BF16)]
        + near_shapes(2),
        [
            pltpu.VMEM(load.shape, F32),
            pltpu.VMEM(row_scale.shape, F32),
            pltpu.SMEM(partner.shape, jnp.int32),
            pltpu.SMEM(off_pattern.shape, jnp.int32),
            pltpu.SMEM((z.peers,), jnp.int32),
            pltpu.SemaphoreType.DMA((5,)),
        ],
        light,
        [partner, off_pattern, load, row_scale, corner_coupling],
        False, range(5),
    )
    near = across(near, 1)
    beside = across(beside, 1)
    arrived = [beside, *far_exchange(2, [loaded, lift], near)]
    weight = (diag_blocks.shape, BF16)
    operator, diag, off = call(
        kernel(prepare), [((z.all_corners, z.all_corners), F32), weight, weight],
        [
            pltpu.VMEM(corner_index.shape, jnp.int32),
            pltpu.VMEM(coarse_inverse.shape, F32),
            pltpu.SemaphoreType.DMA((4,)),
        ],
        heavy, [corner_index, coarse_inverse, diag_blocks, off_blocks], False, range(4),
    )
    half = ((blocks, 2 * cols, width), BF16)
    fields, totals = [], []
    image, own_extra, jump_lift = loaded, None, None
    for step in range(1, ITERS + 1):
        last = step == ITERS
        more = [near, own_extra, jump_lift] if step > 1 else []
        newest, part, parts, *total, own_extra, near = call(
            kernel(first_half, step),
            [field, field, half] + [extra] * (step > 1) + [extra, near_shapes(1)[0]],
            [other], heavy, [table, *arrived, image, *more, wide, diag, off, coupling],
        )
        near = across(near, 1)
        older = [own_extra, *fields] if last else []
        image, beside, *finished = call(
            kernel(second_half, last),
            [field, near_shapes(1)[1]] + [extra] * last, [], heavy,
            [table, wide, diag, off, parts, newest, part, *older],
        )
        beside = across(beside, 1)
        fields.append(newest)
        totals += total
        if step == 1:
            (jump_lift,) = call(
                kernel(build_lift), [((blocks, 2 * z.all_corners, width), BF16)], [other], heavy,
                [table, operator, lift, *arrived],
            )
        if last:
            (own_extra,) = finished
        late = [beside] if last else []
        arrived = [beside, *far_exchange(1, [image, own_extra], near, late)]
    (own_gram,) = call(
        kernel(cluster_gram), [gram], [], light,
        [operator, own_extra, near, *arrived, *totals], False,
    )
    power = z.groups & (z.groups - 1) == 0
    grams = [own_gram] + [
        lax.ppermute(
            own_gram, "group",
            [(a, a ^ k if power else (a + k) % z.groups) for a in range(z.groups)],
        )
        for k in range(1, z.groups)
    ]
    (newest,) = call(
        kernel(last_vector), [field], [other], light,
        [table, image, own_extra, jump_lift, near, *arrived],
    )
    multipliers, residual = call(
        kernel(finish), [(load.shape, F32)] * 2, [], light, [*grams, *fields, newest], False
    )
    return multipliers, residual


def solution(mesh):
    return jax.shard_map(
        functools.partial(on_device, mesh=dict(mesh.shape)),
        mesh=mesh,
        in_specs=(
            P(None, ("group", "sub"), None),
            P(("group", "sub"), None),
            P(("group", "sub"), None, None),
            P(("group", "sub"), None, None),
            P(("group", "sub"), None),
            P(("group", "sub"), None),
            P(("group", "sub"), None),
            P("group", None),
            P("group", None),
        ),
        out_specs=(P(None, ("group", "sub"), None), P(None, ("group", "sub"), None)),
        check_vma=False,
    )
```

```python
import functools

import jax
import jax.numpy as jnp
from jax import lax
from jax.experimental import pallas as pl
from jax.experimental.pallas import tpu as pltpu
from jax.sharding import PartitionSpec as P

ITERS = 4
HIGH = lax.Precision.HIGHEST
F32 = jnp.float32
BF16 = jnp.bfloat16
VMEM = pl.BlockSpec(memory_space=pltpu.VMEM)
SMEM = pl.BlockSpec(memory_space=pltpu.SMEM)
HBM = pl.BlockSpec(memory_space=pltpu.HBM)
LIMIT = 24 * 1024 * 1024
LANES = 128
PAIRS = [(i, j) for j in range(ITERS) for i in range(j + 1)]
ENTRIES = len(PAIRS) + ITERS
NN = (((1,), (0,)), ((), ()))
NT = (((1,), (1,)), ((), ()))
TN = (((0,), (0,)), ((), ()))


def dot(a, b, dims):
    return lax.dot_general(a, b, dims, preferred_element_type=F32)


def dot_high(a, b, dims):
    return lax.dot_general(a, b, dims, precision=HIGH, preferred_element_type=F32)


def split(a):
    high = a.astype(BF16).astype(F32)
    return jnp.concatenate([high, a - high], axis=0).astype(BF16)


def fold(a):
    half = a.shape[0] // 2
    return a[:half] + a[half:]


def lane_ids(shape):
    return lax.broadcasted_iota(jnp.int32, shape, 1)


class Sizes:
    def __init__(self, load, corner_coupling, coarse_inverse, mesh):
        self.columns = load.shape[0]
        self.blocks = load.shape[1]
        self.width = load.shape[2]
        self.corners = corner_coupling.shape[0]
        assert self.corners == self.columns
        self.coarse = coarse_inverse.shape[1]
        self.peers = mesh["sub"]
        self.groups = mesh["group"]
        self.capacity = (self.blocks + self.peers - 2) // (self.peers - 1)
        self.all_corners = self.peers * self.corners
        self.max_lane = self.all_corners
        self.gram_lane = self.max_lane + self.peers
        self.extra_chunks = -(-(self.gram_lane + ENTRIES) // LANES)
        self.extra = self.extra_chunks * LANES
        self.halves = self.width // LANES
        evens = range(2, self.peers, 2)
        self.beyond = [m for m in evens if m & (m - 1)]
        self.beside = [m for m in evens if m & (m - 1) == 0]
        self.far = self.beyond + self.beside
        self.handed = [m + 1 for m in self.far]
        self.slots = self.peers * self.capacity
        self.inverse = self.slots
        self.pattern = self.inverse + self.blocks
        self.partner = self.pattern + self.blocks
        self.order = self.partner + self.blocks
        self.count = self.order + self.blocks + 1
        self.table = self.count + 1
        most = len(self.far) * self.capacity
        self.early = min(-(-most * 3 // 4), self.blocks)
        self.middle = max(self.early, min(most, self.blocks))

    def rows(self, kinds):
        return kinds * self.capacity * self.halves

    def near_rows(self, kinds):
        return len(self.handed) * self.rows(kinds)

    def at(self, k, core):
        first = len(self.beyond)
        return k if k < first else first + (k - first + core) % len(self.beside)

    def mine(self, k):
        core = lax.axis_index("sub") & 1
        at = [self.at(k, c) for c in range(2)]
        return tuple(
            jnp.where(core == 0, jnp.int32(a), jnp.int32(b))
            for a, b in [at, [self.far[n] for n in at]]
        )

    def sources(self):
        found = [(1, 0, 0)]
        for k in range(len(self.far)):
            _, m = self.mine(k)
            found += [(m + side, 1 + k, side) for side in range(2)]
        return found


def fill_table(z, partner, pattern, table, counts):
    me = lax.axis_index("sub")
    for entry in range(z.slots):
        table[entry] = z.blocks
    for m in range(z.peers):
        counts[m] = 0
    for i in range(z.blocks):
        mate = partner[0, i]
        source = pattern[0, i]
        m = mate ^ me
        rank = counts[m]
        table[m * z.capacity + rank] = i
        counts[m] = rank + 1
        table[z.inverse + source] = i
        table[z.pattern + i] = source
        table[z.partner + i] = mate
    place = jnp.int32(0)
    for m in z.handed + z.far + [1]:
        for r in range(z.capacity):
            block = table[m * z.capacity + r]
            table[z.order + place] = block
            place = place + (block < z.blocks).astype(jnp.int32)
        if m == z.handed[-1]:
            table[z.count] = place


def fill_piece(z, table, sources, m, piece, row):
    for source in sources:
        for r in range(z.capacity):
            value = source[jnp.minimum(table[m * z.capacity + r], z.blocks - 1)]
            for h in range(z.halves):
                piece[row] = value[:, h * LANES : (h + 1) * LANES]
                row += 1


def fill_near(z, table, sources, near):
    for k, m in enumerate(z.handed):
        fill_piece(z, table, sources, m, near, k * z.rows(len(sources)))


def store_extra(z, tile, piece, row):
    for j in range(z.extra_chunks):
        piece[row + j] = tile[:, j * LANES : (j + 1) * LANES]


def load_extra(z, piece, row):
    return jnp.concatenate([piece[row + j] for j in range(z.extra_chunks)], axis=1)


def relay(z, kinds, table, *rest):
    sources, rest = rest[:kinds], rest[kinds:]
    if kinds == 1:
        extra, rest = rest[0], rest[1:]
    near, pieces = rest[0], rest[1:]
    rows = z.rows(kinds)
    if kinds == 1:
        tile = extra[...] + load_extra(z, near, z.near_rows(1))
    for k, piece in enumerate(pieces):
        which, m = z.mine(k)
        fill_piece(z, table, sources, m, piece, 0)
        for row in range(rows):
            piece[rows + row] = near[which * rows + row]
        if kinds == 1:
            store_extra(z, tile, piece, 2 * rows)


def place(z, table, arrived, kind, kinds, target):
    for m, transfer, piece in z.sources():
        row = piece * z.rows(kinds) + z.rows(kind)
        for r in range(z.capacity):
            block = table[m * z.capacity + r]
            for h in range(z.halves):
                target[block, :, h * LANES : (h + 1) * LANES] = arrived[transfer][row]
                row += 1


def begin(z, partner, pattern, load, scale, coupling, table, field, lift, wide, corners, near, beside, *scratch):
    here, scale_here, coupling_here, partner_here, pattern_here, counts, sems = scratch
    copies = [
        pltpu.make_async_copy(a, b, sems.at[k])
        for k, (a, b) in enumerate(
            [
                (partner, partner_here),
                (pattern, pattern_here),
                (load, here),
                (scale, scale_here),
                (coupling, coupling_here),
            ]
        )
    ]
    for copy in copies:
        copy.start()
    copies[0].wait()
    copies[1].wait()
    fill_table(z, partner_here, pattern_here, table, counts)
    for copy in copies[2:]:
        copy.wait()
    for i in range(z.blocks):
        field[i] = here[:, i, :]
        row = jnp.broadcast_to(scale_here[i : i + 1, :], (z.columns, z.width))
        wide[i] = row
        part = coupling_here[:, i * z.width : (i + 1) * z.width].astype(F32)
        lift[i] = row * part
        corners[i] = jnp.concatenate([part, jnp.zeros_like(part)], axis=0).astype(BF16)
    fill_near(z, table, [field, lift], near)
    fill_piece(z, table, [field, lift], 1, beside, 0)


def split3(a):
    high = a.astype(BF16).astype(F32)
    middle = (a - high).astype(BF16).astype(F32)
    return [high, middle, a - high - middle]


def prepare(z, index_in, inverse_in, diag, off, operator, diag_out, off_out, index, inverse, sems):
    copies = [
        pltpu.make_async_copy(a, b, sems.at[k])
        for k, (a, b) in enumerate(
            [(index_in, index), (inverse_in, inverse), (diag, diag_out), (off, off_out)]
        )
    ]
    for copy in copies:
        copy.start()
    copies[0].wait()
    copies[1].wait()
    rows = lax.broadcasted_iota(jnp.int32, (z.coarse, z.all_corners), 0)
    select = (rows == index[...]).astype(BF16)
    parts = jnp.concatenate(split3(inverse[...]), axis=0).astype(BF16)
    half = dot(parts, select, NN)
    half = sum(half[k * z.coarse : (k + 1) * z.coarse] for k in range(3))
    parts = jnp.concatenate(split3(half), axis=1).astype(BF16)
    full = dot(select, parts, TN)
    operator[...] = sum(full[:, k * z.all_corners : (k + 1) * z.all_corners] for k in range(3))
    copies[2].wait()
    copies[3].wait()


def build_lift(z, table, operator, lift, wide, diag, off, corners, *rest):
    count = 1 + len(z.far)
    arrived, (jump_lift, image_lift, corner_lift, other, scaled, half) = rest[:count], rest[count:]
    place(z, table, arrived, 1, 2, other)
    me = lax.axis_index("sub")
    own = operator[pl.ds(pl.multiple_of(me * z.corners, z.corners), z.corners), :]
    size = 2 * z.corners
    to_corners = jnp.zeros((2 * z.all_corners, size), F32)
    for i in range(z.blocks):
        at = pl.multiple_of(table[z.partner + i] * z.corners, z.corners)
        left = split(jnp.concatenate([own, -operator[pl.ds(at, z.corners), :]], axis=0))
        right = split(jnp.concatenate([lift[i], other[i]], axis=0))
        left = jnp.concatenate([left, left[:size]], axis=0)
        right = jnp.concatenate([right[:size], right[:size], right[size:]], axis=0)
        jump = dot(left, right, TN)
        jump_lift[i] = split(jump)
        jump = wide[i, 0:1, :] * jump
        scaled[i] = jump
        half[i] = jump.astype(BF16)
        to_corners = to_corners + dot(split(jump), corners[i], NT)
    corner_lift[...] = split(fold(to_corners))
    for i in range(z.blocks):
        source = table[z.inverse + i]
        mine = half[i]
        coupled = dot(mine, diag[i], NT) + dot(mine, diag[i], NN)
        coupled = coupled + dot(half[table[z.pattern + i]], off[i], NT)
        coupled = coupled + dot(half[source], off[source], NN)
        image_lift[i] = split(wide[i, 0:1, :] * (scaled[i] + coupled))


def extra_sum(z, own, near, *far):
    total = own[...] + load_extra(z, near, z.near_rows(1))
    for piece in far:
        total = total + load_extra(z, piece, 2 * z.rows(1))
    return total


def cluster_max(z, total):
    lanes = lane_ids(total.shape)
    own = (lanes >= z.max_lane) & (lanes < z.gram_lane)
    return jnp.max(jnp.where(own, total, 0.0), axis=1, keepdims=True)


def corner_rows(z, total):
    rows = split(total[:, : z.all_corners])
    return jnp.concatenate([rows, rows], axis=1)


def lane_sum(a):
    return jnp.sum(a, axis=1, keepdims=True)


def couple(z, i, table, wide, diag, off, parts, diff, rows, image_lift, shrink):
    source = table[z.inverse + i]
    mine = parts[i]
    coupled = dot(mine, diag[i], NT) + dot(mine, diag[i], NN)
    coupled = coupled + dot(parts[table[z.pattern + i]], off[i], NT)
    coupled = coupled + dot(parts[source], off[source], NN)
    row = wide[i]
    value = row * (row * diff[i] + fold(coupled))
    if rows is not None:
        value = (value + fold(dot(rows, image_lift[i], NN))) * shrink
    return value


def corner_data(z, total):
    return corner_rows(z, total), 1.0 / cluster_max(z, total)


def first_half(z, step, table, *rest):
    first, last = step == 1, step == ITERS
    rest = list(rest)
    take = lambda n: [rest.pop(0) for _ in range(n)]
    beside, *far = take(1 + len(z.far))
    (before,) = take(1)
    if not first:
        near, own_extra, image_lift, corner_lift = take(4)
    wide, diag, off, corners = take(4)
    if last:
        jump_lift, *older = take(ITERS)
    elif not first:
        take(step - 2)
    diff, image = take(2)
    if not last:
        (parts,) = take(1)
    if not first:
        (total_out,) = take(1)
    if last:
        field, beside_out = take(2)
    extra, near_out, other = take(3)
    if last:
        (parts,) = rest
    place(z, table, [beside, *far], 0, 2 if first else 1, other)
    partial = jnp.zeros((2 * z.columns, 2 * z.corners), F32)
    top = jnp.zeros((z.columns, z.width), F32)
    for i in range(z.blocks):
        value = before[i] - other[i]
        diff[i] = value
        scaled = wide[i] * value
        top = jnp.maximum(top, jnp.abs(wide[i] * scaled))
        mine = split(scaled)
        parts[i] = mine
        partial = partial + dot(mine, corners[i], NT)
    sums = fold(partial)
    if first:
        more = (None, None, None)
    else:
        total = extra_sum(z, own_extra, near, *far)
        total_out[...] = total
        rows, shrink = corner_data(z, total)
        sums = (sums + fold(dot(rows, corner_lift[...], NN))) * shrink
        top = top * shrink
        more = (rows, image_lift, shrink)
    refs = (table, wide, diag, off, parts, diff, *more)
    if last:
        for i in range(z.blocks):
            value = couple(z, i, *refs)
            image[i] = value
            top = jnp.maximum(top, jnp.abs(value))
        fill_piece(z, table, [image], 1, beside_out, 0)
    else:
        for position in range(z.early):
            i = table[z.order + position]
            value = couple(z, i, *refs)
            image[i] = value
            top = jnp.maximum(top, jnp.abs(value))

        @pl.when(table[z.count] > z.early)
        def _():
            for position in range(z.early, z.middle):
                i = table[z.order + position]
                image[i] = couple(z, i, *refs)

    fill_near(z, table, [image], near_out)
    me = lax.axis_index("sub")
    lanes = lane_ids((z.columns, z.extra))
    padded = jnp.concatenate(
        [sums, jnp.zeros((z.columns, z.extra - sums.shape[1]), F32)], axis=1
    )
    tile = pltpu.roll(padded, me * z.corners, 1)
    tile = jnp.where(lanes == z.max_lane + me, jnp.max(top, axis=1, keepdims=True), tile)
    if last:
        for i in range(z.blocks):
            field[i] = (diff[i] + fold(dot(rows, jump_lift[i], NN))) * shrink
        fields = older + [field]
        products = [(fields[i], fields[j]) for i, j in PAIRS] + [(f, image) for f in fields]
        for entry, (a, b) in enumerate(products):
            acc = a[0] * b[0]
            for i in range(1, z.blocks):
                acc = acc + a[i] * b[i]
            tile = jnp.where(lanes == z.gram_lane + entry, lane_sum(acc), tile)
    extra[...] = tile
    store_extra(z, tile, near_out, z.near_rows(1))


def second_half(z, first, table, wide, diag, off, parts, diff, image_in, *rest):
    if first:
        image, beside = rest
        more = (None, None, None)
    else:
        total, image_lift, image, beside = rest
        rows, shrink = corner_data(z, total[...])
        more = (rows, image_lift, shrink)
    refs = (table, wide, diag, off, parts, diff, *more)
    for i in range(z.blocks):
        image[i] = image_in[i]

    @pl.when(table[z.count] <= z.early)
    def _():
        for position in range(z.early, z.middle):
            i = table[z.order + position]
            image[i] = couple(z, i, *refs)

    for position in range(z.middle, z.blocks):
        i = table[z.order + position]
        image[i] = couple(z, i, *refs)
    fill_piece(z, table, [image], 1, beside, 0)


def vector(z, total, diff, jump_lift, field):
    rows, shrink = corner_data(z, total[...])
    for i in range(z.blocks):
        field[i] = (diff[i] + fold(dot(rows, jump_lift[i], NN))) * shrink


def cluster_gram(z, operator, own_extra, near, *rest):
    count = len(z.far)
    far, totals, (gram,) = rest[:count], rest[count:-1], rest[-1:]
    total = extra_sum(z, own_extra, near, *far)
    totals = [t[...] for t in totals]
    partials = [t[:, : z.all_corners] for t in totals + [total]]
    lifted = dot_high(partials[-1], operator[...], NT)
    lanes = lane_ids(gram.shape)
    tile = jnp.zeros(gram.shape, F32)
    for entry in range(ENTRIES):
        lane = z.gram_lane + entry
        value = total[:, lane : lane + 1]
        if entry >= len(PAIRS):
            value = 2.0 * (value + lane_sum(partials[entry - len(PAIRS)] * lifted))
        tile = jnp.where(lanes == entry, value, tile)
    for step, t in enumerate(totals):
        tile = jnp.where(lanes == ENTRIES + step, cluster_max(z, t), tile)
    gram[...] = tile


def last_vector(z, table, before, own_extra, jump_lift, near, beside, *rest):
    far, (field, other) = rest[:-2], rest[-2:]
    place(z, table, [beside, *far], 0, 1, other)
    rows = corner_rows(z, extra_sum(z, own_extra, near, *far))
    for i in range(z.blocks):
        field[i] = before[i] - other[i] + fold(dot(rows, jump_lift[i], NN))


def finish(z, *rest):
    grams, rest = rest[: z.groups], rest[z.groups :]
    fields, (multipliers, residual) = rest[:-2], rest[-2:]
    tables = [gram[...] for gram in grams]
    shape = (z.columns, LANES)
    lanes = lane_ids(shape)

    def column(table, lane):
        return jnp.broadcast_to(table[:, lane : lane + 1], shape)

    one = jnp.ones(shape, F32)
    ratio = [[one] * z.groups]
    growth = [None]
    for step in range(1, ITERS + 1):
        grown = ratio[-1]
        if step < ITERS:
            grown = [q * column(t, ENTRIES + step - 1) for q, t in zip(grown, tables)]
        top = functools.reduce(jnp.maximum, grown)
        inverse = 1.0 / top
        ratio.append([q * inverse for q in grown])
        growth.append(top)
    pairs = PAIRS + [(i, ITERS) for i in range(ITERS)]

    def lanes_of(side, level):
        chosen = [e for e, pair in enumerate(pairs) if pair[side] == level]
        return functools.reduce(jnp.logical_or, [lanes == e for e in chosen])

    where = [[lanes_of(side, level) for level in range(side, ITERS + side)] for side in range(2)]
    total = jnp.zeros(shape, F32)
    for g, table in enumerate(tables):
        for side in range(2):
            weight = one
            for level in range(1, ITERS + side):
                weight = jnp.where(where[side][level - side], ratio[level][g], weight)
            table = table * weight
        total = total + table
    gram = {}
    for entry, (i, j) in enumerate(pairs):
        gram[i, j] = gram[j, i] = column(total, entry)

    def inner(a, b):
        return sum(a[i] * sum(gram[i, j] * b[j] for j in b) for i in a)

    def add(a, weight, b):
        out = dict(a)
        for i, value in b.items():
            out[i] = out[i] + weight * value if i in out else weight * value
        return out

    rest_of, way, found = {0: one}, {0: one}, {}
    norm = gram[0, 0]
    for step in range(ITERS):
        product = {i + 1: growth[i + 1] * value for i, value in way.items()}
        alpha = norm / inner(way, product)
        found = add(found, alpha, way)
        rest_of = add(rest_of, -alpha, product)
        if step < ITERS - 1:
            following = inner(rest_of, rest_of)
            way = add(rest_of, following / norm, way)
            norm = following
    found = {i: value * ratio[i][0] for i, value in found.items()}
    rest_of = {i: value * ratio[i][0] for i, value in rest_of.items()}
    for i in range(z.blocks):
        for h in range(z.halves):
            part = slice(h * LANES, (h + 1) * LANES)
            values = [f[i, :, part] for f in fields]
            multipliers[:, i, part] = sum(c * values[j] for j, c in found.items())
            residual[:, i, part] = sum(c * values[j] for j, c in rest_of.items())


def call(body, outs, scratch, cost, args, table=True, away=()):
    args = [
        pltpu.with_memory_space_constraint(a, pltpu.HBM) if k in away else a
        for k, a in enumerate(args)
    ]
    specs = [HBM if k in away else VMEM for k in range(len(args))]
    if table:
        specs[0] = SMEM
    shapes = [
        pltpu.SMEM(s, t) if t == jnp.int32 else jax.ShapeDtypeStruct(s, t) for s, t in outs
    ]
    return pl.pallas_call(
        body,
        out_shape=shapes,
        in_specs=specs,
        out_specs=[SMEM if t == jnp.int32 else VMEM for _, t in outs],
        scratch_shapes=scratch,
        compiler_params=pltpu.CompilerParams(vmem_limit_bytes=LIMIT),
        cost_estimate=pl.CostEstimate(flops=cost, bytes_accessed=cost // 16, transcendentals=0),
    )(*args)


def on_device(
    load,
    row_scale,
    diag_blocks,
    off_blocks,
    off_pattern,
    partner,
    corner_coupling,
    corner_index,
    coarse_inverse,
    *,
    mesh,
):
    z = Sizes(load, corner_coupling, coarse_inverse, mesh)
    cols, blocks, width = z.columns, z.blocks, z.width
    field = ((blocks, cols, width), F32)
    other = pltpu.VMEM((blocks + 1, cols, width), F32)
    extra = ((cols, z.extra), F32)
    gram = ((cols, 128), F32)
    light, heavy = 4_000_000, 600_000_000

    def shape(rows, kinds):
        return ((rows + (z.extra_chunks if kinds == 1 else 0), cols, LANES), F32)

    def near_shapes(kinds):
        return [shape(z.near_rows(kinds), kinds), ((z.rows(kinds), cols, LANES), F32)]

    def kernel(body, *extra_args):
        return functools.partial(body, z, *extra_args)

    def across(piece, mask_of):
        pairs = [(t, t ^ mask_of(t & 1)) for t in range(z.peers)]
        return lax.ppermute(piece, "sub", pairs)

    def to_near(piece):
        return across(piece, lambda core: 1)

    def far_exchange(kinds, sources, near):
        pieces = call(
            kernel(relay, kinds), [shape(2 * z.rows(kinds), kinds)] * len(z.far), [], light,
            [table, *sources, near],
        )
        return [
            across(piece, lambda core: z.far[z.at(k, core)]) for k, piece in enumerate(pieces)
        ]

    table, loaded, lift, wide, corners, near, beside = call(
        kernel(begin),
        [((z.table,), jnp.int32), field, field, field, ((blocks, 2 * z.corners, width), BF16)]
        + near_shapes(2),
        [
            pltpu.VMEM(load.shape, F32),
            pltpu.VMEM(row_scale.shape, F32),
            pltpu.VMEM(corner_coupling.shape, BF16),
            pltpu.SMEM(partner.shape, jnp.int32),
            pltpu.SMEM(off_pattern.shape, jnp.int32),
            pltpu.SMEM((z.peers,), jnp.int32),
            pltpu.SemaphoreType.DMA((5,)),
        ],
        light,
        [partner, off_pattern, load, row_scale, corner_coupling],
        False, range(5),
    )
    near = to_near(near)
    beside = to_near(beside)
    arrived = [beside, *far_exchange(2, [loaded, lift], near)]
    weight = (diag_blocks.shape, BF16)
    operator, diag, off = call(
        kernel(prepare), [((z.all_corners, z.all_corners), F32), weight, weight],
        [
            pltpu.VMEM(corner_index.shape, jnp.int32),
            pltpu.VMEM(coarse_inverse.shape, F32),
            pltpu.SemaphoreType.DMA((4,)),
        ],
        heavy, [corner_index, coarse_inverse, diag_blocks, off_blocks], False, range(4),
    )
    half = ((blocks, 2 * cols, width), BF16)
    coarse = (2 * z.all_corners, width)
    fixed = [wide, diag, off, corners]
    fields, totals = [], []
    image = loaded
    for step in range(1, ITERS + 1):
        first, last = step == 1, step == ITERS
        more = [] if first else [near, own_extra, image_lift, corner_lift]
        older = [jump_lift, *fields] if last else fields[1:]
        near_shape, beside_shape = near_shapes(1)
        diff, part, *rest = call(
            kernel(first_half, step),
            [field, field] + [half] * (not last) + [extra] * (not first)
            + [field, beside_shape] * last + [extra, near_shape],
            [other] + [pltpu.VMEM(*half)] * last, heavy,
            [table, *arrived, image, *more, *fixed, *older],
        )
        parts = None if last else rest.pop(0)
        if not first:
            totals.append(rest.pop(0))
        if last:
            fields.append(rest.pop(0))
            image, beside = part, rest.pop(0)
        own_extra, near = rest
        near = to_near(near)
        if not last:
            more = [] if first else [totals[-1], image_lift]
            image, beside = call(
                kernel(second_half, first), [field, beside_shape], [], heavy,
                [table, wide, diag, off, parts, diff, part, *more],
            )
        beside = to_near(beside)
        if first:
            fields.append(diff)
            jump_lift, image_lift, corner_lift = call(
                kernel(build_lift),
                [((blocks, *coarse), BF16)] * 2 + [((coarse[0], 2 * z.corners), BF16)],
                [
                    other,
                    pltpu.VMEM((blocks, z.all_corners, width), F32),
                    pltpu.VMEM((blocks, z.all_corners, width), BF16),
                ],
                heavy, [table, operator, lift, *fixed, *arrived],
            )
        elif not last:
            fields += call(
                kernel(vector), [field], [], heavy, [totals[-1], diff, jump_lift], False
            )
        arrived = [beside, *far_exchange(1, [image, own_extra], near)]
    (own_gram,) = call(
        kernel(cluster_gram), [gram], [], light,
        [operator, own_extra, near, *arrived[1:], *totals], False,
    )
    power = z.groups & (z.groups - 1) == 0
    grams = [own_gram] + [
        lax.ppermute(
            own_gram, "group",
            [(a, a ^ k if power else (a + k) % z.groups) for a in range(z.groups)],
        )
        for k in range(1, z.groups)
    ]
    (newest,) = call(
        kernel(last_vector), [field], [other], light,
        [table, image, own_extra, jump_lift, near, *arrived],
    )
    multipliers, residual = call(
        kernel(finish), [(load.shape, F32)] * 2, [], light, [*grams, *fields, newest], False
    )
    return multipliers, residual


def solution(mesh):
    return jax.shard_map(
        functools.partial(on_device, mesh=dict(mesh.shape)),
        mesh=mesh,
        in_specs=(
            P(None, ("group", "sub"), None),
            P(("group", "sub"), None),
            P(("group", "sub"), None, None),
            P(("group", "sub"), None, None),
            P(("group", "sub"), None),
            P(("group", "sub"), None),
            P(("group", "sub"), None),
            P("group", None),
            P("group", None),
        ),
        out_specs=(P(None, ("group", "sub"), None), P(None, ("group", "sub"), None)),
        check_vma=False,
    )
```

```python
import functools

import jax
import jax.numpy as jnp
from jax import lax
from jax.experimental import pallas as pl
from jax.experimental.pallas import tpu as pltpu
from jax.sharding import PartitionSpec as P

ITERS = 4
HIGH = lax.Precision.HIGHEST
F32 = jnp.float32
BF16 = jnp.bfloat16
VMEM = pl.BlockSpec(memory_space=pltpu.VMEM)
SMEM = pl.BlockSpec(memory_space=pltpu.SMEM)
HBM = pl.BlockSpec(memory_space=pltpu.HBM)
LIMIT = 24 * 1024 * 1024
LANES = 128
RR, DP, RP, PP = range(4)
NN = (((1,), (0,)), ((), ()))
NT = (((1,), (1,)), ((), ()))
TN = (((0,), (0,)), ((), ()))


def dot(a, b, dims):
    return lax.dot_general(a, b, dims, preferred_element_type=F32)


def dot_high(a, b, dims):
    return lax.dot_general(a, b, dims, precision=HIGH, preferred_element_type=F32)


def pad(a):
    return jnp.concatenate([a, jnp.zeros_like(a)], axis=0).astype(BF16)


def split(a):
    high = a.astype(BF16).astype(F32)
    return jnp.concatenate([high, a - high], axis=0).astype(BF16)


def fold(a):
    half = a.shape[0] // 2
    return a[:half] + a[half:]


def lane_ids(shape):
    return lax.broadcasted_iota(jnp.int32, shape, 1)


class Sizes:
    def __init__(self, load, corner_coupling, coarse_inverse, mesh):
        self.columns = load.shape[0]
        self.blocks = load.shape[1]
        self.width = load.shape[2]
        self.corners = corner_coupling.shape[0]
        assert self.corners == self.columns
        self.coarse = coarse_inverse.shape[1]
        self.peers = mesh["sub"]
        self.groups = mesh["group"]
        self.capacity = (self.blocks + self.peers - 2) // (self.peers - 1)
        self.all_corners = self.peers * self.corners
        self.extra_chunks = -(-self.all_corners // LANES)
        self.extra = self.extra_chunks * LANES
        self.halves = self.width // LANES
        evens = range(2, self.peers, 2)
        self.beyond = [m for m in evens if m & (m - 1)]
        self.beside = [m for m in evens if m & (m - 1) == 0]
        self.far = self.beyond + self.beside
        self.handed = [m + 1 for m in self.far]
        self.slots = self.peers * self.capacity
        self.inverse = self.slots
        self.pattern = self.inverse + self.blocks
        self.partner = self.pattern + self.blocks
        self.order = self.partner + self.blocks
        self.count = self.order + self.blocks + 1
        self.table = self.count + 1
        most = len(self.far) * self.capacity
        self.early = min(-(-most * 7 // 8), self.blocks)
        self.middle = max(self.early, min(most, self.blocks))

    def rows(self, kinds):
        return kinds * self.capacity * self.halves

    def near_rows(self, kinds):
        return len(self.handed) * self.rows(kinds)

    def at(self, k, core):
        first = len(self.beyond)
        return k if k < first else first + (k - first + core) % len(self.beside)

    def mine(self, k):
        core = lax.axis_index("sub") & 1
        at = [self.at(k, c) for c in range(2)]
        return tuple(
            jnp.where(core == 0, jnp.int32(a), jnp.int32(b))
            for a, b in [at, [self.far[n] for n in at]]
        )

    def sources(self):
        found = [(1, 0, 0)]
        for k in range(len(self.far)):
            _, m = self.mine(k)
            found += [(m + side, 1 + k, side) for side in range(2)]
        return found


def fill_table(z, partner, pattern, table, counts):
    me = lax.axis_index("sub")
    for entry in range(z.slots):
        table[entry] = z.blocks
    for m in range(z.peers):
        counts[m] = 0
    for i in range(z.blocks):
        mate = partner[0, i]
        source = pattern[0, i]
        m = mate ^ me
        rank = counts[m]
        table[m * z.capacity + rank] = i
        counts[m] = rank + 1
        table[z.inverse + source] = i
        table[z.pattern + i] = source
        table[z.partner + i] = mate
    place = jnp.int32(0)
    for m in z.handed + z.far + [1]:
        for r in range(z.capacity):
            block = table[m * z.capacity + r]
            table[z.order + place] = block
            place = place + (block < z.blocks).astype(jnp.int32)
        if m == z.handed[-1]:
            table[z.count] = place


def fill_piece(z, table, sources, m, piece, row):
    for source in sources:
        for r in range(z.capacity):
            value = source[jnp.minimum(table[m * z.capacity + r], z.blocks - 1)]
            for h in range(z.halves):
                piece[row] = value[:, h * LANES : (h + 1) * LANES]
                row += 1


def fill_near(z, table, sources, near):
    for k, m in enumerate(z.handed):
        fill_piece(z, table, sources, m, near, k * z.rows(len(sources)))


def store_extra(z, tile, piece, row):
    for j in range(z.extra_chunks):
        piece[row + j] = tile[:, j * LANES : (j + 1) * LANES]


def load_extra(z, piece, row):
    return jnp.concatenate([piece[row + j] for j in range(z.extra_chunks)], axis=1)


def relay(z, kinds, table, *rest):
    sources, rest = rest[:kinds], rest[kinds:]
    if kinds == 1:
        extra, rest = rest[0], rest[1:]
    near, pieces, beside = rest[0], rest[1:-1], rest[-1]
    rows = z.rows(kinds)
    fill_piece(z, table, sources, 1, beside, 0)
    if kinds == 1:
        tile = extra[...] + load_extra(z, near, z.near_rows(1))
    for k, piece in enumerate(pieces):
        which, m = z.mine(k)
        fill_piece(z, table, sources, m, piece, 0)
        for row in range(rows):
            piece[rows + row] = near[which * rows + row]
        if kinds == 1:
            store_extra(z, tile, piece, 2 * rows)


def place(z, table, arrived, kind, kinds, target):
    for m, transfer, piece in z.sources():
        row = piece * z.rows(kinds) + z.rows(kind)
        for r in range(z.capacity):
            block = table[m * z.capacity + r]
            for h in range(z.halves):
                target[block, :, h * LANES : (h + 1) * LANES] = arrived[transfer][row]
                row += 1


def begin(z, partner, pattern, load, scale, coupling, table, field, lift, wide, corners, near, *scratch):
    here, scale_here, coupling_here, partner_here, pattern_here, counts, sems = scratch
    copies = [
        pltpu.make_async_copy(a, b, sems.at[k])
        for k, (a, b) in enumerate(
            [
                (partner, partner_here),
                (pattern, pattern_here),
                (load, here),
                (scale, scale_here),
                (coupling, coupling_here),
            ]
        )
    ]
    for copy in copies:
        copy.start()
    copies[0].wait()
    copies[1].wait()
    fill_table(z, partner_here, pattern_here, table, counts)
    for copy in copies[2:]:
        copy.wait()
    for i in range(z.blocks):
        field[i] = here[:, i, :]
        row = jnp.broadcast_to(scale_here[i : i + 1, :], (z.columns, z.width))
        wide[i] = row
        part = coupling_here[:, i * z.width : (i + 1) * z.width].astype(F32)
        lift[i] = row * part
        corners[i] = jnp.concatenate([part, jnp.zeros_like(part)], axis=0).astype(BF16)
    fill_near(z, table, [field, lift], near)


def split3(a):
    high = a.astype(BF16).astype(F32)
    middle = (a - high).astype(BF16).astype(F32)
    return [high, middle, a - high - middle]


def prepare(z, index_in, inverse_in, diag, off, operator, diag_out, off_out, index, inverse, sems):
    copies = [
        pltpu.make_async_copy(a, b, sems.at[k])
        for k, (a, b) in enumerate(
            [(index_in, index), (inverse_in, inverse), (diag, diag_out), (off, off_out)]
        )
    ]
    for copy in copies:
        copy.start()
    copies[0].wait()
    copies[1].wait()
    rows = lax.broadcasted_iota(jnp.int32, (z.coarse, z.all_corners), 0)
    select = (rows == index[...]).astype(BF16)
    parts = jnp.concatenate(split3(inverse[...]), axis=0).astype(BF16)
    half = dot(parts, select, NN)
    half = sum(half[k * z.coarse : (k + 1) * z.coarse] for k in range(3))
    parts = jnp.concatenate(split3(half), axis=1).astype(BF16)
    full = dot(select, parts, TN)
    operator[...] = sum(full[:, k * z.all_corners : (k + 1) * z.all_corners] for k in range(3))
    copies[2].wait()
    copies[3].wait()


def build_lift(z, table, lift, *rest):
    count = 1 + len(z.far)
    arrived, (jump_lift, other, full) = rest[:count], rest[count:]
    place(z, table, [arrived[-1], *arrived[:-1]], 1, 2, other)
    me = lax.axis_index("sub")
    for i in range(z.blocks):
        full[i] = jnp.zeros((z.all_corners, z.width), F32)
        own = pl.multiple_of(me * z.corners, z.corners)
        theirs = pl.multiple_of(table[z.partner + i] * z.corners, z.corners)
        full[i, pl.ds(own, z.corners), :] = lift[i]
        full[i, pl.ds(theirs, z.corners), :] = -other[i]
        jump_lift[i] = split(full[i])


def extra_sum(z, own, near, *far):
    total = own[...] + load_extra(z, near, z.near_rows(1))
    for piece in far:
        total = total + load_extra(z, piece, 2 * z.rows(1))
    return total


def lane_sum(a):
    return jnp.sum(a, axis=1, keepdims=True)


def column(table, lane):
    return jnp.broadcast_to(table[:, lane : lane + 1], table.shape)


def scalars(z, gathered):
    shape = (z.columns, LANES)
    zero = jnp.zeros(shape, F32)
    count = gathered.shape[0]
    unroll = 32 if count % 32 == 0 else 1
    total = lax.fori_loop(0, count, lambda k, acc: acc + gathered[k], zero, unroll=unroll)
    norm = column(total, RR)
    alpha = norm / column(total, DP)

    def squares(k, acc):
        tile = gathered[k]
        step = alpha * pltpu.roll(tile, LANES // 2, 1)
        return acc + tile * step * step

    moved = lax.fori_loop(0, count, squares, zero, unroll=unroll)
    following = norm - 2.0 * alpha * column(total, RP) + column(moved, PP)
    return alpha, following / norm


def across_block(z, tile):
    return jnp.concatenate([tile] * z.halves, axis=1)


def couple(z, i, table, wide, diag, off, parts):
    source = table[z.inverse + i]
    mine = parts[i]
    coupled = dot(mine, diag[i], NT) + dot(mine, diag[i], NN)
    coupled = coupled + dot(parts[table[z.pattern + i]], off[i], NT)
    coupled = coupled + dot(parts[source], off[source], NN)
    return wide[i] * fold(coupled + mine.astype(F32))


def first_half(z, step, table, *rest):
    rest = list(rest)
    take = lambda n: [rest.pop(0) for _ in range(n)]
    wide, diag, off, corners = take(4)
    if step == 0:
        *far, beside, loaded = take(2 + len(z.far))
        residual, image, parts, extra, near_out, other = rest
        direction = residual
        place(z, table, [beside, *far], 0, 2, other)
    else:
        gathered, before, way, product = take(4)
        residual, direction, step_out, image, parts, extra, near_out = rest
        alpha, beta = scalars(z, gathered)
        step_out[...] = alpha
        alpha, beta = across_block(z, alpha), across_block(z, beta)
    partial = jnp.zeros((2 * z.columns, 2 * z.corners), F32)
    for i in range(z.blocks):
        if step == 0:
            value = loaded[i] - other[i]
            residual[i] = value
        else:
            value = before[i] - alpha * product[i]
            residual[i] = value
            value = value + beta * way[i]
            direction[i] = value
        mine = pad(wide[i] * value)
        parts[i] = mine
        partial = partial + dot(mine, corners[i], NT)
    refs = (table, wide, diag, off, parts)
    for position in range(z.early):
        i = table[z.order + position]
        image[i] = couple(z, i, *refs)

    @pl.when(table[z.count] > z.early)
    def _():
        for position in range(z.early, z.middle):
            i = table[z.order + position]
            image[i] = couple(z, i, *refs)

    fill_near(z, table, [image], near_out)
    sums = fold(partial)
    padded = jnp.concatenate(
        [sums, jnp.zeros((z.columns, z.extra - sums.shape[1]), F32)], axis=1
    )
    tile = pltpu.roll(padded, lax.axis_index("sub") * z.corners, 1)
    extra[...] = tile
    store_extra(z, tile, near_out, z.near_rows(1))


def second_half(z, step, table, wide, diag, off, parts, image_in, *rest):
    if step == 0:
        (image,) = rest
    elif step == 1:
        alpha, way, image, multipliers = rest
    else:
        alpha, way, before, image, multipliers = rest
    refs = (table, wide, diag, off, parts)
    for i in range(z.blocks):
        image[i] = image_in[i]

    @pl.when(table[z.count] <= z.early)
    def _():
        for position in range(z.early, z.middle):
            i = table[z.order + position]
            image[i] = couple(z, i, *refs)

    for position in range(z.middle, z.blocks):
        i = table[z.order + position]
        image[i] = couple(z, i, *refs)
    if step > 0:
        size = across_block(z, alpha[...])
        for i in range(z.blocks):
            value = size * way[i]
            multipliers[i] = value if step == 1 else before[i] + value


def finish_product(z, table, operator, image, own_extra, jump_lift, residual, direction, near, *rest):
    *far, beside, product, sent, other = rest
    place(z, table, [beside, *far], 0, 1, other)
    partials = extra_sum(z, own_extra, near, *far)[:, : z.all_corners]
    local = dot_high(partials, operator[...], NT)
    rows = pad(jnp.concatenate([local, local], axis=1))
    zero = jnp.zeros((z.columns, z.width), F32)
    sums = [zero] * 3
    top = zero
    for i in range(z.blocks):
        value = image[i] - other[i] + fold(dot(rows, jump_lift[i], NN))
        product[i] = value
        top = jnp.maximum(top, jnp.abs(value))
        r, d = residual[i], direction[i]
        sums = [s + a * b for s, (a, b) in zip(sums, [(r, r), (d, value), (r, value)])]
    top = jnp.max(top, axis=1, keepdims=True)
    shrink = jnp.where(top > 0.0, 1.0 / top, 0.0)
    squares = zero
    for i in range(z.blocks):
        value = product[i] * shrink
        squares = squares + value * value
    lanes = lane_ids((z.columns, LANES))
    tile = jnp.where(lanes == PP + LANES // 2, top, 0.0)
    for lane, value in zip([RR, DP, RP, PP], sums + [squares]):
        tile = jnp.where(lanes == lane, lane_sum(value), tile)
    for k in range(sent.shape[0]):
        sent[k] = tile


def finish(z, gathered, before, residual_in, direction, product, multipliers, residual):
    alpha, _ = scalars(z, gathered)
    for i in range(z.blocks):
        for h in range(z.halves):
            part = slice(h * LANES, (h + 1) * LANES)
            multipliers[:, i, part] = before[i, :, part] + alpha * direction[i, :, part]
            residual[:, i, part] = residual_in[i, :, part] - alpha * product[i, :, part]


def call(body, outs, scratch, cost, args, table=True, away=()):
    args = [
        pltpu.with_memory_space_constraint(a, pltpu.HBM) if k in away else a
        for k, a in enumerate(args)
    ]
    specs = [HBM if k in away else VMEM for k in range(len(args))]
    if table:
        specs[0] = SMEM
    shapes = [
        pltpu.SMEM(s, t) if t == jnp.int32 else jax.ShapeDtypeStruct(s, t) for s, t in outs
    ]
    return pl.pallas_call(
        body,
        out_shape=shapes,
        in_specs=specs,
        out_specs=[SMEM if t == jnp.int32 else VMEM for _, t in outs],
        scratch_shapes=scratch,
        compiler_params=pltpu.CompilerParams(vmem_limit_bytes=LIMIT),
        cost_estimate=pl.CostEstimate(flops=cost, bytes_accessed=cost // 16, transcendentals=0),
    )(*args)


def on_device(
    load,
    row_scale,
    diag_blocks,
    off_blocks,
    off_pattern,
    partner,
    corner_coupling,
    corner_index,
    coarse_inverse,
    *,
    mesh,
):
    z = Sizes(load, corner_coupling, coarse_inverse, mesh)
    cols, blocks, width = z.columns, z.blocks, z.width
    field = ((blocks, cols, width), F32)
    other = pltpu.VMEM((blocks + 1, cols, width), F32)
    extra = ((cols, z.extra), F32)
    light, heavy = 4_000_000, 600_000_000

    def shape(rows, kinds):
        return ((rows + (z.extra_chunks if kinds == 1 else 0), cols, LANES), F32)

    def kernel(body, *extra_args):
        return functools.partial(body, z, *extra_args)

    def across(piece, mask_of):
        pairs = [(t, t ^ mask_of(t & 1)) for t in range(z.peers)]
        return lax.ppermute(piece, "sub", pairs)

    def to_near(piece):
        return across(piece, lambda core: 1)

    def exchange(kinds, sources, near):
        *pieces, beside = call(
            kernel(relay, kinds),
            [shape(2 * z.rows(kinds), kinds)] * (len(z.far) + 1), [], light, [table, *sources, near],
        )
        far = [across(piece, lambda core: z.far[z.at(k, core)]) for k, piece in enumerate(pieces)]
        return [*far, to_near(beside)]

    table, loaded, lift, wide, corners, near = call(
        kernel(begin),
        [((z.table,), jnp.int32), field, field, field, ((blocks, 2 * z.corners, width), BF16)]
        + [shape(z.near_rows(2), 2)],
        [
            pltpu.VMEM(load.shape, F32),
            pltpu.VMEM(row_scale.shape, F32),
            pltpu.VMEM(corner_coupling.shape, BF16),
            pltpu.SMEM(partner.shape, jnp.int32),
            pltpu.SMEM(off_pattern.shape, jnp.int32),
            pltpu.SMEM((z.peers,), jnp.int32),
            pltpu.SemaphoreType.DMA((5,)),
        ],
        light,
        [partner, off_pattern, load, row_scale, corner_coupling],
        False, range(5),
    )
    arrived = exchange(2, [loaded, lift], to_near(near))
    weight = (diag_blocks.shape, BF16)
    operator, diag, off = call(
        kernel(prepare), [((z.all_corners, z.all_corners), F32), weight, weight],
        [
            pltpu.VMEM(corner_index.shape, jnp.int32),
            pltpu.VMEM(coarse_inverse.shape, F32),
            pltpu.SemaphoreType.DMA((4,)),
        ],
        heavy, [corner_index, coarse_inverse, diag_blocks, off_blocks], False, range(4),
    )
    half = ((blocks, 2 * cols, width), BF16)
    tile = ((cols, LANES), F32)
    devices = z.groups * z.peers
    fixed = [wide, diag, off, corners]
    multipliers = None
    for step in range(ITERS):
        early = [field, half, extra, shape(z.near_rows(1), 1)]
        if step == 0:
            residual, part, parts, own_extra, near = call(
                kernel(first_half, step), [field] + early, [other], heavy,
                [table, *fixed, *arrived, loaded],
            )
            direction = residual
            older = []
        else:
            way = direction
            residual, direction, alpha, part, parts, own_extra, near = call(
                kernel(first_half, step), [field, field, tile] + early, [], heavy,
                [table, *fixed, gathered, residual, way, product],
            )
            older = [alpha, way] + [multipliers] * (step > 1)
        near = to_near(near)
        image, *more = call(
            kernel(second_half, step), [field] + [field] * (step > 0), [], heavy,
            [table, wide, diag, off, parts, part, *older],
        )
        if more:
            (multipliers,) = more
        if step == 0:
            (jump_lift,) = call(
                kernel(build_lift), [((blocks, 2 * z.all_corners, width), BF16)],
                [other, pltpu.VMEM((blocks, z.all_corners, width), F32)], heavy,
                [table, lift, *arrived],
            )
        arrived = exchange(1, [image, own_extra], near)
        product, sent = call(
            kernel(finish_product), [field, ((devices, cols, LANES), F32)], [other], heavy,
            [table, operator, image, own_extra, jump_lift, residual, direction, near, *arrived],
        )
        gathered = lax.all_to_all(sent, ("group", "sub"), 0, 0, tiled=True)
    multipliers, residual = call(
        kernel(finish), [(load.shape, F32)] * 2, [], light,
        [gathered, multipliers, residual, direction, product], False,
    )
    return multipliers, residual


def solution(mesh):
    return jax.shard_map(
        functools.partial(on_device, mesh=dict(mesh.shape)),
        mesh=mesh,
        in_specs=(
            P(None, ("group", "sub"), None),
            P(("group", "sub"), None),
            P(("group", "sub"), None, None),
            P(("group", "sub"), None, None),
            P(("group", "sub"), None),
            P(("group", "sub"), None),
            P(("group", "sub"), None),
            P("group", None),
            P("group", None),
        ),
        out_specs=(P(None, ("group", "sub"), None), P(None, ("group", "sub"), None)),
        check_vma=False,
    )
```

```python
import functools

import jax
import jax.numpy as jnp
from jax import lax
from jax.experimental import pallas as pl
from jax.experimental.pallas import tpu as pltpu
from jax.sharding import PartitionSpec as P

ITERS = 4
HIGH = lax.Precision.HIGHEST
F32 = jnp.float32
BF16 = jnp.bfloat16
VMEM = pl.BlockSpec(memory_space=pltpu.VMEM)
SMEM = pl.BlockSpec(memory_space=pltpu.SMEM)
HBM = pl.BlockSpec(memory_space=pltpu.HBM)
LIMIT = 24 * 1024 * 1024
LANES = 128
RR, DP, RP, PP = range(4)
NN = (((1,), (0,)), ((), ()))
NT = (((1,), (1,)), ((), ()))
TN = (((0,), (0,)), ((), ()))


def dot(a, b, dims):
    return lax.dot_general(a, b, dims, preferred_element_type=F32)


def dot_high(a, b, dims):
    return lax.dot_general(a, b, dims, precision=HIGH, preferred_element_type=F32)


def pad(a):
    return jnp.concatenate([a, jnp.zeros_like(a)], axis=0).astype(BF16)


def split(a):
    high = a.astype(BF16).astype(F32)
    return jnp.concatenate([high, a - high], axis=0).astype(BF16)


def fold(a):
    half = a.shape[0] // 2
    return a[:half] + a[half:]


def lane_ids(shape):
    return lax.broadcasted_iota(jnp.int32, shape, 1)


class Sizes:
    def __init__(self, load, corner_coupling, coarse_inverse, mesh):
        self.columns = load.shape[0]
        self.blocks = load.shape[1]
        self.width = load.shape[2]
        self.corners = corner_coupling.shape[0]
        assert self.corners == self.columns
        self.coarse = coarse_inverse.shape[1]
        self.peers = mesh["sub"]
        self.groups = mesh["group"]
        self.capacity = (self.blocks + self.peers - 2) // (self.peers - 1)
        self.all_corners = self.peers * self.corners
        self.extra_chunks = -(-self.all_corners // LANES)
        self.extra = self.extra_chunks * LANES
        self.halves = self.width // LANES
        evens = range(2, self.peers, 2)
        self.beyond = [m for m in evens if m & (m - 1)]
        self.beside = [m for m in evens if m & (m - 1) == 0]
        self.far = self.beyond + self.beside
        self.handed = [m + 1 for m in self.far]
        self.slots = self.peers * self.capacity
        self.inverse = self.slots
        self.pattern = self.inverse + self.blocks
        self.partner = self.pattern + self.blocks
        self.order = self.partner + self.blocks
        self.count = self.order + self.blocks + 1
        self.table = self.count + 1
        most = len(self.far) * self.capacity
        self.early = min(-(-most * 7 // 8), self.blocks)
        self.middle = max(self.early, min(most, self.blocks))

    def rows(self, kinds):
        return kinds * self.capacity * self.halves

    def near_rows(self, kinds):
        return len(self.handed) * self.rows(kinds)

    def at(self, k, core):
        first = len(self.beyond)
        return k if k < first else first + (k - first + core) % len(self.beside)

    def mine(self, k):
        core = lax.axis_index("sub") & 1
        at = [self.at(k, c) for c in range(2)]
        return tuple(
            jnp.where(core == 0, jnp.int32(a), jnp.int32(b))
            for a, b in [at, [self.far[n] for n in at]]
        )

    def sources(self):
        found = [(1, 0, 0)]
        for k in range(len(self.far)):
            _, m = self.mine(k)
            found += [(m + side, 1 + k, side) for side in range(2)]
        return found


def fill_table(z, partner, pattern, table, counts):
    me = lax.axis_index("sub")
    for entry in range(z.slots):
        table[entry] = z.blocks
    for m in range(z.peers):
        counts[m] = 0
    for i in range(z.blocks):
        mate = partner[0, i]
        source = pattern[0, i]
        m = mate ^ me
        rank = counts[m]
        table[m * z.capacity + rank] = i
        counts[m] = rank + 1
        table[z.inverse + source] = i
        table[z.pattern + i] = source
        table[z.partner + i] = mate
    place = jnp.int32(0)
    for m in z.handed + z.far + [1]:
        for r in range(z.capacity):
            block = table[m * z.capacity + r]
            table[z.order + place] = block
            place = place + (block < z.blocks).astype(jnp.int32)
        if m == z.handed[-1]:
            table[z.count] = place


def fill_piece(z, table, sources, m, piece, row):
    for source in sources:
        for r in range(z.capacity):
            value = source[jnp.minimum(table[m * z.capacity + r], z.blocks - 1)]
            for h in range(z.halves):
                piece[row] = value[:, h * LANES : (h + 1) * LANES]
                row += 1


def fill_near(z, table, sources, near):
    for k, m in enumerate(z.handed):
        fill_piece(z, table, sources, m, near, k * z.rows(len(sources)))


def store_extra(z, tile, piece, row):
    for j in range(z.extra_chunks):
        piece[row + j] = tile[:, j * LANES : (j + 1) * LANES]


def load_extra(z, piece, row):
    return jnp.concatenate([piece[row + j] for j in range(z.extra_chunks)], axis=1)


def relay(z, kinds, table, *rest):
    sources, rest = rest[:kinds], rest[kinds:]
    if kinds == 1:
        extra, rest = rest[0], rest[1:]
    near, pieces, beside = rest[0], rest[1:-1], rest[-1]
    rows = z.rows(kinds)
    fill_piece(z, table, sources, 1, beside, 0)
    if kinds == 1:
        tile = extra[...] + load_extra(z, near, z.near_rows(1))
    for k, piece in enumerate(pieces):
        which, m = z.mine(k)
        fill_piece(z, table, sources, m, piece, 0)
        for row in range(rows):
            piece[rows + row] = near[which * rows + row]
        if kinds == 1:
            store_extra(z, tile, piece, 2 * rows)


def place(z, table, arrived, kind, kinds, target):
    for m, transfer, piece in z.sources():
        row = piece * z.rows(kinds) + z.rows(kind)
        for r in range(z.capacity):
            block = table[m * z.capacity + r]
            for h in range(z.halves):
                target[block, :, h * LANES : (h + 1) * LANES] = arrived[transfer][row]
                row += 1


def begin(z, partner, pattern, load, scale, coupling, table, field, lift, wide, corners, near, *scratch):
    here, scale_here, coupling_here, partner_here, pattern_here, counts, sems = scratch
    copies = [
        pltpu.make_async_copy(a, b, sems.at[k])
        for k, (a, b) in enumerate(
            [
                (partner, partner_here),
                (pattern, pattern_here),
                (load, here),
                (scale, scale_here),
                (coupling, coupling_here),
            ]
        )
    ]
    for copy in copies:
        copy.start()
    copies[0].wait()
    copies[1].wait()
    fill_table(z, partner_here, pattern_here, table, counts)
    for copy in copies[2:]:
        copy.wait()
    for i in range(z.blocks):
        field[i] = here[:, i, :]
        row = jnp.broadcast_to(scale_here[i : i + 1, :], (z.columns, z.width))
        wide[i] = row
        part = coupling_here[:, i * z.width : (i + 1) * z.width].astype(F32)
        lift[i] = row * part
        corners[i] = jnp.concatenate([part, jnp.zeros_like(part)], axis=0).astype(BF16)
    fill_near(z, table, [field, lift], near)


def split3(a):
    high = a.astype(BF16).astype(F32)
    middle = (a - high).astype(BF16).astype(F32)
    return [high, middle, a - high - middle]


def prepare(z, index_in, inverse_in, diag, off, operator, diag_out, off_out, index, inverse, sems):
    copies = [
        pltpu.make_async_copy(a, b, sems.at[k])
        for k, (a, b) in enumerate(
            [(index_in, index), (inverse_in, inverse), (diag, diag_out), (off, off_out)]
        )
    ]
    for copy in copies:
        copy.start()
    copies[0].wait()
    copies[1].wait()
    rows = lax.broadcasted_iota(jnp.int32, (z.coarse, z.all_corners), 0)
    select = (rows == index[...]).astype(BF16)
    parts = jnp.concatenate(split3(inverse[...]), axis=0).astype(BF16)
    half = dot(parts, select, NN)
    half = sum(half[k * z.coarse : (k + 1) * z.coarse] for k in range(3))
    parts = jnp.concatenate(split3(half), axis=1).astype(BF16)
    full = dot(select, parts, TN)
    operator[...] = sum(full[:, k * z.all_corners : (k + 1) * z.all_corners] for k in range(3))
    copies[2].wait()
    copies[3].wait()


def build_lift(z, table, lift, *rest):
    count = 1 + len(z.far)
    arrived, (jump_lift, other, full) = rest[:count], rest[count:]
    place(z, table, [arrived[-1], *arrived[:-1]], 1, 2, other)
    me = lax.axis_index("sub")
    for i in range(z.blocks):
        full[i] = jnp.zeros((z.all_corners, z.width), F32)
        own = pl.multiple_of(me * z.corners, z.corners)
        theirs = pl.multiple_of(table[z.partner + i] * z.corners, z.corners)
        full[i, pl.ds(own, z.corners), :] = lift[i]
        full[i, pl.ds(theirs, z.corners), :] = -other[i]
        jump_lift[i] = split(full[i])


def extra_sum(z, own, near, *far):
    total = own[...] + load_extra(z, near, z.near_rows(1))
    for piece in far:
        total = total + load_extra(z, piece, 2 * z.rows(1))
    return total


def lane_sum(a):
    return jnp.sum(a, axis=1, keepdims=True)


def to_row(z, values):
    shape = (z.columns, LANES)
    lanes = lane_ids(shape)
    rows = lax.broadcasted_iota(jnp.int32, shape, 0)
    tile = jnp.zeros(shape, F32)
    for first, value in values:
        tile = jnp.where(lanes == first + rows, value, tile)
    return jnp.sum(tile, axis=0, keepdims=True)


def to_tile(z, row):
    shape = (z.columns, LANES)
    rows = lax.broadcasted_iota(jnp.int32, shape, 0)
    tile = jnp.where(lane_ids(shape) == rows, jnp.broadcast_to(row, shape), 0.0)
    return jnp.broadcast_to(lane_sum(tile), shape)


def scalars(z, gathered):
    zero = jnp.zeros((1, LANES), F32)
    count = gathered.shape[0]
    unroll = 32 if count % 32 == 0 else 1
    total = lax.fori_loop(0, count, lambda k, acc: acc + gathered[k], zero, unroll=unroll)

    def group(row, at):
        return pltpu.roll(row, LANES - at * z.columns, 1) if at else row

    norm = group(total, RR)
    alpha = norm / group(total, DP)
    placed = pltpu.roll(alpha, PP * z.columns, 1)

    def squares(k, acc):
        row = gathered[k]
        step = placed * pltpu.roll(row, LANES // 2, 1)
        return acc + row * step * step

    moved = lax.fori_loop(0, count, squares, zero, unroll=unroll)
    following = norm - 2.0 * alpha * group(total, RP) + group(moved, PP)
    return to_tile(z, alpha), to_tile(z, following / norm)


def across_block(z, tile):
    return jnp.concatenate([tile] * z.halves, axis=1)


def couple(z, i, table, wide, diag, off, parts):
    source = table[z.inverse + i]
    mine = parts[i]
    coupled = dot(mine, diag[i], NT) + dot(mine, diag[i], NN)
    coupled = coupled + dot(parts[table[z.pattern + i]], off[i], NT)
    coupled = coupled + dot(parts[source], off[source], NN)
    return wide[i] * fold(coupled + mine.astype(F32))


def first_half(z, step, table, *rest):
    rest = list(rest)
    take = lambda n: [rest.pop(0) for _ in range(n)]
    wide, diag, off, corners = take(4)
    if step == 0:
        *far, beside, loaded = take(2 + len(z.far))
        residual, image, parts, extra, near_out, other = rest
        direction = residual
        place(z, table, [beside, *far], 0, 2, other)
    else:
        gathered, before, way, product = take(4)
        residual, direction, step_out, image, parts, extra, near_out = rest
        alpha, beta = scalars(z, gathered)
        step_out[...] = alpha
        alpha, beta = across_block(z, alpha), across_block(z, beta)
    partial = jnp.zeros((2 * z.columns, 2 * z.corners), F32)
    for i in range(z.blocks):
        if step == 0:
            value = loaded[i] - other[i]
            residual[i] = value
        else:
            value = before[i] - alpha * product[i]
            residual[i] = value
            value = value + beta * way[i]
            direction[i] = value
        mine = pad(wide[i] * value)
        parts[i] = mine
        partial = partial + dot(mine, corners[i], NT)
    refs = (table, wide, diag, off, parts)
    for position in range(z.early):
        i = table[z.order + position]
        image[i] = couple(z, i, *refs)

    @pl.when(table[z.count] > z.early)
    def _():
        for position in range(z.early, z.middle):
            i = table[z.order + position]
            image[i] = couple(z, i, *refs)

    fill_near(z, table, [image], near_out)
    sums = fold(partial)
    padded = jnp.concatenate(
        [sums, jnp.zeros((z.columns, z.extra - sums.shape[1]), F32)], axis=1
    )
    tile = pltpu.roll(padded, lax.axis_index("sub") * z.corners, 1)
    extra[...] = tile
    store_extra(z, tile, near_out, z.near_rows(1))


def second_half(z, step, table, wide, diag, off, parts, image_in, *rest):
    if step == 0:
        (image,) = rest
    elif step == 1:
        alpha, way, image, multipliers = rest
    else:
        alpha, way, before, image, multipliers = rest
    refs = (table, wide, diag, off, parts)
    for i in range(z.blocks):
        image[i] = image_in[i]

    @pl.when(table[z.count] <= z.early)
    def _():
        for position in range(z.early, z.middle):
            i = table[z.order + position]
            image[i] = couple(z, i, *refs)

    for position in range(z.middle, z.blocks):
        i = table[z.order + position]
        image[i] = couple(z, i, *refs)
    if step > 0:
        size = across_block(z, alpha[...])
        for i in range(z.blocks):
            value = size * way[i]
            multipliers[i] = value if step == 1 else before[i] + value


def finish_product(z, table, operator, image, own_extra, jump_lift, residual, direction, near, *rest):
    *far, beside, product, sent, other = rest
    place(z, table, [beside, *far], 0, 1, other)
    partials = extra_sum(z, own_extra, near, *far)[:, : z.all_corners]
    local = dot_high(partials, operator[...], NT)
    rows = pad(jnp.concatenate([local, local], axis=1))
    zero = jnp.zeros((z.columns, z.width), F32)
    sums = [zero] * 3
    top = zero
    for i in range(z.blocks):
        value = image[i] - other[i] + fold(dot(rows, jump_lift[i], NN))
        product[i] = value
        top = jnp.maximum(top, jnp.abs(value))
        r, d = residual[i], direction[i]
        sums = [s + a * b for s, (a, b) in zip(sums, [(r, r), (d, value), (r, value)])]
    top = jnp.max(top, axis=1, keepdims=True)
    shrink = jnp.where(top > 0.0, 1.0 / top, 0.0)
    squares = zero
    for i in range(z.blocks):
        value = product[i] * shrink
        squares = squares + value * value
    values = [(k * z.columns, lane_sum(v)) for k, v in enumerate(sums + [squares])]
    row = to_row(z, values + [(PP * z.columns + LANES // 2, top)])
    for k in range(sent.shape[0]):
        sent[k] = row


def finish(z, gathered, before, residual_in, direction, product, multipliers, residual):
    alpha, _ = scalars(z, gathered)
    for i in range(z.blocks):
        for h in range(z.halves):
            part = slice(h * LANES, (h + 1) * LANES)
            multipliers[:, i, part] = before[i, :, part] + alpha * direction[i, :, part]
            residual[:, i, part] = residual_in[i, :, part] - alpha * product[i, :, part]


def call(body, outs, scratch, cost, args, table=True, away=()):
    args = [
        pltpu.with_memory_space_constraint(a, pltpu.HBM) if k in away else a
        for k, a in enumerate(args)
    ]
    specs = [HBM if k in away else VMEM for k in range(len(args))]
    if table:
        specs[0] = SMEM
    shapes = [
        pltpu.SMEM(s, t) if t == jnp.int32 else jax.ShapeDtypeStruct(s, t) for s, t in outs
    ]
    return pl.pallas_call(
        body,
        out_shape=shapes,
        in_specs=specs,
        out_specs=[SMEM if t == jnp.int32 else VMEM for _, t in outs],
        scratch_shapes=scratch,
        compiler_params=pltpu.CompilerParams(vmem_limit_bytes=LIMIT),
        cost_estimate=pl.CostEstimate(flops=cost, bytes_accessed=cost // 16, transcendentals=0),
    )(*args)


def on_device(
    load,
    row_scale,
    diag_blocks,
    off_blocks,
    off_pattern,
    partner,
    corner_coupling,
    corner_index,
    coarse_inverse,
    *,
    mesh,
):
    z = Sizes(load, corner_coupling, coarse_inverse, mesh)
    cols, blocks, width = z.columns, z.blocks, z.width
    field = ((blocks, cols, width), F32)
    other = pltpu.VMEM((blocks + 1, cols, width), F32)
    extra = ((cols, z.extra), F32)
    light, heavy = 4_000_000, 600_000_000

    def shape(rows, kinds):
        return ((rows + (z.extra_chunks if kinds == 1 else 0), cols, LANES), F32)

    def kernel(body, *extra_args):
        return functools.partial(body, z, *extra_args)

    def across(piece, mask_of):
        pairs = [(t, t ^ mask_of(t & 1)) for t in range(z.peers)]
        return lax.ppermute(piece, "sub", pairs)

    def to_near(piece):
        return across(piece, lambda core: 1)

    def exchange(kinds, sources, near):
        *pieces, beside = call(
            kernel(relay, kinds),
            [shape(2 * z.rows(kinds), kinds)] * (len(z.far) + 1), [], light, [table, *sources, near],
        )
        far = [across(piece, lambda core: z.far[z.at(k, core)]) for k, piece in enumerate(pieces)]
        return [*far, to_near(beside)]

    table, loaded, lift, wide, corners, near = call(
        kernel(begin),
        [((z.table,), jnp.int32), field, field, field, ((blocks, 2 * z.corners, width), BF16)]
        + [shape(z.near_rows(2), 2)],
        [
            pltpu.VMEM(load.shape, F32),
            pltpu.VMEM(row_scale.shape, F32),
            pltpu.VMEM(corner_coupling.shape, BF16),
            pltpu.SMEM(partner.shape, jnp.int32),
            pltpu.SMEM(off_pattern.shape, jnp.int32),
            pltpu.SMEM((z.peers,), jnp.int32),
            pltpu.SemaphoreType.DMA((5,)),
        ],
        light,
        [partner, off_pattern, load, row_scale, corner_coupling],
        False, range(5),
    )
    arrived = exchange(2, [loaded, lift], to_near(near))
    weight = (diag_blocks.shape, BF16)
    operator, diag, off = call(
        kernel(prepare), [((z.all_corners, z.all_corners), F32), weight, weight],
        [
            pltpu.VMEM(corner_index.shape, jnp.int32),
            pltpu.VMEM(coarse_inverse.shape, F32),
            pltpu.SemaphoreType.DMA((4,)),
        ],
        heavy, [corner_index, coarse_inverse, diag_blocks, off_blocks], False, range(4),
    )
    half = ((blocks, 2 * cols, width), BF16)
    tile = ((cols, LANES), F32)
    devices = z.groups * z.peers
    fixed = [wide, diag, off, corners]
    multipliers = None
    for step in range(ITERS):
        early = [field, half, extra, shape(z.near_rows(1), 1)]
        if step == 0:
            residual, part, parts, own_extra, near = call(
                kernel(first_half, step), [field] + early, [other], heavy,
                [table, *fixed, *arrived, loaded],
            )
            direction = residual
            older = []
        else:
            way = direction
            residual, direction, alpha, part, parts, own_extra, near = call(
                kernel(first_half, step), [field, field, tile] + early, [], heavy,
                [table, *fixed, gathered, residual, way, product],
            )
            older = [alpha, way] + [multipliers] * (step > 1)
        near = to_near(near)
        image, *more = call(
            kernel(second_half, step), [field] + [field] * (step > 0), [], heavy,
            [table, wide, diag, off, parts, part, *older],
        )
        if more:
            (multipliers,) = more
        if step == 0:
            (jump_lift,) = call(
                kernel(build_lift), [((blocks, 2 * z.all_corners, width), BF16)],
                [other, pltpu.VMEM((blocks, z.all_corners, width), F32)], heavy,
                [table, lift, *arrived],
            )
        arrived = exchange(1, [image, own_extra], near)
        product, sent = call(
            kernel(finish_product), [field, ((devices, 1, LANES), F32)], [other], heavy,
            [table, operator, image, own_extra, jump_lift, residual, direction, near, *arrived],
        )
        gathered = lax.all_to_all(sent, ("group", "sub"), 0, 0, tiled=True)
    multipliers, residual = call(
        kernel(finish), [(load.shape, F32)] * 2, [], light,
        [gathered, multipliers, residual, direction, product], False,
    )
    return multipliers, residual


def solution(mesh):
    return jax.shard_map(
        functools.partial(on_device, mesh=dict(mesh.shape)),
        mesh=mesh,
        in_specs=(
            P(None, ("group", "sub"), None),
            P(("group", "sub"), None),
            P(("group", "sub"), None, None),
            P(("group", "sub"), None, None),
            P(("group", "sub"), None),
            P(("group", "sub"), None),
            P(("group", "sub"), None),
            P("group", None),
            P("group", None),
        ),
        out_specs=(P(None, ("group", "sub"), None), P(None, ("group", "sub"), None)),
        check_vma=False,
    )
```

```python
import functools

import jax
import jax.numpy as jnp
from jax import lax
from jax.experimental import pallas as pl
from jax.experimental.pallas import tpu as pltpu
from jax.sharding import PartitionSpec as P

ITERS = 4
HIGH = lax.Precision.HIGHEST
F32 = jnp.float32
BF16 = jnp.bfloat16
VMEM = pl.BlockSpec(memory_space=pltpu.VMEM)
SMEM = pl.BlockSpec(memory_space=pltpu.SMEM)
HBM = pl.BlockSpec(memory_space=pltpu.HBM)
LIMIT = 24 * 1024 * 1024
LANES = 128
RR, DP, RP, PP = range(4)
NN = (((1,), (0,)), ((), ()))
NT = (((1,), (1,)), ((), ()))
TN = (((0,), (0,)), ((), ()))


def dot(a, b, dims):
    return lax.dot_general(a, b, dims, preferred_element_type=F32)


def dot_high(a, b, dims):
    return lax.dot_general(a, b, dims, precision=HIGH, preferred_element_type=F32)


def pad(a):
    return jnp.concatenate([a, jnp.zeros_like(a)], axis=0).astype(BF16)


def split(a):
    high = a.astype(BF16).astype(F32)
    return jnp.concatenate([high, a - high], axis=0).astype(BF16)


def fold(a):
    half = a.shape[0] // 2
    return a[:half] + a[half:]


def lane_ids(shape):
    return lax.broadcasted_iota(jnp.int32, shape, 1)


class Sizes:
    def __init__(self, load, corner_coupling, coarse_inverse, mesh):
        self.columns = load.shape[0]
        self.blocks = load.shape[1]
        self.width = load.shape[2]
        self.corners = corner_coupling.shape[0]
        assert self.corners == self.columns
        self.coarse = coarse_inverse.shape[1]
        self.peers = mesh["sub"]
        self.groups = mesh["group"]
        self.capacity = (self.blocks + self.peers - 2) // (self.peers - 1)
        self.all_corners = self.peers * self.corners
        self.extra_chunks = -(-self.all_corners // LANES)
        self.extra = self.extra_chunks * LANES
        self.halves = self.width // LANES
        evens = range(2, self.peers, 2)
        self.beyond = [m for m in evens if m & (m - 1)]
        self.beside = [m for m in evens if m & (m - 1) == 0]
        self.far = self.beyond + self.beside
        self.handed = [m + 1 for m in self.far]
        self.slots = self.peers * self.capacity
        self.inverse = self.slots
        self.pattern = self.inverse + self.blocks
        self.partner = self.pattern + self.blocks
        self.order = self.partner + self.blocks
        self.count = self.order + self.blocks + 1
        self.table = self.count + 1
        most = len(self.far) * self.capacity
        self.early = min(-(-most * 7 // 8), self.blocks)
        self.middle = max(self.early, min(most, self.blocks))

    def rows(self, kinds):
        return kinds * self.capacity * self.halves

    def near_rows(self, kinds):
        return len(self.handed) * self.rows(kinds)

    def at(self, k, core):
        first = len(self.beyond)
        return k if k < first else first + (k - first + core) % len(self.beside)

    def mine(self, k):
        core = lax.axis_index("sub") & 1
        at = [self.at(k, c) for c in range(2)]
        return tuple(
            jnp.where(core == 0, jnp.int32(a), jnp.int32(b))
            for a, b in [at, [self.far[n] for n in at]]
        )

    def sources(self):
        found = [(1, 0, 0)]
        for k in range(len(self.far)):
            _, m = self.mine(k)
            found += [(m + side, 1 + k, side) for side in range(2)]
        return found


def fill_table(z, partner, pattern, table, counts):
    me = lax.axis_index("sub")
    for entry in range(z.slots):
        table[entry] = z.blocks
    for m in range(z.peers):
        counts[m] = 0
    for i in range(z.blocks):
        mate = partner[0, i]
        source = pattern[0, i]
        m = mate ^ me
        rank = counts[m]
        table[m * z.capacity + rank] = i
        counts[m] = rank + 1
        table[z.inverse + source] = i
        table[z.pattern + i] = source
        table[z.partner + i] = mate
    place = jnp.int32(0)
    for m in z.handed + z.far + [1]:
        for r in range(z.capacity):
            block = table[m * z.capacity + r]
            table[z.order + place] = block
            place = place + (block < z.blocks).astype(jnp.int32)
        if m == z.handed[-1]:
            table[z.count] = place


def fill_piece(z, table, sources, m, piece, row):
    for source in sources:
        for r in range(z.capacity):
            value = source[jnp.minimum(table[m * z.capacity + r], z.blocks - 1)]
            for h in range(z.halves):
                piece[row] = value[:, h * LANES : (h + 1) * LANES]
                row += 1


def fill_near(z, table, sources, near):
    for k, m in enumerate(z.handed):
        fill_piece(z, table, sources, m, near, k * z.rows(len(sources)))


def store_extra(z, tile, piece, row):
    for j in range(z.extra_chunks):
        piece[row + j] = tile[:, j * LANES : (j + 1) * LANES]


def load_extra(z, piece, row):
    return jnp.concatenate([piece[row + j] for j in range(z.extra_chunks)], axis=1)


def relay(z, kinds, table, *rest):
    sources, rest = rest[:kinds], rest[kinds:]
    if kinds == 1:
        extra, rest = rest[0], rest[1:]
    near, pieces, beside = rest[0], rest[1:-1], rest[-1]
    rows = z.rows(kinds)
    fill_piece(z, table, sources, 1, beside, 0)
    if kinds == 1:
        tile = extra[...] + load_extra(z, near, z.near_rows(1))
    for k, piece in enumerate(pieces):
        which, m = z.mine(k)
        fill_piece(z, table, sources, m, piece, 0)
        for row in range(rows):
            piece[rows + row] = near[which * rows + row]
        if kinds == 1:
            store_extra(z, tile, piece, 2 * rows)


def place(z, table, arrived, kind, kinds, target):
    for m, transfer, piece in z.sources():
        row = piece * z.rows(kinds) + z.rows(kind)
        for r in range(z.capacity):
            block = table[m * z.capacity + r]
            for h in range(z.halves):
                target[block, :, h * LANES : (h + 1) * LANES] = arrived[transfer][row]
                row += 1


def begin(z, partner, pattern, load, scale, coupling, table, field, lift, wide, corners, near, *scratch):
    here, scale_here, coupling_here, partner_here, pattern_here, counts, sems = scratch
    copies = [
        pltpu.make_async_copy(a, b, sems.at[k])
        for k, (a, b) in enumerate(
            [
                (partner, partner_here),
                (pattern, pattern_here),
                (load, here),
                (scale, scale_here),
                (coupling, coupling_here),
            ]
        )
    ]
    for copy in copies:
        copy.start()
    copies[0].wait()
    copies[1].wait()
    fill_table(z, partner_here, pattern_here, table, counts)
    for copy in copies[2:]:
        copy.wait()
    for i in range(z.blocks):
        field[i] = here[:, i, :]
        row = jnp.broadcast_to(scale_here[i : i + 1, :], (z.columns, z.width))
        wide[i] = row
        part = coupling_here[:, i * z.width : (i + 1) * z.width].astype(F32)
        lift[i] = row * part
        corners[i] = jnp.concatenate([part, jnp.zeros_like(part)], axis=0).astype(BF16)
    fill_near(z, table, [field, lift], near)


def split3(a):
    high = a.astype(BF16).astype(F32)
    middle = (a - high).astype(BF16).astype(F32)
    return [high, middle, a - high - middle]


def prepare(z, index_in, inverse_in, diag, off, operator, diag_out, off_out, index, inverse, sems):
    copies = [
        pltpu.make_async_copy(a, b, sems.at[k])
        for k, (a, b) in enumerate(
            [(index_in, index), (inverse_in, inverse), (diag, diag_out), (off, off_out)]
        )
    ]
    for copy in copies:
        copy.start()
    copies[0].wait()
    copies[1].wait()
    rows = lax.broadcasted_iota(jnp.int32, (z.coarse, z.all_corners), 0)
    select = (rows == index[...]).astype(BF16)
    parts = jnp.concatenate(split3(inverse[...]), axis=0).astype(BF16)
    half = dot(parts, select, NN)
    half = sum(half[k * z.coarse : (k + 1) * z.coarse] for k in range(3))
    parts = jnp.concatenate(split3(half), axis=1).astype(BF16)
    full = dot(select, parts, TN)
    operator[...] = sum(full[:, k * z.all_corners : (k + 1) * z.all_corners] for k in range(3))
    copies[2].wait()
    copies[3].wait()


def build_lift(z, table, lift, *rest):
    count = 1 + len(z.far)
    arrived, (jump_lift, other, full) = rest[:count], rest[count:]
    place(z, table, [arrived[-1], *arrived[:-1]], 1, 2, other)
    me = lax.axis_index("sub")
    for i in range(z.blocks):
        full[i] = jnp.zeros((z.all_corners, z.width), F32)
        own = pl.multiple_of(me * z.corners, z.corners)
        theirs = pl.multiple_of(table[z.partner + i] * z.corners, z.corners)
        full[i, pl.ds(own, z.corners), :] = lift[i]
        full[i, pl.ds(theirs, z.corners), :] = -other[i]
        jump_lift[i] = split(full[i])


def extra_sum(z, own, near, *far):
    total = own[...] + load_extra(z, near, z.near_rows(1))
    for piece in far:
        total = total + load_extra(z, piece, 2 * z.rows(1))
    return total


def lane_sum(a):
    return jnp.sum(a, axis=1, keepdims=True)


def to_row(z, values):
    shape = (z.columns, LANES)
    lanes = lane_ids(shape)
    rows = lax.broadcasted_iota(jnp.int32, shape, 0)
    tile = jnp.zeros(shape, F32)
    for first, value in values:
        tile = jnp.where(lanes == first + rows, value, tile)
    return jnp.sum(tile, axis=0, keepdims=True)


def to_tile(z, row):
    shape = (z.columns, LANES)
    rows = lax.broadcasted_iota(jnp.int32, shape, 0)
    tile = jnp.where(lane_ids(shape) == rows, jnp.broadcast_to(row, shape), 0.0)
    return jnp.broadcast_to(lane_sum(tile), shape)


def scalars(z, gathered):
    zero = jnp.zeros((1, LANES), F32)
    count = gathered.shape[0]
    unroll = 32 if count % 32 == 0 else 1
    total = lax.fori_loop(0, count, lambda k, acc: acc + gathered[k], zero, unroll=unroll)

    def group(row, at):
        return pltpu.roll(row, LANES - at * z.columns, 1) if at else row

    norm = group(total, RR)
    alpha = norm / group(total, DP)
    placed = pltpu.roll(alpha, PP * z.columns, 1)

    def squares(k, acc):
        row = gathered[k]
        step = placed * pltpu.roll(row, LANES // 2, 1)
        return acc + row * step * step

    moved = lax.fori_loop(0, count, squares, zero, unroll=unroll)
    following = norm - 2.0 * alpha * group(total, RP) + group(moved, PP)
    return to_tile(z, alpha), to_tile(z, following / norm)


def across_block(z, tile):
    return jnp.concatenate([tile] * z.halves, axis=1)


def couple(z, i, table, wide, diag, off, parts):
    source = table[z.inverse + i]
    mine = parts[i]
    coupled = dot(mine, diag[i], NT) + dot(mine, diag[i], NN)
    coupled = coupled + dot(parts[table[z.pattern + i]], off[i], NT)
    coupled = coupled + dot(parts[source], off[source], NN)
    return wide[i] * fold(coupled + mine.astype(F32))


def first_half(z, step, table, *rest):
    rest = list(rest)
    take = lambda n: [rest.pop(0) for _ in range(n)]
    wide, diag, off, corners = take(4)
    if step == 0:
        *far, beside, loaded = take(2 + len(z.far))
        residual, image, parts, extra, near_out, other = rest
        direction = residual
        place(z, table, [beside, *far], 0, 2, other)
    else:
        gathered, before, way, product = take(4)
        residual, direction, step_out, image, parts, extra, near_out = rest
        alpha, beta = scalars(z, gathered)
        step_out[...] = alpha
        alpha, beta = across_block(z, alpha), across_block(z, beta)
    partial = jnp.zeros((2 * z.columns, 2 * z.corners), F32)
    for i in range(z.blocks):
        if step == 0:
            value = loaded[i] - other[i]
            residual[i] = value
        else:
            value = before[i] - alpha * product[i]
            residual[i] = value
            value = value + beta * way[i]
            direction[i] = value
        mine = pad(wide[i] * value)
        parts[i] = mine
        partial = partial + dot(mine, corners[i], NT)
    refs = (table, wide, diag, off, parts)
    for position in range(z.early):
        i = table[z.order + position]
        image[i] = couple(z, i, *refs)

    @pl.when(table[z.count] > z.early)
    def _():
        for position in range(z.early, z.middle):
            i = table[z.order + position]
            image[i] = couple(z, i, *refs)

    fill_near(z, table, [image], near_out)
    sums = fold(partial)
    padded = jnp.concatenate(
        [sums, jnp.zeros((z.columns, z.extra - sums.shape[1]), F32)], axis=1
    )
    tile = pltpu.roll(padded, lax.axis_index("sub") * z.corners, 1)
    extra[...] = tile
    store_extra(z, tile, near_out, z.near_rows(1))


def second_half(z, step, table, wide, diag, off, parts, image_in, *rest):
    if step == 0:
        (image,) = rest
    elif step == 1:
        alpha, way, image, multipliers = rest
    else:
        alpha, way, before, image, multipliers = rest
    refs = (table, wide, diag, off, parts)
    for i in range(z.blocks):
        image[i] = image_in[i]

    @pl.when(table[z.count] <= z.early)
    def _():
        for position in range(z.early, z.middle):
            i = table[z.order + position]
            image[i] = couple(z, i, *refs)

    for position in range(z.middle, z.blocks):
        i = table[z.order + position]
        image[i] = couple(z, i, *refs)
    if step > 0:
        size = across_block(z, alpha[...])
        for i in range(z.blocks):
            value = size * way[i]
            multipliers[i] = value if step == 1 else before[i] + value


def finish_product(z, table, operator, image, own_extra, jump_lift, residual, direction, near, *rest):
    *far, beside, product, sent, other = rest
    place(z, table, [beside, *far], 0, 1, other)
    partials = extra_sum(z, own_extra, near, *far)[:, : z.all_corners]
    local = dot_high(partials, operator[...], NT)
    rows = pad(jnp.concatenate([local, local], axis=1))
    zero = jnp.zeros((z.columns, z.width), F32)
    sums = [zero] * 3
    top = zero
    for i in range(z.blocks):
        value = image[i] - other[i] + fold(dot(rows, jump_lift[i], NN))
        product[i] = value
        top = jnp.maximum(top, jnp.abs(value))
        r, d = residual[i], direction[i]
        sums = [s + a * b for s, (a, b) in zip(sums, [(r, r), (d, value), (r, value)])]
    top = jnp.max(top, axis=1, keepdims=True)
    shrink = jnp.where(top > 0.0, 1.0 / top, 0.0)
    squares = zero
    for i in range(z.blocks):
        value = product[i] * shrink
        squares = squares + value * value
    values = [(k * z.columns, lane_sum(v)) for k, v in enumerate(sums + [squares])]
    sent[...] = to_row(z, values + [(PP * z.columns + LANES // 2, top)])


def finish(z, gathered, before, residual_in, direction, product, multipliers, residual):
    alpha, _ = scalars(z, gathered)
    for i in range(z.blocks):
        for h in range(z.halves):
            part = slice(h * LANES, (h + 1) * LANES)
            multipliers[:, i, part] = before[i, :, part] + alpha * direction[i, :, part]
            residual[:, i, part] = residual_in[i, :, part] - alpha * product[i, :, part]


def call(body, outs, scratch, cost, args, table=True, away=()):
    args = [
        pltpu.with_memory_space_constraint(a, pltpu.HBM) if k in away else a
        for k, a in enumerate(args)
    ]
    specs = [HBM if k in away else VMEM for k in range(len(args))]
    if table:
        specs[0] = SMEM
    shapes = [
        pltpu.SMEM(s, t) if t == jnp.int32 else jax.ShapeDtypeStruct(s, t) for s, t in outs
    ]
    return pl.pallas_call(
        body,
        out_shape=shapes,
        in_specs=specs,
        out_specs=[SMEM if t == jnp.int32 else VMEM for _, t in outs],
        scratch_shapes=scratch,
        compiler_params=pltpu.CompilerParams(vmem_limit_bytes=LIMIT),
        cost_estimate=pl.CostEstimate(flops=cost, bytes_accessed=cost // 16, transcendentals=0),
    )(*args)


def on_device(
    load,
    row_scale,
    diag_blocks,
    off_blocks,
    off_pattern,
    partner,
    corner_coupling,
    corner_index,
    coarse_inverse,
    *,
    mesh,
):
    z = Sizes(load, corner_coupling, coarse_inverse, mesh)
    cols, blocks, width = z.columns, z.blocks, z.width
    field = ((blocks, cols, width), F32)
    other = pltpu.VMEM((blocks + 1, cols, width), F32)
    extra = ((cols, z.extra), F32)
    light, heavy = 4_000_000, 600_000_000

    def shape(rows, kinds):
        return ((rows + (z.extra_chunks if kinds == 1 else 0), cols, LANES), F32)

    def kernel(body, *extra_args):
        return functools.partial(body, z, *extra_args)

    def across(piece, mask_of):
        pairs = [(t, t ^ mask_of(t & 1)) for t in range(z.peers)]
        return lax.ppermute(piece, "sub", pairs)

    def to_near(piece):
        return across(piece, lambda core: 1)

    def exchange(kinds, sources, near):
        *pieces, beside = call(
            kernel(relay, kinds),
            [shape(2 * z.rows(kinds), kinds)] * (len(z.far) + 1), [], light, [table, *sources, near],
        )
        far = [across(piece, lambda core: z.far[z.at(k, core)]) for k, piece in enumerate(pieces)]
        return [*far, to_near(beside)]

    table, loaded, lift, wide, corners, near = call(
        kernel(begin),
        [((z.table,), jnp.int32), field, field, field, ((blocks, 2 * z.corners, width), BF16)]
        + [shape(z.near_rows(2), 2)],
        [
            pltpu.VMEM(load.shape, F32),
            pltpu.VMEM(row_scale.shape, F32),
            pltpu.VMEM(corner_coupling.shape, BF16),
            pltpu.SMEM(partner.shape, jnp.int32),
            pltpu.SMEM(off_pattern.shape, jnp.int32),
            pltpu.SMEM((z.peers,), jnp.int32),
            pltpu.SemaphoreType.DMA((5,)),
        ],
        light,
        [partner, off_pattern, load, row_scale, corner_coupling],
        False, range(5),
    )
    arrived = exchange(2, [loaded, lift], to_near(near))
    weight = (diag_blocks.shape, BF16)
    operator, diag, off = call(
        kernel(prepare), [((z.all_corners, z.all_corners), F32), weight, weight],
        [
            pltpu.VMEM(corner_index.shape, jnp.int32),
            pltpu.VMEM(coarse_inverse.shape, F32),
            pltpu.SemaphoreType.DMA((4,)),
        ],
        heavy, [corner_index, coarse_inverse, diag_blocks, off_blocks], False, range(4),
    )
    half = ((blocks, 2 * cols, width), BF16)
    tile = ((cols, LANES), F32)
    fixed = [wide, diag, off, corners]
    multipliers = None
    for step in range(ITERS):
        early = [field, half, extra, shape(z.near_rows(1), 1)]
        if step == 0:
            residual, part, parts, own_extra, near = call(
                kernel(first_half, step), [field] + early, [other], heavy,
                [table, *fixed, *arrived, loaded],
            )
            direction = residual
            older = []
        else:
            way = direction
            residual, direction, alpha, part, parts, own_extra, near = call(
                kernel(first_half, step), [field, field, tile] + early, [], heavy,
                [table, *fixed, gathered, residual, way, product],
            )
            older = [alpha, way] + [multipliers] * (step > 1)
        near = to_near(near)
        image, *more = call(
            kernel(second_half, step), [field] + [field] * (step > 0), [], heavy,
            [table, wide, diag, off, parts, part, *older],
        )
        if more:
            (multipliers,) = more
        if step == 0:
            (jump_lift,) = call(
                kernel(build_lift), [((blocks, 2 * z.all_corners, width), BF16)],
                [other, pltpu.VMEM((blocks, z.all_corners, width), F32)], heavy,
                [table, lift, *arrived],
            )
        arrived = exchange(1, [image, own_extra], near)
        product, sent = call(
            kernel(finish_product), [field, ((1, LANES), F32)], [other], heavy,
            [table, operator, image, own_extra, jump_lift, residual, direction, near, *arrived],
        )
        gathered = lax.all_gather(sent, ("group", "sub"))
    multipliers, residual = call(
        kernel(finish), [(load.shape, F32)] * 2, [], light,
        [gathered, multipliers, residual, direction, product], False,
    )
    return multipliers, residual


def solution(mesh):
    return jax.shard_map(
        functools.partial(on_device, mesh=dict(mesh.shape)),
        mesh=mesh,
        in_specs=(
            P(None, ("group", "sub"), None),
            P(("group", "sub"), None),
            P(("group", "sub"), None, None),
            P(("group", "sub"), None, None),
            P(("group", "sub"), None),
            P(("group", "sub"), None),
            P(("group", "sub"), None),
            P("group", None),
            P("group", None),
        ),
        out_specs=(P(None, ("group", "sub"), None), P(None, ("group", "sub"), None)),
        check_vma=False,
    )
```

```python
import functools

import jax
import jax.numpy as jnp
from jax import lax
from jax.experimental import pallas as pl
from jax.experimental.pallas import tpu as pltpu
from jax.sharding import PartitionSpec as P

ITERS = 4
HIGH = lax.Precision.HIGHEST
F32 = jnp.float32
BF16 = jnp.bfloat16
VMEM = pl.BlockSpec(memory_space=pltpu.VMEM)
SMEM = pl.BlockSpec(memory_space=pltpu.SMEM)
HBM = pl.BlockSpec(memory_space=pltpu.HBM)
LIMIT = 24 * 1024 * 1024
LANES = 128
RR, DP, RP, PP = range(4)
NN = (((1,), (0,)), ((), ()))
NT = (((1,), (1,)), ((), ()))
TN = (((0,), (0,)), ((), ()))


def dot(a, b, dims):
    return lax.dot_general(a, b, dims, preferred_element_type=F32)


def dot_high(a, b, dims):
    return lax.dot_general(a, b, dims, precision=HIGH, preferred_element_type=F32)


def pad(a):
    return jnp.concatenate([a, jnp.zeros_like(a)], axis=0).astype(BF16)


def split(a):
    high = a.astype(BF16).astype(F32)
    return jnp.concatenate([high, a - high], axis=0).astype(BF16)


def fold(a):
    half = a.shape[0] // 2
    return a[:half] + a[half:]


def lane_ids(shape):
    return lax.broadcasted_iota(jnp.int32, shape, 1)


class Sizes:
    def __init__(self, load, corner_coupling, coarse_inverse, mesh):
        self.columns = load.shape[0]
        self.blocks = load.shape[1]
        self.width = load.shape[2]
        self.corners = corner_coupling.shape[0]
        assert self.corners == self.columns
        self.coarse = coarse_inverse.shape[1]
        self.peers = mesh["sub"]
        self.groups = mesh["group"]
        self.capacity = (self.blocks + self.peers - 2) // (self.peers - 1)
        self.all_corners = self.peers * self.corners
        self.extra_chunks = -(-self.all_corners // LANES)
        self.extra = self.extra_chunks * LANES
        self.halves = self.width // LANES
        evens = range(2, self.peers, 2)
        self.beyond = [m for m in evens if m & (m - 1)]
        self.beside = [m for m in evens if m & (m - 1) == 0]
        self.far = self.beyond + self.beside
        self.handed = [m + 1 for m in self.far]
        self.slots = self.peers * self.capacity
        self.inverse = self.slots
        self.pattern = self.inverse + self.blocks
        self.partner = self.pattern + self.blocks
        self.order = self.partner + self.blocks
        self.count = self.order + self.blocks + 1
        self.table = self.count + 1
        most = len(self.far) * self.capacity
        self.early = min(-(-most * 7 // 8), self.blocks)
        self.middle = max(self.early, min(most, self.blocks))

    def rows(self, kinds):
        return kinds * self.capacity * self.halves

    def near_rows(self, kinds):
        return len(self.handed) * self.rows(kinds)

    def at(self, k, core):
        first = len(self.beyond)
        return k if k < first else first + (k - first + core) % len(self.beside)

    def mine(self, k):
        core = lax.axis_index("sub") & 1
        at = [self.at(k, c) for c in range(2)]
        return tuple(
            jnp.where(core == 0, jnp.int32(a), jnp.int32(b))
            for a, b in [at, [self.far[n] for n in at]]
        )

    def sources(self):
        found = [(1, 0, 0)]
        for k in range(len(self.far)):
            _, m = self.mine(k)
            found += [(m + side, 1 + k, side) for side in range(2)]
        return found


def fill_table(z, partner, pattern, table, counts):
    me = lax.axis_index("sub")
    for entry in range(z.slots):
        table[entry] = z.blocks
    for m in range(z.peers):
        counts[m] = 0
    for i in range(z.blocks):
        mate = partner[0, i]
        source = pattern[0, i]
        m = mate ^ me
        rank = counts[m]
        table[m * z.capacity + rank] = i
        counts[m] = rank + 1
        table[z.inverse + source] = i
        table[z.pattern + i] = source
        table[z.partner + i] = mate
    place = jnp.int32(0)
    for m in z.handed + z.far + [1]:
        for r in range(z.capacity):
            block = table[m * z.capacity + r]
            table[z.order + place] = block
            place = place + (block < z.blocks).astype(jnp.int32)
        if m == z.handed[-1]:
            table[z.count] = place


def fill_piece(z, table, sources, m, piece, row):
    for source in sources:
        for r in range(z.capacity):
            value = source[jnp.minimum(table[m * z.capacity + r], z.blocks - 1)]
            for h in range(z.halves):
                piece[row] = value[:, h * LANES : (h + 1) * LANES]
                row += 1


def fill_near(z, table, sources, near):
    for k, m in enumerate(z.handed):
        fill_piece(z, table, sources, m, near, k * z.rows(len(sources)))


def store_extra(z, tile, piece, row):
    for j in range(z.extra_chunks):
        piece[row + j] = tile[:, j * LANES : (j + 1) * LANES]


def load_extra(z, piece, row):
    return jnp.concatenate([piece[row + j] for j in range(z.extra_chunks)], axis=1)


def relay(z, kinds, table, *rest):
    sources, rest = rest[:kinds], rest[kinds:]
    if kinds == 1:
        extra, rest = rest[0], rest[1:]
    near, pieces, beside = rest[0], rest[1:-1], rest[-1]
    rows = z.rows(kinds)
    fill_piece(z, table, sources, 1, beside, 0)
    if kinds == 1:
        tile = extra[...] + load_extra(z, near, z.near_rows(1))
    for k, piece in enumerate(pieces):
        which, m = z.mine(k)
        fill_piece(z, table, sources, m, piece, 0)
        for row in range(rows):
            piece[rows + row] = near[which * rows + row]
        if kinds == 1:
            store_extra(z, tile, piece, 2 * rows)


def place(z, table, arrived, kind, kinds, target):
    for m, transfer, piece in z.sources():
        row = piece * z.rows(kinds) + z.rows(kind)
        for r in range(z.capacity):
            block = table[m * z.capacity + r]
            for h in range(z.halves):
                target[block, :, h * LANES : (h + 1) * LANES] = arrived[transfer][row]
                row += 1


def begin(z, partner, pattern, load, scale, coupling, table, field, lift, wide, corners, near, *scratch):
    here, scale_here, coupling_here, partner_here, pattern_here, counts, sems = scratch
    copies = [
        pltpu.make_async_copy(a, b, sems.at[k])
        for k, (a, b) in enumerate(
            [
                (partner, partner_here),
                (pattern, pattern_here),
                (load, here),
                (scale, scale_here),
                (coupling, coupling_here),
            ]
        )
    ]
    for copy in copies:
        copy.start()
    copies[0].wait()
    copies[1].wait()
    fill_table(z, partner_here, pattern_here, table, counts)
    for copy in copies[2:]:
        copy.wait()
    for i in range(z.blocks):
        field[i] = here[:, i, :]
        row = jnp.broadcast_to(scale_here[i : i + 1, :], (z.columns, z.width))
        wide[i] = row
        part = coupling_here[:, i * z.width : (i + 1) * z.width].astype(F32)
        lift[i] = row * part
        corners[i] = jnp.concatenate([part, jnp.zeros_like(part)], axis=0).astype(BF16)
    fill_near(z, table, [field, lift], near)


def split3(a):
    high = a.astype(BF16).astype(F32)
    middle = (a - high).astype(BF16).astype(F32)
    return [high, middle, a - high - middle]


def prepare(z, index_in, inverse_in, diag, off, operator, diag_out, off_out, index, inverse, sems):
    copies = [
        pltpu.make_async_copy(a, b, sems.at[k])
        for k, (a, b) in enumerate(
            [(index_in, index), (inverse_in, inverse), (diag, diag_out), (off, off_out)]
        )
    ]
    for copy in copies:
        copy.start()
    copies[0].wait()
    copies[1].wait()
    rows = lax.broadcasted_iota(jnp.int32, (z.coarse, z.all_corners), 0)
    select = (rows == index[...]).astype(BF16)
    parts = jnp.concatenate(split3(inverse[...]), axis=0).astype(BF16)
    half = dot(parts, select, NN)
    half = sum(half[k * z.coarse : (k + 1) * z.coarse] for k in range(3))
    parts = jnp.concatenate(split3(half), axis=1).astype(BF16)
    full = dot(select, parts, TN)
    operator[...] = sum(full[:, k * z.all_corners : (k + 1) * z.all_corners] for k in range(3))
    copies[2].wait()
    copies[3].wait()


def build_lift(z, table, lift, *rest):
    count = 1 + len(z.far)
    arrived, (jump_lift, other, full) = rest[:count], rest[count:]
    place(z, table, [arrived[-1], *arrived[:-1]], 1, 2, other)
    me = lax.axis_index("sub")
    for i in range(z.blocks):
        full[i] = jnp.zeros((z.all_corners, z.width), F32)
        own = pl.multiple_of(me * z.corners, z.corners)
        theirs = pl.multiple_of(table[z.partner + i] * z.corners, z.corners)
        full[i, pl.ds(own, z.corners), :] = lift[i]
        full[i, pl.ds(theirs, z.corners), :] = -other[i]
        jump_lift[i] = split(full[i])


def extra_sum(z, own, near, *far):
    total = own[...] + load_extra(z, near, z.near_rows(1))
    for piece in far:
        total = total + load_extra(z, piece, 2 * z.rows(1))
    return total


def lane_sum(a):
    return jnp.sum(a, axis=1, keepdims=True)


def to_row(z, values):
    shape = (z.columns, LANES)
    lanes = lane_ids(shape)
    rows = lax.broadcasted_iota(jnp.int32, shape, 0)
    tile = jnp.zeros(shape, F32)
    for first, value in values:
        tile = jnp.where(lanes == first + rows, value, tile)
    return jnp.sum(tile, axis=0, keepdims=True)


def to_tile(z, row, first):
    shape = (z.columns, LANES)
    rows = lax.broadcasted_iota(jnp.int32, shape, 0)
    tile = jnp.where(lane_ids(shape) == first + rows, jnp.broadcast_to(row, shape), 0.0)
    return jnp.broadcast_to(lane_sum(tile), shape)


def scalars(z, gathered, previous):
    zero = jnp.zeros((1, LANES), F32)
    count = gathered.shape[0]
    unroll = 32 if count % 32 == 0 else 1
    total = lax.fori_loop(0, count, lambda k, acc: acc + gathered[k], zero, unroll=unroll)
    norm, way, rest = [to_tile(z, total, k * z.columns) for k in (RR, DP, RP)]
    alpha = norm / way
    if previous is None:
        placed = to_row(z, [(PP * z.columns, alpha)])

        def squares(k, acc):
            row = gathered[k]
            step = placed * pltpu.roll(row, LANES // 2, 1)
            return acc + row * step * step

        moved = lax.fori_loop(0, count, squares, zero, unroll=unroll)
        moved = to_tile(z, moved, PP * z.columns)
    else:
        ratio = alpha / used_step(previous)
        moved = to_tile(z, total, PP * z.columns) * ratio * ratio
    return alpha, (norm - 2.0 * alpha * rest + moved) / norm


def used_step(previous):
    return jnp.where(previous == 0.0, 1.0, previous)


def across_block(z, tile):
    return jnp.concatenate([tile] * z.halves, axis=1)


def couple(z, i, table, wide, diag, off, parts):
    source = table[z.inverse + i]
    mine = parts[i]
    coupled = dot(mine, diag[i], NT) + dot(mine, diag[i], NN)
    coupled = coupled + dot(parts[table[z.pattern + i]], off[i], NT)
    coupled = coupled + dot(parts[source], off[source], NN)
    return wide[i] * fold(coupled + mine.astype(F32))


def first_half(z, step, table, *rest):
    rest = list(rest)
    take = lambda n: [rest.pop(0) for _ in range(n)]
    wide, diag, off, corners = take(4)
    if step == 0:
        *far, beside, loaded = take(2 + len(z.far))
        residual, image, parts, extra, near_out, other = rest
        direction = residual
        place(z, table, [beside, *far], 0, 2, other)
    else:
        gathered, before, way, product = take(4)
        previous = take(1)[0][...] if step > 1 else None
        residual, direction, step_out, image, parts, extra, near_out = rest
        alpha, beta = scalars(z, gathered, previous)
        step_out[...] = alpha
        alpha, beta = across_block(z, alpha), across_block(z, beta)
    partial = jnp.zeros((2 * z.columns, 2 * z.corners), F32)
    for i in range(z.blocks):
        if step == 0:
            value = loaded[i] - other[i]
            residual[i] = value
        else:
            value = before[i] - alpha * product[i]
            residual[i] = value
            value = value + beta * way[i]
            direction[i] = value
        mine = pad(wide[i] * value)
        parts[i] = mine
        partial = partial + dot(mine, corners[i], NT)
    refs = (table, wide, diag, off, parts)
    for position in range(z.early):
        i = table[z.order + position]
        image[i] = couple(z, i, *refs)

    @pl.when(table[z.count] > z.early)
    def _():
        for position in range(z.early, z.middle):
            i = table[z.order + position]
            image[i] = couple(z, i, *refs)

    fill_near(z, table, [image], near_out)
    sums = fold(partial)
    padded = jnp.concatenate(
        [sums, jnp.zeros((z.columns, z.extra - sums.shape[1]), F32)], axis=1
    )
    tile = pltpu.roll(padded, lax.axis_index("sub") * z.corners, 1)
    extra[...] = tile
    store_extra(z, tile, near_out, z.near_rows(1))


def second_half(z, step, table, wide, diag, off, parts, image_in, *rest):
    if step == 0:
        (image,) = rest
    elif step == 1:
        alpha, way, image, multipliers = rest
    else:
        alpha, way, before, image, multipliers = rest
    refs = (table, wide, diag, off, parts)
    for i in range(z.blocks):
        image[i] = image_in[i]

    @pl.when(table[z.count] <= z.early)
    def _():
        for position in range(z.early, z.middle):
            i = table[z.order + position]
            image[i] = couple(z, i, *refs)

    for position in range(z.middle, z.blocks):
        i = table[z.order + position]
        image[i] = couple(z, i, *refs)
    if step > 0:
        size = across_block(z, alpha[...])
        for i in range(z.blocks):
            value = size * way[i]
            multipliers[i] = value if step == 1 else before[i] + value


def finish_product(z, step, table, operator, image, own_extra, jump_lift, residual, direction, near, *rest):
    *far, beside, product, sent, other = rest
    if step > 0:
        previous, far = far[0], far[1:]
        scale = across_block(z, used_step(previous[...]))
    place(z, table, [beside, *far], 0, 1, other)
    partials = extra_sum(z, own_extra, near, *far)[:, : z.all_corners]
    local = dot_high(partials, operator[...], NT)
    rows = pad(jnp.concatenate([local, local], axis=1))
    zero = jnp.zeros((z.columns, z.width), F32)
    sums = [zero] * (4 if step > 0 else 3)
    top = zero
    for i in range(z.blocks):
        value = image[i] - other[i] + fold(dot(rows, jump_lift[i], NN))
        product[i] = value
        r, d = residual[i], direction[i]
        pairs = [(r, r), (d, value), (r, value)]
        if step > 0:
            scaled = scale * value
            pairs.append((scaled, scaled))
        else:
            top = jnp.maximum(top, jnp.abs(value))
        sums = [s + a * b for s, (a, b) in zip(sums, pairs)]
    more = []
    if step == 0:
        top = jnp.max(top, axis=1, keepdims=True)
        shrink = jnp.where(top > 0.0, 1.0 / top, 0.0)
        squares = zero
        for i in range(z.blocks):
            value = product[i] * shrink
            squares = squares + value * value
        sums.append(squares)
        more.append((PP * z.columns + LANES // 2, top))
    row = to_row(z, [(k * z.columns, lane_sum(v)) for k, v in enumerate(sums)] + more)
    for k in range(sent.shape[0]):
        sent[k] = row


def finish(z, gathered, before, residual_in, direction, product, previous, multipliers, residual):
    alpha, _ = scalars(z, gathered, previous[...])
    for i in range(z.blocks):
        for h in range(z.halves):
            part = slice(h * LANES, (h + 1) * LANES)
            multipliers[:, i, part] = before[i, :, part] + alpha * direction[i, :, part]
            residual[:, i, part] = residual_in[i, :, part] - alpha * product[i, :, part]


def call(body, outs, scratch, cost, args, table=True, away=()):
    args = [
        pltpu.with_memory_space_constraint(a, pltpu.HBM) if k in away else a
        for k, a in enumerate(args)
    ]
    specs = [HBM if k in away else VMEM for k in range(len(args))]
    if table:
        specs[0] = SMEM
    shapes = [
        pltpu.SMEM(s, t) if t == jnp.int32 else jax.ShapeDtypeStruct(s, t) for s, t in outs
    ]
    return pl.pallas_call(
        body,
        out_shape=shapes,
        in_specs=specs,
        out_specs=[SMEM if t == jnp.int32 else VMEM for _, t in outs],
        scratch_shapes=scratch,
        compiler_params=pltpu.CompilerParams(vmem_limit_bytes=LIMIT),
        cost_estimate=pl.CostEstimate(flops=cost, bytes_accessed=cost // 16, transcendentals=0),
    )(*args)


def on_device(
    load,
    row_scale,
    diag_blocks,
    off_blocks,
    off_pattern,
    partner,
    corner_coupling,
    corner_index,
    coarse_inverse,
    *,
    mesh,
):
    z = Sizes(load, corner_coupling, coarse_inverse, mesh)
    cols, blocks, width = z.columns, z.blocks, z.width
    field = ((blocks, cols, width), F32)
    other = pltpu.VMEM((blocks + 1, cols, width), F32)
    extra = ((cols, z.extra), F32)
    light, heavy = 4_000_000, 600_000_000

    def shape(rows, kinds):
        return ((rows + (z.extra_chunks if kinds == 1 else 0), cols, LANES), F32)

    def kernel(body, *extra_args):
        return functools.partial(body, z, *extra_args)

    def across(piece, mask_of):
        pairs = [(t, t ^ mask_of(t & 1)) for t in range(z.peers)]
        return lax.ppermute(piece, "sub", pairs)

    def to_near(piece):
        return across(piece, lambda core: 1)

    def exchange(kinds, sources, near):
        *pieces, beside = call(
            kernel(relay, kinds),
            [shape(2 * z.rows(kinds), kinds)] * (len(z.far) + 1), [], light, [table, *sources, near],
        )
        far = [across(piece, lambda core: z.far[z.at(k, core)]) for k, piece in enumerate(pieces)]
        return [*far, to_near(beside)]

    table, loaded, lift, wide, corners, near = call(
        kernel(begin),
        [((z.table,), jnp.int32), field, field, field, ((blocks, 2 * z.corners, width), BF16)]
        + [shape(z.near_rows(2), 2)],
        [
            pltpu.VMEM(load.shape, F32),
            pltpu.VMEM(row_scale.shape, F32),
            pltpu.VMEM(corner_coupling.shape, BF16),
            pltpu.SMEM(partner.shape, jnp.int32),
            pltpu.SMEM(off_pattern.shape, jnp.int32),
            pltpu.SMEM((z.peers,), jnp.int32),
            pltpu.SemaphoreType.DMA((5,)),
        ],
        light,
        [partner, off_pattern, load, row_scale, corner_coupling],
        False, range(5),
    )
    arrived = exchange(2, [loaded, lift], to_near(near))
    weight = (diag_blocks.shape, BF16)
    operator, diag, off = call(
        kernel(prepare), [((z.all_corners, z.all_corners), F32), weight, weight],
        [
            pltpu.VMEM(corner_index.shape, jnp.int32),
            pltpu.VMEM(coarse_inverse.shape, F32),
            pltpu.SemaphoreType.DMA((4,)),
        ],
        heavy, [corner_index, coarse_inverse, diag_blocks, off_blocks], False, range(4),
    )
    half = ((blocks, 2 * cols, width), BF16)
    tile = ((cols, LANES), F32)
    devices = z.groups * z.peers
    fixed = [wide, diag, off, corners]
    multipliers = alpha = None
    for step in range(ITERS):
        early = [field, half, extra, shape(z.near_rows(1), 1)]
        if step == 0:
            residual, part, parts, own_extra, near = call(
                kernel(first_half, step), [field] + early, [other], heavy,
                [table, *fixed, *arrived, loaded],
            )
            direction = residual
            older = []
        else:
            way = direction
            residual, direction, alpha, part, parts, own_extra, near = call(
                kernel(first_half, step), [field, field, tile] + early, [], heavy,
                [table, *fixed, gathered, residual, way, product] + [alpha] * (step > 1),
            )
            older = [alpha, way] + [multipliers] * (step > 1)
        near = to_near(near)
        image, *more = call(
            kernel(second_half, step), [field] + [field] * (step > 0), [], heavy,
            [table, wide, diag, off, parts, part, *older],
        )
        if more:
            (multipliers,) = more
        if step == 0:
            (jump_lift,) = call(
                kernel(build_lift), [((blocks, 2 * z.all_corners, width), BF16)],
                [other, pltpu.VMEM((blocks, z.all_corners, width), F32)], heavy,
                [table, lift, *arrived],
            )
        arrived = exchange(1, [image, own_extra], near)
        product, sent = call(
            kernel(finish_product, step), [field, ((devices, 1, LANES), F32)], [other], heavy,
            [table, operator, image, own_extra, jump_lift, residual, direction, near]
            + [alpha] * (step > 0) + arrived,
        )
        gathered = lax.all_to_all(sent, ("group", "sub"), 0, 0, tiled=True)
    multipliers, residual = call(
        kernel(finish), [(load.shape, F32)] * 2, [], light,
        [gathered, multipliers, residual, direction, product, alpha], False,
    )
    return multipliers, residual


def solution(mesh):
    return jax.shard_map(
        functools.partial(on_device, mesh=dict(mesh.shape)),
        mesh=mesh,
        in_specs=(
            P(None, ("group", "sub"), None),
            P(("group", "sub"), None),
            P(("group", "sub"), None, None),
            P(("group", "sub"), None, None),
            P(("group", "sub"), None),
            P(("group", "sub"), None),
            P(("group", "sub"), None),
            P("group", None),
            P("group", None),
        ),
        out_specs=(P(None, ("group", "sub"), None), P(None, ("group", "sub"), None)),
        check_vma=False,
    )
```

```python
import functools

import jax
import jax.numpy as jnp
from jax import lax
from jax.experimental import pallas as pl
from jax.experimental.pallas import tpu as pltpu
from jax.sharding import PartitionSpec as P

ITERS = 4
HIGH = lax.Precision.HIGHEST
F32 = jnp.float32
BF16 = jnp.bfloat16
VMEM = pl.BlockSpec(memory_space=pltpu.VMEM)
SMEM = pl.BlockSpec(memory_space=pltpu.SMEM)
HBM = pl.BlockSpec(memory_space=pltpu.HBM)
LIMIT = 24 * 1024 * 1024
LANES = 128
RR, DP, RP, PP = range(4)
NN = (((1,), (0,)), ((), ()))
NT = (((1,), (1,)), ((), ()))
TN = (((0,), (0,)), ((), ()))


def dot(a, b, dims):
    return lax.dot_general(a, b, dims, preferred_element_type=F32)


def dot_high(a, b, dims):
    return lax.dot_general(a, b, dims, precision=HIGH, preferred_element_type=F32)


def pad(a):
    return jnp.concatenate([a, jnp.zeros_like(a)], axis=0).astype(BF16)


def split(a):
    high = a.astype(BF16).astype(F32)
    return jnp.concatenate([high, a - high], axis=0).astype(BF16)


def fold(a):
    half = a.shape[0] // 2
    return a[:half] + a[half:]


def lane_ids(shape):
    return lax.broadcasted_iota(jnp.int32, shape, 1)


class Sizes:
    def __init__(self, load, corner_coupling, coarse_inverse, mesh):
        self.columns = load.shape[0]
        self.blocks = load.shape[1]
        self.width = load.shape[2]
        self.corners = corner_coupling.shape[0]
        assert self.corners == self.columns
        self.coarse = coarse_inverse.shape[1]
        self.peers = mesh["sub"]
        self.groups = mesh["group"]
        self.capacity = (self.blocks + self.peers - 2) // (self.peers - 1)
        self.all_corners = self.peers * self.corners
        self.extra_chunks = -(-self.all_corners // LANES)
        self.extra = self.extra_chunks * LANES
        self.halves = self.width // LANES
        evens = range(2, self.peers, 2)
        self.beyond = [m for m in evens if m & (m - 1)]
        self.beside = [m for m in evens if m & (m - 1) == 0]
        self.far = self.beyond + self.beside
        self.handed = [m + 1 for m in self.far]
        self.slots = self.peers * self.capacity
        self.inverse = self.slots
        self.pattern = self.inverse + self.blocks
        self.partner = self.pattern + self.blocks
        self.order = self.partner + self.blocks
        self.count = self.order + self.blocks + 1
        self.table = self.count + 1
        most = len(self.far) * self.capacity
        self.early = min(-(-most * 7 // 8), self.blocks)
        self.middle = max(self.early, min(most, self.blocks))

    def rows(self, kinds):
        return kinds * self.capacity * self.halves

    def near_rows(self, kinds):
        return len(self.handed) * self.rows(kinds)

    def at(self, k, core):
        return (k + core) % len(self.far)

    def mine(self, k):
        core = lax.axis_index("sub") & 1
        at = [self.at(k, c) for c in range(2)]
        return tuple(
            jnp.where(core == 0, jnp.int32(a), jnp.int32(b))
            for a, b in [at, [self.far[n] for n in at]]
        )

    def sources(self):
        found = [(1, 0, 0)]
        for k in range(len(self.far)):
            _, m = self.mine(k)
            found += [(m + side, 1 + k, side) for side in range(2)]
        return found


def fill_table(z, partner, pattern, table, counts):
    me = lax.axis_index("sub")
    for entry in range(z.slots):
        table[entry] = z.blocks
    for m in range(z.peers):
        counts[m] = 0
    for i in range(z.blocks):
        mate = partner[0, i]
        source = pattern[0, i]
        m = mate ^ me
        rank = counts[m]
        table[m * z.capacity + rank] = i
        counts[m] = rank + 1
        table[z.inverse + source] = i
        table[z.pattern + i] = source
        table[z.partner + i] = mate
    place = jnp.int32(0)
    for m in z.handed + z.far + [1]:
        for r in range(z.capacity):
            block = table[m * z.capacity + r]
            table[z.order + place] = block
            place = place + (block < z.blocks).astype(jnp.int32)
        if m == z.handed[-1]:
            table[z.count] = place


def fill_piece(z, table, sources, m, piece, row):
    for source in sources:
        for r in range(z.capacity):
            value = source[jnp.minimum(table[m * z.capacity + r], z.blocks - 1)]
            for h in range(z.halves):
                piece[row] = value[:, h * LANES : (h + 1) * LANES]
                row += 1


def fill_near(z, table, sources, near):
    for k, m in enumerate(z.handed):
        fill_piece(z, table, sources, m, near, k * z.rows(len(sources)))


def store_extra(z, tile, piece, row):
    for j in range(z.extra_chunks):
        piece[row + j] = tile[:, j * LANES : (j + 1) * LANES]


def load_extra(z, piece, row):
    return jnp.concatenate([piece[row + j] for j in range(z.extra_chunks)], axis=1)


def relay(z, kinds, table, *rest):
    sources, rest = rest[:kinds], rest[kinds:]
    if kinds == 1:
        extra, rest = rest[0], rest[1:]
    near, pieces, beside = rest[0], rest[1:-1], rest[-1]
    rows = z.rows(kinds)
    fill_piece(z, table, sources, 1, beside, 0)
    if kinds == 1:
        tile = extra[...] + load_extra(z, near, z.near_rows(1))
    for k, piece in enumerate(pieces):
        which, m = z.mine(k)
        fill_piece(z, table, sources, m, piece, 0)
        for row in range(rows):
            piece[rows + row] = near[which * rows + row]
        if kinds == 1:
            store_extra(z, tile, piece, 2 * rows)


def place(z, table, arrived, kind, kinds, target):
    for m, transfer, piece in z.sources():
        row = piece * z.rows(kinds) + z.rows(kind)
        for r in range(z.capacity):
            block = table[m * z.capacity + r]
            for h in range(z.halves):
                target[block, :, h * LANES : (h + 1) * LANES] = arrived[transfer][row]
                row += 1


def begin(z, partner, pattern, load, scale, coupling, table, field, lift, wide, corners, near, *scratch):
    here, scale_here, coupling_here, partner_here, pattern_here, counts, sems = scratch
    copies = [
        pltpu.make_async_copy(a, b, sems.at[k])
        for k, (a, b) in enumerate(
            [
                (partner, partner_here),
                (pattern, pattern_here),
                (load, here),
                (scale, scale_here),
                (coupling, coupling_here),
            ]
        )
    ]
    for copy in copies:
        copy.start()
    copies[0].wait()
    copies[1].wait()
    fill_table(z, partner_here, pattern_here, table, counts)
    for copy in copies[2:]:
        copy.wait()
    for i in range(z.blocks):
        field[i] = here[:, i, :]
        row = jnp.broadcast_to(scale_here[i : i + 1, :], (z.columns, z.width))
        wide[i] = row
        part = coupling_here[:, i * z.width : (i + 1) * z.width].astype(F32)
        lift[i] = row * part
        corners[i] = jnp.concatenate([part, jnp.zeros_like(part)], axis=0).astype(BF16)
    fill_near(z, table, [field, lift], near)


def split3(a):
    high = a.astype(BF16).astype(F32)
    middle = (a - high).astype(BF16).astype(F32)
    return [high, middle, a - high - middle]


def prepare(z, index_in, inverse_in, diag, off, operator, diag_out, off_out, index, inverse, sems):
    copies = [
        pltpu.make_async_copy(a, b, sems.at[k])
        for k, (a, b) in enumerate(
            [(index_in, index), (inverse_in, inverse), (diag, diag_out), (off, off_out)]
        )
    ]
    for copy in copies:
        copy.start()
    copies[0].wait()
    copies[1].wait()
    rows = lax.broadcasted_iota(jnp.int32, (z.coarse, z.all_corners), 0)
    select = (rows == index[...]).astype(BF16)
    parts = jnp.concatenate(split3(inverse[...]), axis=0).astype(BF16)
    half = dot(parts, select, NN)
    half = sum(half[k * z.coarse : (k + 1) * z.coarse] for k in range(3))
    parts = jnp.concatenate(split3(half), axis=1).astype(BF16)
    full = dot(select, parts, TN)
    operator[...] = sum(full[:, k * z.all_corners : (k + 1) * z.all_corners] for k in range(3))
    copies[2].wait()
    copies[3].wait()


def build_lift(z, table, lift, *rest):
    count = 1 + len(z.far)
    arrived, (jump_lift, other, full) = rest[:count], rest[count:]
    place(z, table, [arrived[-1], *arrived[:-1]], 1, 2, other)
    me = lax.axis_index("sub")
    for i in range(z.blocks):
        full[i] = jnp.zeros((z.all_corners, z.width), F32)
        own = pl.multiple_of(me * z.corners, z.corners)
        theirs = pl.multiple_of(table[z.partner + i] * z.corners, z.corners)
        full[i, pl.ds(own, z.corners), :] = lift[i]
        full[i, pl.ds(theirs, z.corners), :] = -other[i]
        jump_lift[i] = split(full[i])


def extra_sum(z, own, near, *far):
    total = own[...] + load_extra(z, near, z.near_rows(1))
    for piece in far:
        total = total + load_extra(z, piece, 2 * z.rows(1))
    return total


def lane_sum(a):
    return jnp.sum(a, axis=1, keepdims=True)


def to_row(z, values):
    shape = (z.columns, LANES)
    lanes = lane_ids(shape)
    rows = lax.broadcasted_iota(jnp.int32, shape, 0)
    tile = jnp.zeros(shape, F32)
    for first, value in values:
        tile = jnp.where(lanes == first + rows, value, tile)
    return jnp.sum(tile, axis=0, keepdims=True)


def to_tile(z, row, first):
    shape = (z.columns, LANES)
    rows = lax.broadcasted_iota(jnp.int32, shape, 0)
    tile = jnp.where(lane_ids(shape) == first + rows, jnp.broadcast_to(row, shape), 0.0)
    return jnp.broadcast_to(lane_sum(tile), shape)


def scalars(z, gathered, previous):
    zero = jnp.zeros((1, LANES), F32)
    count = gathered.shape[0]
    unroll = 32 if count % 32 == 0 else 1
    total = lax.fori_loop(0, count, lambda k, acc: acc + gathered[k], zero, unroll=unroll)
    norm, way, rest = [to_tile(z, total, k * z.columns) for k in (RR, DP, RP)]
    alpha = norm / way
    if previous is None:
        placed = to_row(z, [(PP * z.columns, alpha)])

        def squares(k, acc):
            row = gathered[k]
            step = placed * pltpu.roll(row, LANES // 2, 1)
            return acc + row * step * step

        moved = lax.fori_loop(0, count, squares, zero, unroll=unroll)
        moved = to_tile(z, moved, PP * z.columns)
    else:
        ratio = alpha / used_step(previous)
        moved = to_tile(z, total, PP * z.columns) * ratio * ratio
    return alpha, (norm - 2.0 * alpha * rest + moved) / norm


def used_step(previous):
    return jnp.where(previous == 0.0, 1.0, previous)


def across_block(z, tile):
    return jnp.concatenate([tile] * z.halves, axis=1)


def couple(z, i, table, wide, diag, off, parts):
    source = table[z.inverse + i]
    mine = parts[i]
    coupled = dot(mine, diag[i], NT) + dot(mine, diag[i], NN)
    coupled = coupled + dot(parts[table[z.pattern + i]], off[i], NT)
    coupled = coupled + dot(parts[source], off[source], NN)
    return wide[i] * fold(coupled + mine.astype(F32))


def first_half(z, step, table, *rest):
    rest = list(rest)
    take = lambda n: [rest.pop(0) for _ in range(n)]
    wide, diag, off, corners = take(4)
    if step == 0:
        *far, beside, loaded = take(2 + len(z.far))
        residual, image, parts, extra, near_out, other = rest
        direction = residual
        place(z, table, [beside, *far], 0, 2, other)
    else:
        gathered, before, way, product = take(4)
        previous = take(1)[0][...] if step > 1 else None
        residual, direction, step_out, image, parts, extra, near_out = rest
        alpha, beta = scalars(z, gathered, previous)
        step_out[...] = alpha
        alpha, beta = across_block(z, alpha), across_block(z, beta)
    partial = jnp.zeros((2 * z.columns, 2 * z.corners), F32)
    for i in range(z.blocks):
        if step == 0:
            value = loaded[i] - other[i]
            residual[i] = value
        else:
            value = before[i] - alpha * product[i]
            residual[i] = value
            value = value + beta * way[i]
            direction[i] = value
        mine = pad(wide[i] * value)
        parts[i] = mine
        partial = partial + dot(mine, corners[i], NT)
    refs = (table, wide, diag, off, parts)
    for position in range(z.early):
        i = table[z.order + position]
        image[i] = couple(z, i, *refs)

    @pl.when(table[z.count] > z.early)
    def _():
        for position in range(z.early, z.middle):
            i = table[z.order + position]
            image[i] = couple(z, i, *refs)

    fill_near(z, table, [image], near_out)
    sums = fold(partial)
    padded = jnp.concatenate(
        [sums, jnp.zeros((z.columns, z.extra - sums.shape[1]), F32)], axis=1
    )
    tile = pltpu.roll(padded, lax.axis_index("sub") * z.corners, 1)
    extra[...] = tile
    store_extra(z, tile, near_out, z.near_rows(1))


def second_half(z, step, table, wide, diag, off, parts, image_in, *rest):
    if step == 0:
        (image,) = rest
    elif step == 1:
        alpha, way, image, multipliers = rest
    else:
        alpha, way, before, image, multipliers = rest
    refs = (table, wide, diag, off, parts)
    for i in range(z.blocks):
        image[i] = image_in[i]

    @pl.when(table[z.count] <= z.early)
    def _():
        for position in range(z.early, z.middle):
            i = table[z.order + position]
            image[i] = couple(z, i, *refs)

    for position in range(z.middle, z.blocks):
        i = table[z.order + position]
        image[i] = couple(z, i, *refs)
    if step > 0:
        size = across_block(z, alpha[...])
        for i in range(z.blocks):
            value = size * way[i]
            multipliers[i] = value if step == 1 else before[i] + value


def finish_product(z, step, table, operator, image, own_extra, jump_lift, residual, direction, near, *rest):
    *far, beside, product, sent, other = rest
    if step > 0:
        previous, far = far[0], far[1:]
        scale = across_block(z, used_step(previous[...]))
    place(z, table, [beside, *far], 0, 1, other)
    partials = extra_sum(z, own_extra, near, *far)[:, : z.all_corners]
    local = dot_high(partials, operator[...], NT)
    rows = pad(jnp.concatenate([local, local], axis=1))
    zero = jnp.zeros((z.columns, z.width), F32)
    sums = [zero] * (4 if step > 0 else 3)
    top = zero
    for i in range(z.blocks):
        value = image[i] - other[i] + fold(dot(rows, jump_lift[i], NN))
        product[i] = value
        r, d = residual[i], direction[i]
        pairs = [(r, r), (d, value), (r, value)]
        if step > 0:
            scaled = scale * value
            pairs.append((scaled, scaled))
        else:
            top = jnp.maximum(top, jnp.abs(value))
        sums = [s + a * b for s, (a, b) in zip(sums, pairs)]
    more = []
    if step == 0:
        top = jnp.max(top, axis=1, keepdims=True)
        shrink = jnp.where(top > 0.0, 1.0 / top, 0.0)
        squares = zero
        for i in range(z.blocks):
            value = product[i] * shrink
            squares = squares + value * value
        sums.append(squares)
        more.append((PP * z.columns + LANES // 2, top))
    row = to_row(z, [(k * z.columns, lane_sum(v)) for k, v in enumerate(sums)] + more)
    for k in range(sent.shape[0]):
        sent[k] = row


def finish(z, gathered, before, residual_in, direction, product, previous, multipliers, residual):
    alpha, _ = scalars(z, gathered, previous[...])
    for i in range(z.blocks):
        for h in range(z.halves):
            part = slice(h * LANES, (h + 1) * LANES)
            multipliers[:, i, part] = before[i, :, part] + alpha * direction[i, :, part]
            residual[:, i, part] = residual_in[i, :, part] - alpha * product[i, :, part]


def call(body, outs, scratch, cost, args, table=True, away=()):
    args = [
        pltpu.with_memory_space_constraint(a, pltpu.HBM) if k in away else a
        for k, a in enumerate(args)
    ]
    specs = [HBM if k in away else VMEM for k in range(len(args))]
    if table:
        specs[0] = SMEM
    shapes = [
        pltpu.SMEM(s, t) if t == jnp.int32 else jax.ShapeDtypeStruct(s, t) for s, t in outs
    ]
    return pl.pallas_call(
        body,
        out_shape=shapes,
        in_specs=specs,
        out_specs=[SMEM if t == jnp.int32 else VMEM for _, t in outs],
        scratch_shapes=scratch,
        compiler_params=pltpu.CompilerParams(vmem_limit_bytes=LIMIT),
        cost_estimate=pl.CostEstimate(flops=cost, bytes_accessed=cost // 16, transcendentals=0),
    )(*args)


def on_device(
    load,
    row_scale,
    diag_blocks,
    off_blocks,
    off_pattern,
    partner,
    corner_coupling,
    corner_index,
    coarse_inverse,
    *,
    mesh,
):
    z = Sizes(load, corner_coupling, coarse_inverse, mesh)
    cols, blocks, width = z.columns, z.blocks, z.width
    field = ((blocks, cols, width), F32)
    other = pltpu.VMEM((blocks + 1, cols, width), F32)
    extra = ((cols, z.extra), F32)
    light, heavy = 4_000_000, 600_000_000

    def shape(rows, kinds):
        return ((rows + (z.extra_chunks if kinds == 1 else 0), cols, LANES), F32)

    def kernel(body, *extra_args):
        return functools.partial(body, z, *extra_args)

    def across(piece, mask_of):
        pairs = [(t, t ^ mask_of(t & 1)) for t in range(z.peers)]
        return lax.ppermute(piece, "sub", pairs)

    def to_near(piece):
        return across(piece, lambda core: 1)

    def exchange(kinds, sources, near):
        *pieces, beside = call(
            kernel(relay, kinds),
            [shape(2 * z.rows(kinds), kinds)] * (len(z.far) + 1), [], light, [table, *sources, near],
        )
        far = [across(piece, lambda core: z.far[z.at(k, core)]) for k, piece in enumerate(pieces)]
        return [*far, to_near(beside)]

    table, loaded, lift, wide, corners, near = call(
        kernel(begin),
        [((z.table,), jnp.int32), field, field, field, ((blocks, 2 * z.corners, width), BF16)]
        + [shape(z.near_rows(2), 2)],
        [
            pltpu.VMEM(load.shape, F32),
            pltpu.VMEM(row_scale.shape, F32),
            pltpu.VMEM(corner_coupling.shape, BF16),
            pltpu.SMEM(partner.shape, jnp.int32),
            pltpu.SMEM(off_pattern.shape, jnp.int32),
            pltpu.SMEM((z.peers,), jnp.int32),
            pltpu.SemaphoreType.DMA((5,)),
        ],
        light,
        [partner, off_pattern, load, row_scale, corner_coupling],
        False, range(5),
    )
    arrived = exchange(2, [loaded, lift], to_near(near))
    weight = (diag_blocks.shape, BF16)
    operator, diag, off = call(
        kernel(prepare), [((z.all_corners, z.all_corners), F32), weight, weight],
        [
            pltpu.VMEM(corner_index.shape, jnp.int32),
            pltpu.VMEM(coarse_inverse.shape, F32),
            pltpu.SemaphoreType.DMA((4,)),
        ],
        heavy, [corner_index, coarse_inverse, diag_blocks, off_blocks], False, range(4),
    )
    half = ((blocks, 2 * cols, width), BF16)
    tile = ((cols, LANES), F32)
    devices = z.groups * z.peers
    fixed = [wide, diag, off, corners]
    multipliers = alpha = None
    for step in range(ITERS):
        early = [field, half, extra, shape(z.near_rows(1), 1)]
        if step == 0:
            residual, part, parts, own_extra, near = call(
                kernel(first_half, step), [field] + early, [other], heavy,
                [table, *fixed, *arrived, loaded],
            )
            direction = residual
            older = []
        else:
            way = direction
            residual, direction, alpha, part, parts, own_extra, near = call(
                kernel(first_half, step), [field, field, tile] + early, [], heavy,
                [table, *fixed, gathered, residual, way, product] + [alpha] * (step > 1),
            )
            older = [alpha, way] + [multipliers] * (step > 1)
        near = to_near(near)
        image, *more = call(
            kernel(second_half, step), [field] + [field] * (step > 0), [], heavy,
            [table, wide, diag, off, parts, part, *older],
        )
        if more:
            (multipliers,) = more
        if step == 0:
            (jump_lift,) = call(
                kernel(build_lift), [((blocks, 2 * z.all_corners, width), BF16)],
                [other, pltpu.VMEM((blocks, z.all_corners, width), F32)], heavy,
                [table, lift, *arrived],
            )
        arrived = exchange(1, [image, own_extra], near)
        product, sent = call(
            kernel(finish_product, step), [field, ((devices, 1, LANES), F32)], [other], heavy,
            [table, operator, image, own_extra, jump_lift, residual, direction, near]
            + [alpha] * (step > 0) + arrived,
        )
        gathered = lax.all_to_all(sent, ("group", "sub"), 0, 0, tiled=True)
    multipliers, residual = call(
        kernel(finish), [(load.shape, F32)] * 2, [], light,
        [gathered, multipliers, residual, direction, product, alpha], False,
    )
    return multipliers, residual


def solution(mesh):
    return jax.shard_map(
        functools.partial(on_device, mesh=dict(mesh.shape)),
        mesh=mesh,
        in_specs=(
            P(None, ("group", "sub"), None),
            P(("group", "sub"), None),
            P(("group", "sub"), None, None),
            P(("group", "sub"), None, None),
            P(("group", "sub"), None),
            P(("group", "sub"), None),
            P(("group", "sub"), None),
            P("group", None),
            P("group", None),
        ),
        out_specs=(P(None, ("group", "sub"), None), P(None, ("group", "sub"), None)),
        check_vma=False,
    )
```

```python
import functools

import jax
import jax.numpy as jnp
from jax import lax
from jax.experimental import pallas as pl
from jax.experimental.pallas import tpu as pltpu
from jax.sharding import PartitionSpec as P

ITERS = 4
HIGH = lax.Precision.HIGHEST
F32 = jnp.float32
BF16 = jnp.bfloat16
VMEM = pl.BlockSpec(memory_space=pltpu.VMEM)
SMEM = pl.BlockSpec(memory_space=pltpu.SMEM)
HBM = pl.BlockSpec(memory_space=pltpu.HBM)
LIMIT = 24 * 1024 * 1024
LANES = 128
RR, DP, RP, PP = range(4)
NN = (((1,), (0,)), ((), ()))
NT = (((1,), (1,)), ((), ()))
TN = (((0,), (0,)), ((), ()))


def dot(a, b, dims):
    return lax.dot_general(a, b, dims, preferred_element_type=F32)


def dot_high(a, b, dims):
    return lax.dot_general(a, b, dims, precision=HIGH, preferred_element_type=F32)


def pad(a):
    return jnp.concatenate([a, jnp.zeros_like(a)], axis=0).astype(BF16)


def split(a):
    high = a.astype(BF16).astype(F32)
    return jnp.concatenate([high, a - high], axis=0).astype(BF16)


def fold(a):
    half = a.shape[0] // 2
    return a[:half] + a[half:]


def lane_ids(shape):
    return lax.broadcasted_iota(jnp.int32, shape, 1)


class Sizes:
    def __init__(self, load, corner_coupling, coarse_inverse, mesh):
        self.columns = load.shape[0]
        self.blocks = load.shape[1]
        self.width = load.shape[2]
        self.corners = corner_coupling.shape[0]
        assert self.corners == self.columns
        self.coarse = coarse_inverse.shape[1]
        self.peers = mesh["sub"]
        self.groups = mesh["group"]
        self.capacity = (self.blocks + self.peers - 2) // (self.peers - 1)
        self.all_corners = self.peers * self.corners
        self.extra_chunks = -(-self.all_corners // LANES)
        self.extra = self.extra_chunks * LANES
        self.halves = self.width // LANES
        evens = range(2, self.peers, 2)
        self.beyond = [m for m in evens if m & (m - 1)]
        self.beside = [m for m in evens if m & (m - 1) == 0]
        self.far = self.beyond + self.beside
        self.handed = [m + 1 for m in self.far]
        self.slots = self.peers * self.capacity
        self.inverse = self.slots
        self.pattern = self.inverse + self.blocks
        self.partner = self.pattern + self.blocks
        self.order = self.partner + self.blocks
        self.count = self.order + self.blocks + 1
        self.table = self.count + 1
        most = len(self.far) * self.capacity
        self.early = min(-(-most * 3 // 4), self.blocks)
        self.middle = max(self.early, min(most, self.blocks))

    def rows(self, kinds):
        return kinds * self.capacity * self.halves

    def near_rows(self, kinds):
        return len(self.handed) * self.rows(kinds)

    def at(self, k, core):
        first = len(self.beyond)
        return k if k < first else first + (k - first + core) % len(self.beside)

    def mine(self, k):
        core = lax.axis_index("sub") & 1
        at = [self.at(k, c) for c in range(2)]
        return tuple(
            jnp.where(core == 0, jnp.int32(a), jnp.int32(b))
            for a, b in [at, [self.far[n] for n in at]]
        )

    def sources(self):
        found = [(1, 0, 0)]
        for k in range(len(self.far)):
            _, m = self.mine(k)
            found += [(m + side, 1 + k, side) for side in range(2)]
        return found


def fill_table(z, partner, pattern, table, counts):
    me = lax.axis_index("sub")
    for entry in range(z.slots):
        table[entry] = z.blocks
    for m in range(z.peers):
        counts[m] = 0
    for i in range(z.blocks):
        mate = partner[0, i]
        source = pattern[0, i]
        m = mate ^ me
        rank = counts[m]
        table[m * z.capacity + rank] = i
        counts[m] = rank + 1
        table[z.inverse + source] = i
        table[z.pattern + i] = source
        table[z.partner + i] = mate
    place = jnp.int32(0)
    for m in z.handed + z.far + [1]:
        for r in range(z.capacity):
            block = table[m * z.capacity + r]
            table[z.order + place] = block
            place = place + (block < z.blocks).astype(jnp.int32)
        if m == z.handed[-1]:
            table[z.count] = place


def fill_piece(z, table, sources, m, piece, row):
    for source in sources:
        for r in range(z.capacity):
            value = source[jnp.minimum(table[m * z.capacity + r], z.blocks - 1)]
            for h in range(z.halves):
                piece[row] = value[:, h * LANES : (h + 1) * LANES]
                row += 1


def fill_near(z, table, sources, near):
    for k, m in enumerate(z.handed):
        fill_piece(z, table, sources, m, near, k * z.rows(len(sources)))


def store_extra(z, tile, piece, row):
    for j in range(z.extra_chunks):
        piece[row + j] = tile[:, j * LANES : (j + 1) * LANES]


def load_extra(z, piece, row):
    return jnp.concatenate([piece[row + j] for j in range(z.extra_chunks)], axis=1)


def relay(z, kinds, table, *rest):
    sources, rest = rest[:kinds], rest[kinds:]
    if kinds == 1:
        extra, rest = rest[0], rest[1:]
    near, pieces, beside = rest[0], rest[1:-1], rest[-1]
    rows = z.rows(kinds)
    fill_piece(z, table, sources, 1, beside, 0)
    if kinds == 1:
        tile = extra[...] + load_extra(z, near, z.near_rows(1))
    for k, piece in enumerate(pieces):
        which, m = z.mine(k)
        fill_piece(z, table, sources, m, piece, 0)
        for row in range(rows):
            piece[rows + row] = near[which * rows + row]
        if kinds == 1:
            store_extra(z, tile, piece, 2 * rows)


def place(z, table, arrived, kind, kinds, target):
    for m, transfer, piece in z.sources():
        row = piece * z.rows(kinds) + z.rows(kind)
        for r in range(z.capacity):
            block = table[m * z.capacity + r]
            for h in range(z.halves):
                target[block, :, h * LANES : (h + 1) * LANES] = arrived[transfer][row]
                row += 1


def begin(z, partner, pattern, load, scale, coupling, table, field, lift, wide, corners, near, *scratch):
    here, scale_here, coupling_here, partner_here, pattern_here, counts, sems = scratch
    copies = [
        pltpu.make_async_copy(a, b, sems.at[k])
        for k, (a, b) in enumerate(
            [
                (partner, partner_here),
                (pattern, pattern_here),
                (load, here),
                (scale, scale_here),
                (coupling, coupling_here),
            ]
        )
    ]
    for copy in copies:
        copy.start()
    copies[0].wait()
    copies[1].wait()
    fill_table(z, partner_here, pattern_here, table, counts)
    for copy in copies[2:]:
        copy.wait()
    for i in range(z.blocks):
        field[i] = here[:, i, :]
        row = jnp.broadcast_to(scale_here[i : i + 1, :], (z.columns, z.width))
        wide[i] = row
        part = coupling_here[:, i * z.width : (i + 1) * z.width].astype(F32)
        lift[i] = row * part
        corners[i] = jnp.concatenate([part, jnp.zeros_like(part)], axis=0).astype(BF16)
    fill_near(z, table, [field, lift], near)


def split3(a):
    high = a.astype(BF16).astype(F32)
    middle = (a - high).astype(BF16).astype(F32)
    return [high, middle, a - high - middle]


def prepare(z, index_in, inverse_in, diag, off, operator, diag_out, off_out, index, inverse, sems):
    copies = [
        pltpu.make_async_copy(a, b, sems.at[k])
        for k, (a, b) in enumerate(
            [(index_in, index), (inverse_in, inverse), (diag, diag_out), (off, off_out)]
        )
    ]
    for copy in copies:
        copy.start()
    copies[0].wait()
    copies[1].wait()
    rows = lax.broadcasted_iota(jnp.int32, (z.coarse, z.all_corners), 0)
    select = (rows == index[...]).astype(BF16)
    parts = jnp.concatenate(split3(inverse[...]), axis=0).astype(BF16)
    half = dot(parts, select, NN)
    half = sum(half[k * z.coarse : (k + 1) * z.coarse] for k in range(3))
    parts = jnp.concatenate(split3(half), axis=1).astype(BF16)
    full = dot(select, parts, TN)
    operator[...] = sum(full[:, k * z.all_corners : (k + 1) * z.all_corners] for k in range(3))
    copies[2].wait()
    copies[3].wait()


def build_lift(z, table, lift, *rest):
    count = 1 + len(z.far)
    arrived, (jump_lift, other, full) = rest[:count], rest[count:]
    place(z, table, [arrived[-1], *arrived[:-1]], 1, 2, other)
    me = lax.axis_index("sub")
    for i in range(z.blocks):
        full[i] = jnp.zeros((z.all_corners, z.width), F32)
        own = pl.multiple_of(me * z.corners, z.corners)
        theirs = pl.multiple_of(table[z.partner + i] * z.corners, z.corners)
        full[i, pl.ds(own, z.corners), :] = lift[i]
        full[i, pl.ds(theirs, z.corners), :] = -other[i]
        jump_lift[i] = split(full[i])


def extra_sum(z, own, near, *far):
    total = own[...] + load_extra(z, near, z.near_rows(1))
    for piece in far:
        total = total + load_extra(z, piece, 2 * z.rows(1))
    return total


def lane_sum(a):
    return jnp.sum(a, axis=1, keepdims=True)


def to_row(z, values):
    shape = (z.columns, LANES)
    lanes = lane_ids(shape)
    rows = lax.broadcasted_iota(jnp.int32, shape, 0)
    tile = jnp.zeros(shape, F32)
    for first, value in values:
        tile = jnp.where(lanes == first + rows, value, tile)
    return jnp.sum(tile, axis=0, keepdims=True)


def to_tile(z, row, first):
    shape = (z.columns, LANES)
    rows = lax.broadcasted_iota(jnp.int32, shape, 0)
    tile = jnp.where(lane_ids(shape) == first + rows, jnp.broadcast_to(row, shape), 0.0)
    return jnp.broadcast_to(lane_sum(tile), shape)


def scalars(z, gathered, previous):
    zero = jnp.zeros((1, LANES), F32)
    count = gathered.shape[0]
    unroll = 32 if count % 32 == 0 else 1
    total = lax.fori_loop(0, count, lambda k, acc: acc + gathered[k], zero, unroll=unroll)
    norm, way, rest = [to_tile(z, total, k * z.columns) for k in (RR, DP, RP)]
    alpha = norm / way
    if previous is None:
        placed = to_row(z, [(PP * z.columns, alpha)])

        def squares(k, acc):
            row = gathered[k]
            step = placed * pltpu.roll(row, LANES // 2, 1)
            return acc + row * step * step

        moved = lax.fori_loop(0, count, squares, zero, unroll=unroll)
        moved = to_tile(z, moved, PP * z.columns)
    else:
        ratio = alpha / used_step(previous)
        moved = to_tile(z, total, PP * z.columns) * ratio * ratio
    return alpha, (norm - 2.0 * alpha * rest + moved) / norm


def used_step(previous):
    return jnp.where(previous == 0.0, 1.0, previous)


def across_block(z, tile):
    return jnp.concatenate([tile] * z.halves, axis=1)


def couple(z, i, table, wide, diag, off, parts):
    source = table[z.inverse + i]
    mine = parts[i]
    coupled = dot(mine, diag[i], NT) + dot(mine, diag[i], NN)
    coupled = coupled + dot(parts[table[z.pattern + i]], off[i], NT)
    coupled = coupled + dot(parts[source], off[source], NN)
    return wide[i] * fold(coupled + mine.astype(F32))


def first_half(z, step, table, *rest):
    rest = list(rest)
    take = lambda n: [rest.pop(0) for _ in range(n)]
    wide, diag, off, corners = take(4)
    if step == 0:
        *far, beside, loaded = take(2 + len(z.far))
        residual, image, parts, extra, near_out, other = rest
        direction = residual
        place(z, table, [beside, *far], 0, 2, other)
    else:
        gathered, before, way, product = take(4)
        previous = take(1)[0][...] if step > 1 else None
        residual, direction, step_out, image, parts, extra, near_out = rest
        alpha, beta = scalars(z, gathered, previous)
        step_out[...] = alpha
        alpha, beta = across_block(z, alpha), across_block(z, beta)
    partial = jnp.zeros((2 * z.columns, 2 * z.corners), F32)
    for i in range(z.blocks):
        if step == 0:
            value = loaded[i] - other[i]
            residual[i] = value
        else:
            value = before[i] - alpha * product[i]
            residual[i] = value
            value = value + beta * way[i]
            direction[i] = value
        mine = pad(wide[i] * value)
        parts[i] = mine
        partial = partial + dot(mine, corners[i], NT)
    refs = (table, wide, diag, off, parts)
    for position in range(z.early):
        i = table[z.order + position]
        image[i] = couple(z, i, *refs)

    for position in range(z.early, z.middle):

        @pl.when(table[z.count] > position)
        def _():
            i = table[z.order + position]
            image[i] = couple(z, i, *refs)

    fill_near(z, table, [image], near_out)
    sums = fold(partial)
    padded = jnp.concatenate(
        [sums, jnp.zeros((z.columns, z.extra - sums.shape[1]), F32)], axis=1
    )
    tile = pltpu.roll(padded, lax.axis_index("sub") * z.corners, 1)
    extra[...] = tile
    store_extra(z, tile, near_out, z.near_rows(1))


def second_half(z, step, table, wide, diag, off, parts, image_in, *rest):
    if step == 0:
        (image,) = rest
    elif step == 1:
        alpha, way, image, multipliers = rest
    else:
        alpha, way, before, image, multipliers = rest
    refs = (table, wide, diag, off, parts)
    for i in range(z.blocks):
        image[i] = image_in[i]

    for position in range(z.early, z.middle):

        @pl.when(table[z.count] <= position)
        def _():
            i = table[z.order + position]
            image[i] = couple(z, i, *refs)

    for position in range(z.middle, z.blocks):
        i = table[z.order + position]
        image[i] = couple(z, i, *refs)
    if step > 0:
        size = across_block(z, alpha[...])
        for i in range(z.blocks):
            value = size * way[i]
            multipliers[i] = value if step == 1 else before[i] + value


def finish_product(z, step, table, operator, image, own_extra, jump_lift, residual, direction, near, *rest):
    *far, beside, product, sent, other = rest
    if step > 0:
        previous, far = far[0], far[1:]
        scale = across_block(z, used_step(previous[...]))
    place(z, table, [beside, *far], 0, 1, other)
    partials = extra_sum(z, own_extra, near, *far)[:, : z.all_corners]
    local = dot_high(partials, operator[...], NT)
    rows = pad(jnp.concatenate([local, local], axis=1))
    zero = jnp.zeros((z.columns, z.width), F32)
    sums = [zero] * (4 if step > 0 else 3)
    top = zero
    for i in range(z.blocks):
        value = image[i] - other[i] + fold(dot(rows, jump_lift[i], NN))
        product[i] = value
        r, d = residual[i], direction[i]
        pairs = [(r, r), (d, value), (r, value)]
        if step > 0:
            scaled = scale * value
            pairs.append((scaled, scaled))
        else:
            top = jnp.maximum(top, jnp.abs(value))
        sums = [s + a * b for s, (a, b) in zip(sums, pairs)]
    more = []
    if step == 0:
        top = jnp.max(top, axis=1, keepdims=True)
        shrink = jnp.where(top > 0.0, 1.0 / top, 0.0)
        squares = zero
        for i in range(z.blocks):
            value = product[i] * shrink
            squares = squares + value * value
        sums.append(squares)
        more.append((PP * z.columns + LANES // 2, top))
    row = to_row(z, [(k * z.columns, lane_sum(v)) for k, v in enumerate(sums)] + more)
    for k in range(sent.shape[0]):
        sent[k] = row


def finish(z, gathered, before, residual_in, direction, product, previous, multipliers, residual):
    alpha, _ = scalars(z, gathered, previous[...])
    for i in range(z.blocks):
        for h in range(z.halves):
            part = slice(h * LANES, (h + 1) * LANES)
            multipliers[:, i, part] = before[i, :, part] + alpha * direction[i, :, part]
            residual[:, i, part] = residual_in[i, :, part] - alpha * product[i, :, part]


def call(body, outs, scratch, cost, args, table=True, away=()):
    args = [
        pltpu.with_memory_space_constraint(a, pltpu.HBM) if k in away else a
        for k, a in enumerate(args)
    ]
    specs = [HBM if k in away else VMEM for k in range(len(args))]
    if table:
        specs[0] = SMEM
    shapes = [
        pltpu.SMEM(s, t) if t == jnp.int32 else jax.ShapeDtypeStruct(s, t) for s, t in outs
    ]
    return pl.pallas_call(
        body,
        out_shape=shapes,
        in_specs=specs,
        out_specs=[SMEM if t == jnp.int32 else VMEM for _, t in outs],
        scratch_shapes=scratch,
        compiler_params=pltpu.CompilerParams(vmem_limit_bytes=LIMIT),
        cost_estimate=pl.CostEstimate(flops=cost, bytes_accessed=cost // 16, transcendentals=0),
    )(*args)


def on_device(
    load,
    row_scale,
    diag_blocks,
    off_blocks,
    off_pattern,
    partner,
    corner_coupling,
    corner_index,
    coarse_inverse,
    *,
    mesh,
):
    z = Sizes(load, corner_coupling, coarse_inverse, mesh)
    cols, blocks, width = z.columns, z.blocks, z.width
    field = ((blocks, cols, width), F32)
    other = pltpu.VMEM((blocks + 1, cols, width), F32)
    extra = ((cols, z.extra), F32)
    light, heavy = 4_000_000, 600_000_000

    def shape(rows, kinds):
        return ((rows + (z.extra_chunks if kinds == 1 else 0), cols, LANES), F32)

    def kernel(body, *extra_args):
        return functools.partial(body, z, *extra_args)

    def across(piece, mask_of):
        pairs = [(t, t ^ mask_of(t & 1)) for t in range(z.peers)]
        return lax.ppermute(piece, "sub", pairs)

    def to_near(piece):
        return across(piece, lambda core: 1)

    def exchange(kinds, sources, near):
        *pieces, beside = call(
            kernel(relay, kinds),
            [shape(2 * z.rows(kinds), kinds)] * (len(z.far) + 1), [], light, [table, *sources, near],
        )
        far = [across(piece, lambda core: z.far[z.at(k, core)]) for k, piece in enumerate(pieces)]
        return [*far, to_near(beside)]

    table, loaded, lift, wide, corners, near = call(
        kernel(begin),
        [((z.table,), jnp.int32), field, field, field, ((blocks, 2 * z.corners, width), BF16)]
        + [shape(z.near_rows(2), 2)],
        [
            pltpu.VMEM(load.shape, F32),
            pltpu.VMEM(row_scale.shape, F32),
            pltpu.VMEM(corner_coupling.shape, BF16),
            pltpu.SMEM(partner.shape, jnp.int32),
            pltpu.SMEM(off_pattern.shape, jnp.int32),
            pltpu.SMEM((z.peers,), jnp.int32),
            pltpu.SemaphoreType.DMA((5,)),
        ],
        light,
        [partner, off_pattern, load, row_scale, corner_coupling],
        False, range(5),
    )
    arrived = exchange(2, [loaded, lift], to_near(near))
    weight = (diag_blocks.shape, BF16)
    operator, diag, off = call(
        kernel(prepare), [((z.all_corners, z.all_corners), F32), weight, weight],
        [
            pltpu.VMEM(corner_index.shape, jnp.int32),
            pltpu.VMEM(coarse_inverse.shape, F32),
            pltpu.SemaphoreType.DMA((4,)),
        ],
        heavy, [corner_index, coarse_inverse, diag_blocks, off_blocks], False, range(4),
    )
    half = ((blocks, 2 * cols, width), BF16)
    tile = ((cols, LANES), F32)
    devices = z.groups * z.peers
    fixed = [wide, diag, off, corners]
    multipliers = alpha = None
    for step in range(ITERS):
        early = [field, half, extra, shape(z.near_rows(1), 1)]
        if step == 0:
            residual, part, parts, own_extra, near = call(
                kernel(first_half, step), [field] + early, [other], heavy,
                [table, *fixed, *arrived, loaded],
            )
            direction = residual
            older = []
        else:
            way = direction
            residual, direction, alpha, part, parts, own_extra, near = call(
                kernel(first_half, step), [field, field, tile] + early, [], heavy,
                [table, *fixed, gathered, residual, way, product] + [alpha] * (step > 1),
            )
            older = [alpha, way] + [multipliers] * (step > 1)
        near = to_near(near)
        image, *more = call(
            kernel(second_half, step), [field] + [field] * (step > 0), [], heavy,
            [table, wide, diag, off, parts, part, *older],
        )
        if more:
            (multipliers,) = more
        if step == 0:
            (jump_lift,) = call(
                kernel(build_lift), [((blocks, 2 * z.all_corners, width), BF16)],
                [other, pltpu.VMEM((blocks, z.all_corners, width), F32)], heavy,
                [table, lift, *arrived],
            )
        arrived = exchange(1, [image, own_extra], near)
        product, sent = call(
            kernel(finish_product, step), [field, ((devices, 1, LANES), F32)], [other], heavy,
            [table, operator, image, own_extra, jump_lift, residual, direction, near]
            + [alpha] * (step > 0) + arrived,
        )
        gathered = lax.all_to_all(sent, ("sub", "group"), 0, 0, tiled=True)
    multipliers, residual = call(
        kernel(finish), [(load.shape, F32)] * 2, [], light,
        [gathered, multipliers, residual, direction, product, alpha], False,
    )
    return multipliers, residual


def solution(mesh):
    return jax.shard_map(
        functools.partial(on_device, mesh=dict(mesh.shape)),
        mesh=mesh,
        in_specs=(
            P(None, ("group", "sub"), None),
            P(("group", "sub"), None),
            P(("group", "sub"), None, None),
            P(("group", "sub"), None, None),
            P(("group", "sub"), None),
            P(("group", "sub"), None),
            P(("group", "sub"), None),
            P("group", None),
            P("group", None),
        ),
        out_specs=(P(None, ("group", "sub"), None), P(None, ("group", "sub"), None)),
        check_vma=False,
    )
```

```python
import functools

import jax
import jax.numpy as jnp
from jax import lax
from jax.experimental import pallas as pl
from jax.experimental.pallas import tpu as pltpu
from jax.sharding import PartitionSpec as P

ITERS = 4
HIGH = lax.Precision.HIGHEST
F32 = jnp.float32
BF16 = jnp.bfloat16
VMEM = pl.BlockSpec(memory_space=pltpu.VMEM)
SMEM = pl.BlockSpec(memory_space=pltpu.SMEM)
HBM = pl.BlockSpec(memory_space=pltpu.HBM)
LIMIT = 24 * 1024 * 1024
LANES = 128
RR, DP, RP, PP = range(4)
NN = (((1,), (0,)), ((), ()))
NT = (((1,), (1,)), ((), ()))
TN = (((0,), (0,)), ((), ()))


def dot(a, b, dims):
    return lax.dot_general(a, b, dims, preferred_element_type=F32)


def dot_high(a, b, dims):
    return lax.dot_general(a, b, dims, precision=HIGH, preferred_element_type=F32)


def pad(a):
    return jnp.concatenate([a, jnp.zeros_like(a)], axis=0).astype(BF16)


def split(a):
    high = a.astype(BF16).astype(F32)
    return jnp.concatenate([high, a - high], axis=0).astype(BF16)


def fold(a):
    half = a.shape[0] // 2
    return a[:half] + a[half:]


def lane_ids(shape):
    return lax.broadcasted_iota(jnp.int32, shape, 1)


class Sizes:
    def __init__(self, load, corner_coupling, coarse_inverse, mesh):
        self.columns = load.shape[0]
        self.blocks = load.shape[1]
        self.width = load.shape[2]
        self.corners = corner_coupling.shape[0]
        assert self.corners == self.columns
        self.coarse = coarse_inverse.shape[1]
        self.peers = mesh["sub"]
        self.groups = mesh["group"]
        self.capacity = (self.blocks + self.peers - 2) // (self.peers - 1)
        self.all_corners = self.peers * self.corners
        self.extra_chunks = -(-self.all_corners // LANES)
        self.extra = self.extra_chunks * LANES
        self.halves = self.width // LANES
        evens = range(2, self.peers, 2)
        self.beyond = [m for m in evens if m & (m - 1)]
        self.beside = [m for m in evens if m & (m - 1) == 0]
        assert len(self.beside) % 2 == 0
        self.turns = len(self.beside) // 2
        self.slots = self.peers * self.capacity
        self.inverse = self.slots
        self.pattern = self.inverse + self.blocks
        self.partner = self.pattern + self.blocks
        self.order = self.partner + self.blocks
        self.count = self.order + self.blocks + 1
        self.table = self.count + 1
        most = (len(self.beside) + len(self.beyond)) * self.capacity
        self.early = min(-(-most * 7 // 8), self.blocks)
        self.middle = max(self.early, min(most, self.blocks))

    def rows(self, kinds):
        return kinds * self.capacity * self.halves

    def near_rows(self, kinds):
        return (len(self.beside) + len(self.beyond)) * self.rows(kinds)

    def beside_rows(self, kinds):
        return 4 * self.rows(kinds)

    def beyond_rows(self, kinds):
        return 2 * self.rows(kinds)

    def on_rows(self, kinds):
        return (1 + len(self.beside)) * self.rows(kinds)

    def carried(self, k, core):
        return self.beside[2 * k + core]

    def mine(self, k):
        core = lax.axis_index("sub") & 1
        masks = [jnp.int32(self.carried(k, c)) for c in range(2)]
        return tuple(jnp.where(core == c, masks[0], masks[1]) for c in range(2))

    def handed(self):
        theirs = [self.mine(k)[1] for k in range(self.turns)]
        return [m + side for m in theirs for side in range(2)] + [m + 1 for m in self.beyond]

    def kept(self):
        own = [self.mine(k)[0] for k in range(self.turns)]
        return [m + side for m in own for side in range(2)] + self.beyond + [1]

    def sources(self):
        found = []
        last = self.turns + len(self.beyond)
        for k in range(self.turns):
            own, other = self.mine(k)
            found += [(own, k, 0), (own + 1, k, 2)]
            found += [(other + 1, last, 1 + 2 * k), (other, last, 2 + 2 * k)]
        for k, m in enumerate(self.beyond):
            found += [(m, self.turns + k, 0), (m + 1, self.turns + k, 1)]
        return found + [(1, last, 0)]


def fill_table(z, partner, pattern, table, counts):
    me = lax.axis_index("sub")
    for entry in range(z.slots):
        table[entry] = z.blocks
    for m in range(z.peers):
        counts[m] = 0
    for i in range(z.blocks):
        mate = partner[0, i]
        source = pattern[0, i]
        m = mate ^ me
        rank = counts[m]
        table[m * z.capacity + rank] = i
        counts[m] = rank + 1
        table[z.inverse + source] = i
        table[z.pattern + i] = source
        table[z.partner + i] = mate
    place = jnp.int32(0)

    def follow(masks, place):
        for m in masks:
            for r in range(z.capacity):
                block = table[m * z.capacity + r]
                table[z.order + place] = block
                place = place + (block < z.blocks).astype(jnp.int32)
        return place

    place = follow(z.handed(), place)
    table[z.count] = place
    follow(z.kept(), place)


def fill_piece(z, table, sources, m, piece, row):
    for source in sources:
        for r in range(z.capacity):
            value = source[jnp.minimum(table[m * z.capacity + r], z.blocks - 1)]
            for h in range(z.halves):
                piece[row] = value[:, h * LANES : (h + 1) * LANES]
                row += 1


def fill_near(z, table, sources, near):
    for k, m in enumerate(z.handed()):
        fill_piece(z, table, sources, m, near, k * z.rows(len(sources)))


def store_extra(z, tile, piece, row):
    for j in range(z.extra_chunks):
        piece[row + j] = tile[:, j * LANES : (j + 1) * LANES]


def load_extra(z, piece, row):
    return jnp.concatenate([piece[row + j] for j in range(z.extra_chunks)], axis=1)


def copy_piece(rows, source, at, target, to):
    for row in range(rows):
        target[to * rows + row] = source[at * rows + row]


def relay(z, kinds, table, *rest):
    sources, rest = rest[:kinds], rest[kinds:]
    if kinds == 1:
        extra, rest = rest[0], rest[1:]
    near, pieces = rest[0], rest[1:]
    rows = z.rows(kinds)
    if kinds == 1:
        tile = extra[...] + load_extra(z, near, z.near_rows(1))
    for k, piece in enumerate(pieces[: z.turns]):
        m, _ = z.mine(k)
        fill_piece(z, table, sources, m, piece, 0)
        fill_piece(z, table, sources, m + 1, piece, rows)
        copy_piece(rows, near, 2 * k + 1, piece, 2)
        copy_piece(rows, near, 2 * k, piece, 3)
        if kinds == 1:
            store_extra(z, tile, piece, z.beside_rows(1))
    for k, (m, piece) in enumerate(zip(z.beyond, pieces[z.turns :])):
        fill_piece(z, table, sources, m, piece, 0)
        copy_piece(rows, near, len(z.beside) + k, piece, 1)
        if kinds == 1:
            store_extra(z, tile, piece, z.beyond_rows(1))


def keep(z, source, target):
    target[...] = source[...]


def hand_on(z, kinds, table, *rest):
    sources, arrived, piece = rest[:kinds], rest[kinds:-1], rest[-1]
    rows = z.rows(kinds)
    fill_piece(z, table, sources, 1, piece, 0)
    for k, source in enumerate(arrived):
        copy_piece(rows, source, 1, piece, 1 + 2 * k)
        copy_piece(rows, source, 3, piece, 2 + 2 * k)
        if kinds == 1:
            tile = load_extra(z, source, z.beside_rows(1))
            store_extra(z, tile, piece, z.on_rows(1) + k * z.extra_chunks)


def place(z, table, arrived, kind, kinds, target):
    for m, transfer, piece in z.sources():
        row = piece * z.rows(kinds) + z.rows(kind)
        for r in range(z.capacity):
            block = table[m * z.capacity + r]
            for h in range(z.halves):
                target[block, :, h * LANES : (h + 1) * LANES] = arrived[transfer][row]
                row += 1


def begin(z, partner, pattern, load, scale, coupling, table, field, lift, wide, corners, near, *scratch):
    here, scale_here, coupling_here, partner_here, pattern_here, counts, sems = scratch
    copies = [
        pltpu.make_async_copy(a, b, sems.at[k])
        for k, (a, b) in enumerate(
            [
                (partner, partner_here),
                (pattern, pattern_here),
                (load, here),
                (scale, scale_here),
                (coupling, coupling_here),
            ]
        )
    ]
    for copy in copies:
        copy.start()
    copies[0].wait()
    copies[1].wait()
    fill_table(z, partner_here, pattern_here, table, counts)
    for copy in copies[2:]:
        copy.wait()
    for i in range(z.blocks):
        field[i] = here[:, i, :]
        row = jnp.broadcast_to(scale_here[i : i + 1, :], (z.columns, z.width))
        wide[i] = row
        part = coupling_here[:, i * z.width : (i + 1) * z.width].astype(F32)
        lift[i] = row * part
        corners[i] = jnp.concatenate([part, jnp.zeros_like(part)], axis=0).astype(BF16)
    fill_near(z, table, [field, lift], near)


def split3(a):
    high = a.astype(BF16).astype(F32)
    middle = (a - high).astype(BF16).astype(F32)
    return [high, middle, a - high - middle]


def prepare(z, index_in, inverse_in, diag, off, operator, diag_out, off_out, index, inverse, sems):
    copies = [
        pltpu.make_async_copy(a, b, sems.at[k])
        for k, (a, b) in enumerate(
            [(index_in, index), (inverse_in, inverse), (diag, diag_out), (off, off_out)]
        )
    ]
    for copy in copies:
        copy.start()
    copies[0].wait()
    copies[1].wait()
    rows = lax.broadcasted_iota(jnp.int32, (z.coarse, z.all_corners), 0)
    select = (rows == index[...]).astype(BF16)
    parts = jnp.concatenate(split3(inverse[...]), axis=0).astype(BF16)
    half = dot(parts, select, NN)
    half = sum(half[k * z.coarse : (k + 1) * z.coarse] for k in range(3))
    parts = jnp.concatenate(split3(half), axis=1).astype(BF16)
    full = dot(select, parts, TN)
    operator[...] = sum(full[:, k * z.all_corners : (k + 1) * z.all_corners] for k in range(3))
    copies[2].wait()
    copies[3].wait()


def build_lift(z, table, lift, *rest):
    arrived, (jump_lift, other, full) = rest[:-3], rest[-3:]
    place(z, table, arrived, 1, 2, other)
    me = lax.axis_index("sub")
    for i in range(z.blocks):
        full[i] = jnp.zeros((z.all_corners, z.width), F32)
        own = pl.multiple_of(me * z.corners, z.corners)
        theirs = pl.multiple_of(table[z.partner + i] * z.corners, z.corners)
        full[i, pl.ds(own, z.corners), :] = lift[i]
        full[i, pl.ds(theirs, z.corners), :] = -other[i]
        jump_lift[i] = split(full[i])


def extra_sum(z, own, near, arrived):
    total = own[...] + load_extra(z, near, z.near_rows(1))
    for k in range(z.turns):
        total = total + load_extra(z, arrived[k], z.beside_rows(1))
        total = total + load_extra(z, arrived[-1], z.on_rows(1) + k * z.extra_chunks)
    for piece in arrived[z.turns : -1]:
        total = total + load_extra(z, piece, z.beyond_rows(1))
    return total


def lane_sum(a):
    return jnp.sum(a, axis=1, keepdims=True)


def to_row(z, values):
    shape = (z.columns, LANES)
    lanes = lane_ids(shape)
    rows = lax.broadcasted_iota(jnp.int32, shape, 0)
    tile = jnp.zeros(shape, F32)
    for first, value in values:
        tile = jnp.where(lanes == first + rows, value, tile)
    return jnp.sum(tile, axis=0, keepdims=True)


def to_tile(z, row, first):
    shape = (z.columns, LANES)
    rows = lax.broadcasted_iota(jnp.int32, shape, 0)
    tile = jnp.where(lane_ids(shape) == first + rows, jnp.broadcast_to(row, shape), 0.0)
    return jnp.broadcast_to(lane_sum(tile), shape)


def scalars(z, gathered, previous):
    zero = jnp.zeros((1, LANES), F32)
    count = gathered.shape[0]
    unroll = 32 if count % 32 == 0 else 1
    total = lax.fori_loop(0, count, lambda k, acc: acc + gathered[k], zero, unroll=unroll)
    norm, way, rest = [to_tile(z, total, k * z.columns) for k in (RR, DP, RP)]
    alpha = norm / way
    if previous is None:
        placed = to_row(z, [(PP * z.columns, alpha)])

        def squares(k, acc):
            row = gathered[k]
            step = placed * pltpu.roll(row, LANES // 2, 1)
            return acc + row * step * step

        moved = lax.fori_loop(0, count, squares, zero, unroll=unroll)
        moved = to_tile(z, moved, PP * z.columns)
    else:
        ratio = alpha / used_step(previous)
        moved = to_tile(z, total, PP * z.columns) * ratio * ratio
    return alpha, (norm - 2.0 * alpha * rest + moved) / norm


def used_step(previous):
    return jnp.where(previous == 0.0, 1.0, previous)


def across_block(z, tile):
    return jnp.concatenate([tile] * z.halves, axis=1)


def couple(z, i, table, wide, diag, off, parts):
    source = table[z.inverse + i]
    mine = parts[i]
    coupled = dot(mine, diag[i], NT) + dot(mine, diag[i], NN)
    coupled = coupled + dot(parts[table[z.pattern + i]], off[i], NT)
    coupled = coupled + dot(parts[source], off[source], NN)
    return wide[i] * fold(coupled + mine.astype(F32))


def first_half(z, step, table, *rest):
    rest = list(rest)
    take = lambda n: [rest.pop(0) for _ in range(n)]
    wide, diag, off, corners = take(4)
    if step == 0:
        *arrived, loaded = take(2 + z.turns + len(z.beyond))
        residual, image, parts, extra, near_out, other = rest
        direction = residual
        place(z, table, arrived, 0, 2, other)
    else:
        gathered, before, way, product = take(4)
        previous = take(1)[0][...] if step > 1 else None
        residual, direction, step_out, image, parts, extra, near_out = rest
        alpha, beta = scalars(z, gathered, previous)
        step_out[...] = alpha
        alpha, beta = across_block(z, alpha), across_block(z, beta)
    partial = jnp.zeros((2 * z.columns, 2 * z.corners), F32)
    for i in range(z.blocks):
        if step == 0:
            value = loaded[i] - other[i]
            residual[i] = value
        else:
            value = before[i] - alpha * product[i]
            residual[i] = value
            value = value + beta * way[i]
            direction[i] = value
        mine = pad(wide[i] * value)
        parts[i] = mine
        partial = partial + dot(mine, corners[i], NT)
    refs = (table, wide, diag, off, parts)
    for position in range(z.early):
        i = table[z.order + position]
        image[i] = couple(z, i, *refs)

    @pl.when(table[z.count] > z.early)
    def _():
        for position in range(z.early, z.middle):
            i = table[z.order + position]
            image[i] = couple(z, i, *refs)

    fill_near(z, table, [image], near_out)
    sums = fold(partial)
    padded = jnp.concatenate(
        [sums, jnp.zeros((z.columns, z.extra - sums.shape[1]), F32)], axis=1
    )
    tile = pltpu.roll(padded, lax.axis_index("sub") * z.corners, 1)
    extra[...] = tile
    store_extra(z, tile, near_out, z.near_rows(1))


def second_half(z, step, table, wide, diag, off, parts, image_in, *rest):
    if step == 0:
        (image,) = rest
    elif step == 1:
        alpha, way, image, multipliers = rest
    else:
        alpha, way, before, image, multipliers = rest
    refs = (table, wide, diag, off, parts)
    for i in range(z.blocks):
        image[i] = image_in[i]

    @pl.when(table[z.count] <= z.early)
    def _():
        for position in range(z.early, z.middle):
            i = table[z.order + position]
            image[i] = couple(z, i, *refs)

    for position in range(z.middle, z.blocks):
        i = table[z.order + position]
        image[i] = couple(z, i, *refs)
    if step > 0:
        size = across_block(z, alpha[...])
        for i in range(z.blocks):
            value = size * way[i]
            multipliers[i] = value if step == 1 else before[i] + value


def finish_product(z, step, table, operator, image, own_extra, jump_lift, residual, direction, near, *rest):
    *arrived, product, sent, other = rest
    if step > 0:
        previous, arrived = arrived[0], arrived[1:]
        scale = across_block(z, used_step(previous[...]))
    place(z, table, arrived, 0, 1, other)
    partials = extra_sum(z, own_extra, near, arrived)[:, : z.all_corners]
    local = dot_high(partials, operator[...], NT)
    rows = pad(jnp.concatenate([local, local], axis=1))
    zero = jnp.zeros((z.columns, z.width), F32)
    sums = [zero] * (4 if step > 0 else 3)
    top = zero
    for i in range(z.blocks):
        value = image[i] - other[i] + fold(dot(rows, jump_lift[i], NN))
        product[i] = value
        r, d = residual[i], direction[i]
        pairs = [(r, r), (d, value), (r, value)]
        if step > 0:
            scaled = scale * value
            pairs.append((scaled, scaled))
        else:
            top = jnp.maximum(top, jnp.abs(value))
        sums = [s + a * b for s, (a, b) in zip(sums, pairs)]
    more = []
    if step == 0:
        top = jnp.max(top, axis=1, keepdims=True)
        shrink = jnp.where(top > 0.0, 1.0 / top, 0.0)
        squares = zero
        for i in range(z.blocks):
            value = product[i] * shrink
            squares = squares + value * value
        sums.append(squares)
        more.append((PP * z.columns + LANES // 2, top))
    row = to_row(z, [(k * z.columns, lane_sum(v)) for k, v in enumerate(sums)] + more)
    for k in range(sent.shape[0]):
        sent[k] = row


def finish(z, gathered, before, residual_in, direction, product, previous, multipliers, residual):
    alpha, _ = scalars(z, gathered, previous[...])
    for i in range(z.blocks):
        for h in range(z.halves):
            part = slice(h * LANES, (h + 1) * LANES)
            multipliers[:, i, part] = before[i, :, part] + alpha * direction[i, :, part]
            residual[:, i, part] = residual_in[i, :, part] - alpha * product[i, :, part]


def call(body, outs, scratch, cost, args, table=True, away=()):
    args = [
        pltpu.with_memory_space_constraint(a, pltpu.HBM) if k in away else a
        for k, a in enumerate(args)
    ]
    specs = [HBM if k in away else VMEM for k in range(len(args))]
    if table:
        specs[0] = SMEM
    shapes = [
        pltpu.SMEM(s, t) if t == jnp.int32 else jax.ShapeDtypeStruct(s, t) for s, t in outs
    ]
    return pl.pallas_call(
        body,
        out_shape=shapes,
        in_specs=specs,
        out_specs=[SMEM if t == jnp.int32 else VMEM for _, t in outs],
        scratch_shapes=scratch,
        compiler_params=pltpu.CompilerParams(vmem_limit_bytes=LIMIT),
        cost_estimate=pl.CostEstimate(flops=cost, bytes_accessed=cost // 16, transcendentals=0),
    )(*args)


def on_device(
    load,
    row_scale,
    diag_blocks,
    off_blocks,
    off_pattern,
    partner,
    corner_coupling,
    corner_index,
    coarse_inverse,
    *,
    mesh,
):
    z = Sizes(load, corner_coupling, coarse_inverse, mesh)
    cols, blocks, width = z.columns, z.blocks, z.width
    field = ((blocks, cols, width), F32)
    other = pltpu.VMEM((blocks + 1, cols, width), F32)
    extra = ((cols, z.extra), F32)
    light, heavy = 4_000_000, 600_000_000

    def shape(rows, kinds, chunks=1):
        return ((rows + (chunks * z.extra_chunks if kinds == 1 else 0), cols, LANES), F32)

    def kernel(body, *extra_args):
        return functools.partial(body, z, *extra_args)

    def across(piece, mask_of):
        pairs = [(t, t ^ mask_of(t & 1)) for t in range(z.peers)]
        return lax.ppermute(piece, "sub", pairs)

    def to_near(piece):
        return across(piece, lambda core: 1)

    def exchange(kinds, sources, near):
        fields = sources[:kinds]
        pieces = call(
            kernel(relay, kinds),
            [shape(z.beside_rows(kinds), kinds)] * z.turns
            + [shape(z.beyond_rows(kinds), kinds)] * len(z.beyond),
            [], light, [table, *sources, near],
        )
        beside = [
            across(piece, lambda core: z.carried(k, core)) for k, piece in enumerate(pieces[: z.turns])
        ]
        beyond = [across(piece, lambda core: m) for m, piece in zip(z.beyond, pieces[z.turns :])]
        beyond = [
            call(kernel(keep), [(piece.shape, F32)], [], heavy, [piece], False)[0] for piece in beyond
        ]
        (piece,) = call(
            kernel(hand_on, kinds), [shape(z.on_rows(kinds), kinds, z.turns)], [], light,
            [table, *fields, *beside],
        )
        return [*beside, *beyond, to_near(piece)]

    table, loaded, lift, wide, corners, near = call(
        kernel(begin),
        [((z.table,), jnp.int32), field, field, field, ((blocks, 2 * z.corners, width), BF16)]
        + [shape(z.near_rows(2), 2)],
        [
            pltpu.VMEM(load.shape, F32),
            pltpu.VMEM(row_scale.shape, F32),
            pltpu.VMEM(corner_coupling.shape, BF16),
            pltpu.SMEM(partner.shape, jnp.int32),
            pltpu.SMEM(off_pattern.shape, jnp.int32),
            pltpu.SMEM((z.peers,), jnp.int32),
            pltpu.SemaphoreType.DMA((5,)),
        ],
        light,
        [partner, off_pattern, load, row_scale, corner_coupling],
        False, range(5),
    )
    arrived = exchange(2, [loaded, lift], to_near(near))
    weight = (diag_blocks.shape, BF16)
    operator, diag, off = call(
        kernel(prepare), [((z.all_corners, z.all_corners), F32), weight, weight],
        [
            pltpu.VMEM(corner_index.shape, jnp.int32),
            pltpu.VMEM(coarse_inverse.shape, F32),
            pltpu.SemaphoreType.DMA((4,)),
        ],
        heavy, [corner_index, coarse_inverse, diag_blocks, off_blocks], False, range(4),
    )
    half = ((blocks, 2 * cols, width), BF16)
    tile = ((cols, LANES), F32)
    devices = z.groups * z.peers
    fixed = [wide, diag, off, corners]
    multipliers = alpha = None
    for step in range(ITERS):
        early = [field, half, extra, shape(z.near_rows(1), 1)]
        if step == 0:
            residual, part, parts, own_extra, near = call(
                kernel(first_half, step), [field] + early, [other], heavy,
                [table, *fixed, *arrived, loaded],
            )
            direction = residual
            older = []
        else:
            way = direction
            residual, direction, alpha, part, parts, own_extra, near = call(
                kernel(first_half, step), [field, field, tile] + early, [], heavy,
                [table, *fixed, gathered, residual, way, product] + [alpha] * (step > 1),
            )
            older = [alpha, way] + [multipliers] * (step > 1)
        near = to_near(near)
        image, *more = call(
            kernel(second_half, step), [field] + [field] * (step > 0), [], heavy,
            [table, wide, diag, off, parts, part, *older],
        )
        if more:
            (multipliers,) = more
        if step == 0:
            (jump_lift,) = call(
                kernel(build_lift), [((blocks, 2 * z.all_corners, width), BF16)],
                [other, pltpu.VMEM((blocks, z.all_corners, width), F32)], heavy,
                [table, lift, *arrived],
            )
        arrived = exchange(1, [image, own_extra], near)
        product, sent = call(
            kernel(finish_product, step), [field, ((devices, 1, LANES), F32)], [other], heavy,
            [table, operator, image, own_extra, jump_lift, residual, direction, near]
            + [alpha] * (step > 0) + arrived,
        )
        gathered = lax.all_to_all(sent, ("group", "sub"), 0, 0, tiled=True)
    multipliers, residual = call(
        kernel(finish), [(load.shape, F32)] * 2, [], light,
        [gathered, multipliers, residual, direction, product, alpha], False,
    )
    return multipliers, residual


def solution(mesh):
    return jax.shard_map(
        functools.partial(on_device, mesh=dict(mesh.shape)),
        mesh=mesh,
        in_specs=(
            P(None, ("group", "sub"), None),
            P(("group", "sub"), None),
            P(("group", "sub"), None, None),
            P(("group", "sub"), None, None),
            P(("group", "sub"), None),
            P(("group", "sub"), None),
            P(("group", "sub"), None),
            P("group", None),
            P("group", None),
        ),
        out_specs=(P(None, ("group", "sub"), None), P(None, ("group", "sub"), None)),
        check_vma=False,
    )
```

```python
import functools

import jax
import jax.numpy as jnp
from jax import lax
from jax.experimental import pallas as pl
from jax.experimental.pallas import tpu as pltpu
from jax.sharding import PartitionSpec as P

ITERS = 4
HIGH = lax.Precision.HIGHEST
F32 = jnp.float32
BF16 = jnp.bfloat16
VMEM = pl.BlockSpec(memory_space=pltpu.VMEM)
SMEM = pl.BlockSpec(memory_space=pltpu.SMEM)
HBM = pl.BlockSpec(memory_space=pltpu.HBM)
LIMIT = 24 * 1024 * 1024
LANES = 128
RR, DP, RP, PP = range(4)
NN = (((1,), (0,)), ((), ()))
NT = (((1,), (1,)), ((), ()))
TN = (((0,), (0,)), ((), ()))


def dot(a, b, dims):
    return lax.dot_general(a, b, dims, preferred_element_type=F32)


def dot_high(a, b, dims):
    return lax.dot_general(a, b, dims, precision=HIGH, preferred_element_type=F32)


def pad(a):
    return jnp.concatenate([a, jnp.zeros_like(a)], axis=0).astype(BF16)


def split(a):
    high = a.astype(BF16).astype(F32)
    return jnp.concatenate([high, a - high], axis=0).astype(BF16)


def fold(a):
    half = a.shape[0] // 2
    return a[:half] + a[half:]


def lane_ids(shape):
    return lax.broadcasted_iota(jnp.int32, shape, 1)


class Sizes:
    def __init__(self, load, corner_coupling, coarse_inverse, mesh):
        self.columns = load.shape[0]
        self.blocks = load.shape[1]
        self.width = load.shape[2]
        self.corners = corner_coupling.shape[0]
        assert self.corners == self.columns
        self.coarse = coarse_inverse.shape[1]
        self.peers = mesh["sub"]
        self.groups = mesh["group"]
        self.capacity = (self.blocks + self.peers - 2) // (self.peers - 1)
        self.all_corners = self.peers * self.corners
        self.extra_chunks = -(-self.all_corners // LANES)
        self.extra = self.extra_chunks * LANES
        self.halves = self.width // LANES
        evens = range(2, self.peers, 2)
        self.beyond = [m for m in evens if m & (m - 1)]
        self.beside = [m for m in evens if m & (m - 1) == 0]
        self.far = self.beyond + self.beside
        self.handed = [m + 1 for m in self.far]
        self.slots = self.peers * self.capacity
        self.inverse = self.slots
        self.pattern = self.inverse + self.blocks
        self.partner = self.pattern + self.blocks
        self.order = self.partner + self.blocks
        self.count = self.order + self.blocks + 1
        self.table = self.count + 1
        most = len(self.far) * self.capacity
        self.early = min(-(-most * 7 // 8), self.blocks)
        self.middle = max(self.early, min(most, self.blocks))

    def rows(self, kinds):
        return kinds * self.capacity * self.halves

    def near_rows(self, kinds):
        return len(self.handed) * self.rows(kinds)

    def at(self, k, core):
        return k

    def mine(self, k):
        core = lax.axis_index("sub") & 1
        at = [self.at(k, c) for c in range(2)]
        return tuple(
            jnp.where(core == 0, jnp.int32(a), jnp.int32(b))
            for a, b in [at, [self.far[n] for n in at]]
        )

    def sources(self):
        found = [(1, 0, 0)]
        for k in range(len(self.far)):
            _, m = self.mine(k)
            found += [(m + side, 1 + k, side) for side in range(2)]
        return found


def fill_table(z, partner, pattern, table, counts):
    me = lax.axis_index("sub")
    for entry in range(z.slots):
        table[entry] = z.blocks
    for m in range(z.peers):
        counts[m] = 0
    for i in range(z.blocks):
        mate = partner[0, i]
        source = pattern[0, i]
        m = mate ^ me
        rank = counts[m]
        table[m * z.capacity + rank] = i
        counts[m] = rank + 1
        table[z.inverse + source] = i
        table[z.pattern + i] = source
        table[z.partner + i] = mate
    place = jnp.int32(0)
    for m in z.handed + z.far + [1]:
        for r in range(z.capacity):
            block = table[m * z.capacity + r]
            table[z.order + place] = block
            place = place + (block < z.blocks).astype(jnp.int32)
        if m == z.handed[-1]:
            table[z.count] = place


def fill_piece(z, table, sources, m, piece, row):
    for source in sources:
        for r in range(z.capacity):
            value = source[jnp.minimum(table[m * z.capacity + r], z.blocks - 1)]
            for h in range(z.halves):
                piece[row] = value[:, h * LANES : (h + 1) * LANES]
                row += 1


def fill_near(z, table, sources, near):
    for k, m in enumerate(z.handed):
        fill_piece(z, table, sources, m, near, k * z.rows(len(sources)))


def store_extra(z, tile, piece, row):
    for j in range(z.extra_chunks):
        piece[row + j] = tile[:, j * LANES : (j + 1) * LANES]


def load_extra(z, piece, row):
    return jnp.concatenate([piece[row + j] for j in range(z.extra_chunks)], axis=1)


def relay(z, kinds, table, *rest):
    sources, rest = rest[:kinds], rest[kinds:]
    if kinds == 1:
        extra, rest = rest[0], rest[1:]
    near, pieces, beside = rest[0], rest[1:-1], rest[-1]
    rows = z.rows(kinds)
    fill_piece(z, table, sources, 1, beside, 0)
    if kinds == 1:
        tile = extra[...] + load_extra(z, near, z.near_rows(1))
    for k, piece in enumerate(pieces):
        which, m = z.mine(k)
        fill_piece(z, table, sources, m, piece, 0)
        for row in range(rows):
            piece[rows + row] = near[which * rows + row]
        if kinds == 1:
            store_extra(z, tile, piece, 2 * rows)


def place(z, table, arrived, kind, kinds, target):
    for m, transfer, piece in z.sources():
        row = piece * z.rows(kinds) + z.rows(kind)
        for r in range(z.capacity):
            block = table[m * z.capacity + r]
            for h in range(z.halves):
                target[block, :, h * LANES : (h + 1) * LANES] = arrived[transfer][row]
                row += 1


def begin(z, partner, pattern, load, scale, coupling, table, field, lift, wide, corners, near, *scratch):
    here, scale_here, coupling_here, partner_here, pattern_here, counts, sems = scratch
    copies = [
        pltpu.make_async_copy(a, b, sems.at[k])
        for k, (a, b) in enumerate(
            [
                (partner, partner_here),
                (pattern, pattern_here),
                (load, here),
                (scale, scale_here),
                (coupling, coupling_here),
            ]
        )
    ]
    for copy in copies:
        copy.start()
    copies[0].wait()
    copies[1].wait()
    fill_table(z, partner_here, pattern_here, table, counts)
    for copy in copies[2:]:
        copy.wait()
    for i in range(z.blocks):
        field[i] = here[:, i, :]
        row = jnp.broadcast_to(scale_here[i : i + 1, :], (z.columns, z.width))
        wide[i] = row
        part = coupling_here[:, i * z.width : (i + 1) * z.width].astype(F32)
        lift[i] = row * part
        corners[i] = jnp.concatenate([part, jnp.zeros_like(part)], axis=0).astype(BF16)
    fill_near(z, table, [field, lift], near)


def split3(a):
    high = a.astype(BF16).astype(F32)
    middle = (a - high).astype(BF16).astype(F32)
    return [high, middle, a - high - middle]


def prepare(z, index_in, inverse_in, diag, off, operator, diag_out, off_out, index, inverse, sems):
    copies = [
        pltpu.make_async_copy(a, b, sems.at[k])
        for k, (a, b) in enumerate(
            [(index_in, index), (inverse_in, inverse), (diag, diag_out), (off, off_out)]
        )
    ]
    for copy in copies:
        copy.start()
    copies[0].wait()
    copies[1].wait()
    rows = lax.broadcasted_iota(jnp.int32, (z.coarse, z.all_corners), 0)
    select = (rows == index[...]).astype(BF16)
    parts = jnp.concatenate(split3(inverse[...]), axis=0).astype(BF16)
    half = dot(parts, select, NN)
    half = sum(half[k * z.coarse : (k + 1) * z.coarse] for k in range(3))
    parts = jnp.concatenate(split3(half), axis=1).astype(BF16)
    full = dot(select, parts, TN)
    operator[...] = sum(full[:, k * z.all_corners : (k + 1) * z.all_corners] for k in range(3))
    copies[2].wait()
    copies[3].wait()


def build_lift(z, table, lift, *rest):
    count = 1 + len(z.far)
    arrived, (jump_lift, other, full) = rest[:count], rest[count:]
    place(z, table, [arrived[-1], *arrived[:-1]], 1, 2, other)
    me = lax.axis_index("sub")
    for i in range(z.blocks):
        full[i] = jnp.zeros((z.all_corners, z.width), F32)
        own = pl.multiple_of(me * z.corners, z.corners)
        theirs = pl.multiple_of(table[z.partner + i] * z.corners, z.corners)
        full[i, pl.ds(own, z.corners), :] = lift[i]
        full[i, pl.ds(theirs, z.corners), :] = -other[i]
        jump_lift[i] = split(full[i])


def extra_sum(z, own, near, *far):
    total = own[...] + load_extra(z, near, z.near_rows(1))
    for piece in far:
        total = total + load_extra(z, piece, 2 * z.rows(1))
    return total


def lane_sum(a):
    return jnp.sum(a, axis=1, keepdims=True)


def to_row(z, values):
    shape = (z.columns, LANES)
    lanes = lane_ids(shape)
    rows = lax.broadcasted_iota(jnp.int32, shape, 0)
    tile = jnp.zeros(shape, F32)
    for first, value in values:
        tile = jnp.where(lanes == first + rows, value, tile)
    return jnp.sum(tile, axis=0, keepdims=True)


def to_tile(z, row, first):
    shape = (z.columns, LANES)
    rows = lax.broadcasted_iota(jnp.int32, shape, 0)
    tile = jnp.where(lane_ids(shape) == first + rows, jnp.broadcast_to(row, shape), 0.0)
    return jnp.broadcast_to(lane_sum(tile), shape)


def scalars(z, gathered, previous):
    zero = jnp.zeros((1, LANES), F32)
    count = gathered.shape[0]
    unroll = 32 if count % 32 == 0 else 1
    total = lax.fori_loop(0, count, lambda k, acc: acc + gathered[k], zero, unroll=unroll)
    norm, way, rest = [to_tile(z, total, k * z.columns) for k in (RR, DP, RP)]
    alpha = norm / way
    if previous is None:
        placed = to_row(z, [(PP * z.columns, alpha)])

        def squares(k, acc):
            row = gathered[k]
            step = placed * pltpu.roll(row, LANES // 2, 1)
            return acc + row * step * step

        moved = lax.fori_loop(0, count, squares, zero, unroll=unroll)
        moved = to_tile(z, moved, PP * z.columns)
    else:
        ratio = alpha / used_step(previous)
        moved = to_tile(z, total, PP * z.columns) * ratio * ratio
    return alpha, (norm - 2.0 * alpha * rest + moved) / norm


def used_step(previous):
    return jnp.where(previous == 0.0, 1.0, previous)


def across_block(z, tile):
    return jnp.concatenate([tile] * z.halves, axis=1)


def couple(z, i, table, wide, diag, off, parts):
    source = table[z.inverse + i]
    mine = parts[i]
    coupled = dot(mine, diag[i], NT) + dot(mine, diag[i], NN)
    coupled = coupled + dot(parts[table[z.pattern + i]], off[i], NT)
    coupled = coupled + dot(parts[source], off[source], NN)
    return wide[i] * fold(coupled + mine.astype(F32))


def first_half(z, step, table, *rest):
    rest = list(rest)
    take = lambda n: [rest.pop(0) for _ in range(n)]
    wide, diag, off, corners = take(4)
    if step == 0:
        *far, beside, loaded = take(2 + len(z.far))
        residual, image, parts, extra, near_out, other = rest
        direction = residual
        place(z, table, [beside, *far], 0, 2, other)
    else:
        gathered, before, way, product = take(4)
        previous = take(1)[0][...] if step > 1 else None
        residual, direction, step_out, image, parts, extra, near_out = rest
        alpha, beta = scalars(z, gathered, previous)
        step_out[...] = alpha
        alpha, beta = across_block(z, alpha), across_block(z, beta)
    partial = jnp.zeros((2 * z.columns, 2 * z.corners), F32)
    for i in range(z.blocks):
        if step == 0:
            value = loaded[i] - other[i]
            residual[i] = value
        else:
            value = before[i] - alpha * product[i]
            residual[i] = value
            value = value + beta * way[i]
            direction[i] = value
        mine = pad(wide[i] * value)
        parts[i] = mine
        partial = partial + dot(mine, corners[i], NT)
    refs = (table, wide, diag, off, parts)
    for position in range(z.early):
        i = table[z.order + position]
        image[i] = couple(z, i, *refs)

    @pl.when(table[z.count] > z.early)
    def _():
        for position in range(z.early, z.middle):
            i = table[z.order + position]
            image[i] = couple(z, i, *refs)

    fill_near(z, table, [image], near_out)
    sums = fold(partial)
    padded = jnp.concatenate(
        [sums, jnp.zeros((z.columns, z.extra - sums.shape[1]), F32)], axis=1
    )
    tile = pltpu.roll(padded, lax.axis_index("sub") * z.corners, 1)
    extra[...] = tile
    store_extra(z, tile, near_out, z.near_rows(1))


def second_half(z, step, table, wide, diag, off, parts, image_in, *rest):
    if step == 0:
        (image,) = rest
    elif step == 1:
        alpha, way, image, multipliers = rest
    else:
        alpha, way, before, image, multipliers = rest
    refs = (table, wide, diag, off, parts)
    for i in range(z.blocks):
        image[i] = image_in[i]

    @pl.when(table[z.count] <= z.early)
    def _():
        for position in range(z.early, z.middle):
            i = table[z.order + position]
            image[i] = couple(z, i, *refs)

    for position in range(z.middle, z.blocks):
        i = table[z.order + position]
        image[i] = couple(z, i, *refs)
    if step > 0:
        size = across_block(z, alpha[...])
        for i in range(z.blocks):
            value = size * way[i]
            multipliers[i] = value if step == 1 else before[i] + value


def finish_product(z, step, table, operator, image, own_extra, jump_lift, residual, direction, near, *rest):
    *far, beside, product, sent, other = rest
    if step > 0:
        previous, far = far[0], far[1:]
        scale = across_block(z, used_step(previous[...]))
    place(z, table, [beside, *far], 0, 1, other)
    partials = extra_sum(z, own_extra, near, *far)[:, : z.all_corners]
    local = dot_high(partials, operator[...], NT)
    rows = pad(jnp.concatenate([local, local], axis=1))
    zero = jnp.zeros((z.columns, z.width), F32)
    sums = [zero] * (4 if step > 0 else 3)
    top = zero
    for i in range(z.blocks):
        value = image[i] - other[i] + fold(dot(rows, jump_lift[i], NN))
        product[i] = value
        r, d = residual[i], direction[i]
        pairs = [(r, r), (d, value), (r, value)]
        if step > 0:
            scaled = scale * value
            pairs.append((scaled, scaled))
        else:
            top = jnp.maximum(top, jnp.abs(value))
        sums = [s + a * b for s, (a, b) in zip(sums, pairs)]
    more = []
    if step == 0:
        top = jnp.max(top, axis=1, keepdims=True)
        shrink = jnp.where(top > 0.0, 1.0 / top, 0.0)
        squares = zero
        for i in range(z.blocks):
            value = product[i] * shrink
            squares = squares + value * value
        sums.append(squares)
        more.append((PP * z.columns + LANES // 2, top))
    row = to_row(z, [(k * z.columns, lane_sum(v)) for k, v in enumerate(sums)] + more)
    for k in range(sent.shape[0]):
        sent[k] = row


def finish(z, gathered, before, residual_in, direction, product, previous, multipliers, residual):
    alpha, _ = scalars(z, gathered, previous[...])
    for i in range(z.blocks):
        for h in range(z.halves):
            part = slice(h * LANES, (h + 1) * LANES)
            multipliers[:, i, part] = before[i, :, part] + alpha * direction[i, :, part]
            residual[:, i, part] = residual_in[i, :, part] - alpha * product[i, :, part]


def call(body, outs, scratch, cost, args, table=True, away=()):
    args = [
        pltpu.with_memory_space_constraint(a, pltpu.HBM) if k in away else a
        for k, a in enumerate(args)
    ]
    specs = [HBM if k in away else VMEM for k in range(len(args))]
    if table:
        specs[0] = SMEM
    shapes = [
        pltpu.SMEM(s, t) if t == jnp.int32 else jax.ShapeDtypeStruct(s, t) for s, t in outs
    ]
    return pl.pallas_call(
        body,
        out_shape=shapes,
        in_specs=specs,
        out_specs=[SMEM if t == jnp.int32 else VMEM for _, t in outs],
        scratch_shapes=scratch,
        compiler_params=pltpu.CompilerParams(vmem_limit_bytes=LIMIT),
        cost_estimate=pl.CostEstimate(flops=cost, bytes_accessed=cost // 16, transcendentals=0),
    )(*args)


def on_device(
    load,
    row_scale,
    diag_blocks,
    off_blocks,
    off_pattern,
    partner,
    corner_coupling,
    corner_index,
    coarse_inverse,
    *,
    mesh,
):
    z = Sizes(load, corner_coupling, coarse_inverse, mesh)
    cols, blocks, width = z.columns, z.blocks, z.width
    field = ((blocks, cols, width), F32)
    other = pltpu.VMEM((blocks + 1, cols, width), F32)
    extra = ((cols, z.extra), F32)
    light, heavy = 4_000_000, 600_000_000

    def shape(rows, kinds):
        return ((rows + (z.extra_chunks if kinds == 1 else 0), cols, LANES), F32)

    def kernel(body, *extra_args):
        return functools.partial(body, z, *extra_args)

    def across(piece, mask_of):
        pairs = [(t, t ^ mask_of(t & 1)) for t in range(z.peers)]
        return lax.ppermute(piece, "sub", pairs)

    def to_near(piece):
        return across(piece, lambda core: 1)

    def exchange(kinds, sources, near):
        *pieces, beside = call(
            kernel(relay, kinds),
            [shape(2 * z.rows(kinds), kinds)] * (len(z.far) + 1), [], light, [table, *sources, near],
        )
        far = [across(piece, lambda core: z.far[z.at(k, core)]) for k, piece in enumerate(pieces)]
        return [*far, to_near(beside)]

    table, loaded, lift, wide, corners, near = call(
        kernel(begin),
        [((z.table,), jnp.int32), field, field, field, ((blocks, 2 * z.corners, width), BF16)]
        + [shape(z.near_rows(2), 2)],
        [
            pltpu.VMEM(load.shape, F32),
            pltpu.VMEM(row_scale.shape, F32),
            pltpu.VMEM(corner_coupling.shape, BF16),
            pltpu.SMEM(partner.shape, jnp.int32),
            pltpu.SMEM(off_pattern.shape, jnp.int32),
            pltpu.SMEM((z.peers,), jnp.int32),
            pltpu.SemaphoreType.DMA((5,)),
        ],
        light,
        [partner, off_pattern, load, row_scale, corner_coupling],
        False, range(5),
    )
    arrived = exchange(2, [loaded, lift], to_near(near))
    weight = (diag_blocks.shape, BF16)
    operator, diag, off = call(
        kernel(prepare), [((z.all_corners, z.all_corners), F32), weight, weight],
        [
            pltpu.VMEM(corner_index.shape, jnp.int32),
            pltpu.VMEM(coarse_inverse.shape, F32),
            pltpu.SemaphoreType.DMA((4,)),
        ],
        heavy, [corner_index, coarse_inverse, diag_blocks, off_blocks], False, range(4),
    )
    half = ((blocks, 2 * cols, width), BF16)
    tile = ((cols, LANES), F32)
    devices = z.groups * z.peers
    fixed = [wide, diag, off, corners]
    multipliers = alpha = None
    for step in range(ITERS):
        early = [field, half, extra, shape(z.near_rows(1), 1)]
        if step == 0:
            residual, part, parts, own_extra, near = call(
                kernel(first_half, step), [field] + early, [other], heavy,
                [table, *fixed, *arrived, loaded],
            )
            direction = residual
            older = []
        else:
            way = direction
            residual, direction, alpha, part, parts, own_extra, near = call(
                kernel(first_half, step), [field, field, tile] + early, [], heavy,
                [table, *fixed, gathered, residual, way, product] + [alpha] * (step > 1),
            )
            older = [alpha, way] + [multipliers] * (step > 1)
        near = to_near(near)
        image, *more = call(
            kernel(second_half, step), [field] + [field] * (step > 0), [], heavy,
            [table, wide, diag, off, parts, part, *older],
        )
        if more:
            (multipliers,) = more
        if step == 0:
            (jump_lift,) = call(
                kernel(build_lift), [((blocks, 2 * z.all_corners, width), BF16)],
                [other, pltpu.VMEM((blocks, z.all_corners, width), F32)], heavy,
                [table, lift, *arrived],
            )
        arrived = exchange(1, [image, own_extra], near)
        product, sent = call(
            kernel(finish_product, step), [field, ((devices, 1, LANES), F32)], [other], heavy,
            [table, operator, image, own_extra, jump_lift, residual, direction, near]
            + [alpha] * (step > 0) + arrived,
        )
        gathered = lax.all_to_all(sent, ("group", "sub"), 0, 0, tiled=True)
    multipliers, residual = call(
        kernel(finish), [(load.shape, F32)] * 2, [], light,
        [gathered, multipliers, residual, direction, product, alpha], False,
    )
    return multipliers, residual


def solution(mesh):
    return jax.shard_map(
        functools.partial(on_device, mesh=dict(mesh.shape)),
        mesh=mesh,
        in_specs=(
            P(None, ("group", "sub"), None),
            P(("group", "sub"), None),
            P(("group", "sub"), None, None),
            P(("group", "sub"), None, None),
            P(("group", "sub"), None),
            P(("group", "sub"), None),
            P(("group", "sub"), None),
            P("group", None),
            P("group", None),
        ),
        out_specs=(P(None, ("group", "sub"), None), P(None, ("group", "sub"), None)),
        check_vma=False,
    )
```

```python
import functools

import jax
import jax.numpy as jnp
from jax import lax
from jax.experimental import pallas as pl
from jax.experimental.pallas import tpu as pltpu
from jax.sharding import PartitionSpec as P

ITERS = 4
HIGH = lax.Precision.HIGHEST
F32 = jnp.float32
BF16 = jnp.bfloat16
VMEM = pl.BlockSpec(memory_space=pltpu.VMEM)
SMEM = pl.BlockSpec(memory_space=pltpu.SMEM)
HBM = pl.BlockSpec(memory_space=pltpu.HBM)
LIMIT = 24 * 1024 * 1024
LANES = 128
RR, DP, RP, PP = range(4)
NN = (((1,), (0,)), ((), ()))
NT = (((1,), (1,)), ((), ()))
TN = (((0,), (0,)), ((), ()))


def dot(a, b, dims):
    return lax.dot_general(a, b, dims, preferred_element_type=F32)


def dot_high(a, b, dims):
    return lax.dot_general(a, b, dims, precision=HIGH, preferred_element_type=F32)


def pad(a):
    return jnp.concatenate([a, jnp.zeros_like(a)], axis=0).astype(BF16)


def split(a):
    high = a.astype(BF16).astype(F32)
    return jnp.concatenate([high, a - high], axis=0).astype(BF16)


def fold(a):
    half = a.shape[0] // 2
    return a[:half] + a[half:]


def lane_ids(shape):
    return lax.broadcasted_iota(jnp.int32, shape, 1)


class Sizes:
    def __init__(self, load, corner_coupling, coarse_inverse, mesh):
        self.columns = load.shape[0]
        self.blocks = load.shape[1]
        self.width = load.shape[2]
        self.corners = corner_coupling.shape[0]
        assert self.corners == self.columns
        self.coarse = coarse_inverse.shape[1]
        self.peers = mesh["sub"]
        self.groups = mesh["group"]
        self.capacity = (self.blocks + self.peers - 2) // (self.peers - 1)
        self.all_corners = self.peers * self.corners
        self.extra_chunks = -(-self.all_corners // LANES)
        self.extra = self.extra_chunks * LANES
        self.halves = self.width // LANES
        evens = range(2, self.peers, 2)
        self.beyond = [m for m in evens if m & (m - 1)]
        self.beside = [m for m in evens if m & (m - 1) == 0]
        self.far = self.beyond + self.beside
        self.handed = [m + 1 for m in self.far]
        self.slots = self.peers * self.capacity
        self.inverse = self.slots
        self.pattern = self.inverse + self.blocks
        self.partner = self.pattern + self.blocks
        self.order = self.partner + self.blocks
        self.count = self.order + self.blocks + 1
        self.table = self.count + 1
        most = len(self.far) * self.capacity
        self.early = min(-(-most * 7 // 8), self.blocks)
        self.middle = max(self.early, min(most, self.blocks))

    def rows(self, kinds):
        return kinds * self.capacity * self.halves

    def near_rows(self, kinds):
        return len(self.handed) * self.rows(kinds)

    def at(self, k, core):
        first = len(self.beyond)
        return k if k < first else first + (k - first + core) % len(self.beside)

    def mine(self, k):
        core = lax.axis_index("sub") & 1
        at = [self.at(k, c) for c in range(2)]
        return tuple(
            jnp.where(core == 0, jnp.int32(a), jnp.int32(b))
            for a, b in [at, [self.far[n] for n in at]]
        )

    def sources(self):
        found = [(1, 0, 0)]
        for k in range(len(self.far)):
            _, m = self.mine(k)
            found += [(m + side, 1 + k, side) for side in range(2)]
        return found


def fill_table(z, partner, pattern, table, counts):
    me = lax.axis_index("sub")
    for entry in range(z.slots):
        table[entry] = z.blocks
    for m in range(z.peers):
        counts[m] = 0
    for i in range(z.blocks):
        mate = partner[0, i]
        source = pattern[0, i]
        m = mate ^ me
        rank = counts[m]
        table[m * z.capacity + rank] = i
        counts[m] = rank + 1
        table[z.inverse + source] = i
        table[z.pattern + i] = source
        table[z.partner + i] = mate
    place = jnp.int32(0)
    for m in z.handed + z.far + [1]:
        for r in range(z.capacity):
            block = table[m * z.capacity + r]
            table[z.order + place] = block
            place = place + (block < z.blocks).astype(jnp.int32)
        if m == z.handed[-1]:
            table[z.count] = place


def fill_piece(z, table, sources, m, piece, row):
    for source in sources:
        for r in range(z.capacity):
            value = source[jnp.minimum(table[m * z.capacity + r], z.blocks - 1)]
            for h in range(z.halves):
                piece[row] = value[:, h * LANES : (h + 1) * LANES]
                row += 1


def fill_near(z, table, sources, near):
    for k, m in enumerate(z.handed):
        fill_piece(z, table, sources, m, near, k * z.rows(len(sources)))


def store_extra(z, tile, piece, row):
    for j in range(z.extra_chunks):
        piece[row + j] = tile[:, j * LANES : (j + 1) * LANES]


def load_extra(z, piece, row):
    return jnp.concatenate([piece[row + j] for j in range(z.extra_chunks)], axis=1)


def relay(z, kinds, table, *rest):
    sources, rest = rest[:kinds], rest[kinds:]
    if kinds == 1:
        extra, rest = rest[0], rest[1:]
    near, pieces, beside = rest[0], rest[1:-1], rest[-1]
    rows = z.rows(kinds)
    fill_piece(z, table, sources, 1, beside, 0)
    if kinds == 1:
        tile = extra[...] + load_extra(z, near, z.near_rows(1))
    for k, piece in enumerate(pieces):
        which, m = z.mine(k)
        fill_piece(z, table, sources, m, piece, 0)
        for row in range(rows):
            piece[rows + row] = near[which * rows + row]
        if kinds == 1:
            store_extra(z, tile, piece, 2 * rows)


def place(z, table, arrived, kind, kinds, target):
    for m, transfer, piece in z.sources():
        row = piece * z.rows(kinds) + z.rows(kind)
        for r in range(z.capacity):
            block = table[m * z.capacity + r]
            for h in range(z.halves):
                target[block, :, h * LANES : (h + 1) * LANES] = arrived[transfer][row]
                row += 1


def begin(z, partner, pattern, load, scale, coupling, table, field, lift, wide, corners, near, *scratch):
    here, scale_here, coupling_here, partner_here, pattern_here, counts, sems = scratch
    copies = [
        pltpu.make_async_copy(a, b, sems.at[k])
        for k, (a, b) in enumerate(
            [
                (partner, partner_here),
                (pattern, pattern_here),
                (load, here),
                (scale, scale_here),
                (coupling, coupling_here),
            ]
        )
    ]
    for copy in copies:
        copy.start()
    copies[0].wait()
    copies[1].wait()
    fill_table(z, partner_here, pattern_here, table, counts)
    for copy in copies[2:]:
        copy.wait()
    for i in range(z.blocks):
        field[i] = here[:, i, :]
        row = jnp.broadcast_to(scale_here[i : i + 1, :], (z.columns, z.width))
        wide[i] = row
        part = coupling_here[:, i * z.width : (i + 1) * z.width].astype(F32)
        lift[i] = row * part
        corners[i] = jnp.concatenate([part, jnp.zeros_like(part)], axis=0).astype(BF16)
    fill_near(z, table, [field, lift], near)


def split3(a):
    high = a.astype(BF16).astype(F32)
    middle = (a - high).astype(BF16).astype(F32)
    return [high, middle, a - high - middle]


def prepare(z, index_in, inverse_in, diag, off, operator, diag_out, off_out, index, inverse, sems):
    copies = [
        pltpu.make_async_copy(a, b, sems.at[k])
        for k, (a, b) in enumerate(
            [(index_in, index), (inverse_in, inverse), (diag, diag_out), (off, off_out)]
        )
    ]
    for copy in copies:
        copy.start()
    copies[0].wait()
    copies[1].wait()
    rows = lax.broadcasted_iota(jnp.int32, (z.coarse, z.all_corners), 0)
    select = (rows == index[...]).astype(BF16)
    half = sum(dot(part.astype(BF16), select, TN) for part in split3(inverse[...]))
    parts = jnp.concatenate(split3(half), axis=1).astype(BF16)
    full = dot(select, parts, TN)
    operator[...] = sum(full[:, k * z.all_corners : (k + 1) * z.all_corners] for k in range(3))
    copies[2].wait()
    copies[3].wait()


def build_lift(z, table, lift, *rest):
    count = 1 + len(z.far)
    arrived, (jump_lift, other, full) = rest[:count], rest[count:]
    place(z, table, [arrived[-1], *arrived[:-1]], 1, 2, other)
    me = lax.axis_index("sub")
    for i in range(z.blocks):
        full[i] = jnp.zeros((z.all_corners, z.width), F32)
        own = pl.multiple_of(me * z.corners, z.corners)
        theirs = pl.multiple_of(table[z.partner + i] * z.corners, z.corners)
        full[i, pl.ds(own, z.corners), :] = lift[i]
        full[i, pl.ds(theirs, z.corners), :] = -other[i]
        jump_lift[i] = split(full[i])


def extra_sum(z, own, near, *far):
    total = own[...] + load_extra(z, near, z.near_rows(1))
    for piece in far:
        total = total + load_extra(z, piece, 2 * z.rows(1))
    return total


def lane_sum(a):
    return jnp.sum(a, axis=1, keepdims=True)


def to_row(z, values):
    shape = (z.columns, LANES)
    lanes = lane_ids(shape)
    rows = lax.broadcasted_iota(jnp.int32, shape, 0)
    tile = jnp.zeros(shape, F32)
    for first, value in values:
        tile = jnp.where(lanes == first + rows, value, tile)
    return jnp.sum(tile, axis=0, keepdims=True)


def to_tile(z, row, first):
    shape = (z.columns, LANES)
    rows = lax.broadcasted_iota(jnp.int32, shape, 0)
    tile = jnp.where(lane_ids(shape) == first + rows, jnp.broadcast_to(row, shape), 0.0)
    return jnp.broadcast_to(lane_sum(tile), shape)


def scalars(z, gathered, previous):
    zero = jnp.zeros((1, LANES), F32)
    count = gathered.shape[0]
    unroll = 32 if count % 32 == 0 else 1
    total = lax.fori_loop(0, count, lambda k, acc: acc + gathered[k], zero, unroll=unroll)
    norm, way, rest = [to_tile(z, total, k * z.columns) for k in (RR, DP, RP)]
    alpha = norm / way
    turn = 1.0 / norm
    if previous is None:
        placed = to_row(z, [(PP * z.columns, alpha)])

        def squares(k, acc):
            row = gathered[k]
            step = placed * pltpu.roll(row, LANES // 2, 1)
            return acc + row * step * step

        moved = lax.fori_loop(0, count, squares, zero, unroll=unroll)
        moved = to_tile(z, moved, PP * z.columns)
    else:
        ratio = alpha / used_step(previous)
        moved = to_tile(z, total, PP * z.columns) * ratio * ratio
    return alpha, (norm - 2.0 * alpha * rest + moved) * turn


def used_step(previous):
    return jnp.where(previous == 0.0, 1.0, previous)


def across_block(z, tile):
    return jnp.concatenate([tile] * z.halves, axis=1)


def couple(z, i, table, wide, diag, off, parts):
    source = table[z.inverse + i]
    mine = parts[i]
    coupled = dot(mine, diag[i], NT) + dot(mine, diag[i], NN)
    coupled = coupled + dot(parts[table[z.pattern + i]], off[i], NT)
    coupled = coupled + dot(parts[source], off[source], NN)
    return wide[i] * fold(coupled + mine.astype(F32))


def first_half(z, step, table, *rest):
    rest = list(rest)
    take = lambda n: [rest.pop(0) for _ in range(n)]
    wide, diag, off, corners = take(4)
    if step == 0:
        *far, beside, loaded = take(2 + len(z.far))
        residual, image, parts, extra, near_out, other = rest
        direction = residual
        place(z, table, [beside, *far], 0, 2, other)
    else:
        gathered, before, way, product = take(4)
        previous = take(1)[0][...] if step > 1 else None
        residual, direction, step_out, image, parts, extra, near_out = rest
        alpha, beta = scalars(z, gathered, previous)
        step_out[...] = alpha
        alpha, beta = across_block(z, alpha), across_block(z, beta)
    partial = jnp.zeros((2 * z.columns, 2 * z.corners), F32)
    for i in range(z.blocks):
        if step == 0:
            value = loaded[i] - other[i]
            residual[i] = value
        else:
            value = before[i] - alpha * product[i]
            residual[i] = value
            value = value + beta * way[i]
            direction[i] = value
        mine = pad(wide[i] * value)
        parts[i] = mine
        partial = partial + dot(mine, corners[i], NT)
    refs = (table, wide, diag, off, parts)
    for position in range(z.early):
        i = table[z.order + position]
        image[i] = couple(z, i, *refs)

    @pl.when(table[z.count] > z.early)
    def _():
        for position in range(z.early, z.middle):
            i = table[z.order + position]
            image[i] = couple(z, i, *refs)

    fill_near(z, table, [image], near_out)
    sums = fold(partial)
    padded = jnp.concatenate(
        [sums, jnp.zeros((z.columns, z.extra - sums.shape[1]), F32)], axis=1
    )
    tile = pltpu.roll(padded, lax.axis_index("sub") * z.corners, 1)
    extra[...] = tile
    store_extra(z, tile, near_out, z.near_rows(1))


def second_half(z, step, table, wide, diag, off, parts, image_in, *rest):
    if step == 0:
        (image,) = rest
    elif step == 1:
        alpha, way, image, multipliers = rest
    else:
        alpha, way, before, image, multipliers = rest
    refs = (table, wide, diag, off, parts)
    for i in range(z.blocks):
        image[i] = image_in[i]

    @pl.when(table[z.count] <= z.early)
    def _():
        for position in range(z.early, z.middle):
            i = table[z.order + position]
            image[i] = couple(z, i, *refs)

    for position in range(z.middle, z.blocks):
        i = table[z.order + position]
        image[i] = couple(z, i, *refs)
    if step > 0:
        size = across_block(z, alpha[...])
        for i in range(z.blocks):
            value = size * way[i]
            multipliers[i] = value if step == 1 else before[i] + value


def finish_product(z, step, table, operator, image, own_extra, jump_lift, residual, direction, near, *rest):
    *far, beside, product, sent, other = rest
    if step > 0:
        previous, far = far[0], far[1:]
        scale = across_block(z, used_step(previous[...]))
    place(z, table, [beside, *far], 0, 1, other)
    partials = extra_sum(z, own_extra, near, *far)[:, : z.all_corners]
    local = dot_high(partials, operator[...], NN)
    rows = pad(jnp.concatenate([local, local], axis=1))
    zero = jnp.zeros((z.columns, z.width), F32)
    sums = [zero] * (4 if step > 0 else 3)
    top = zero
    for i in range(z.blocks):
        value = image[i] - other[i] + fold(dot(rows, jump_lift[i], NN))
        product[i] = value
        r, d = residual[i], direction[i]
        pairs = [(r, r), (d, value), (r, value)]
        if step > 0:
            scaled = scale * value
            pairs.append((scaled, scaled))
        else:
            top = jnp.maximum(top, jnp.abs(value))
        sums = [s + a * b for s, (a, b) in zip(sums, pairs)]
    more = []
    if step == 0:
        top = jnp.max(top, axis=1, keepdims=True)
        shrink = jnp.where(top > 0.0, 1.0 / top, 0.0)
        squares = zero
        for i in range(z.blocks):
            value = product[i] * shrink
            squares = squares + value * value
        sums.append(squares)
        more.append((PP * z.columns + LANES // 2, top))
    row = to_row(z, [(k * z.columns, lane_sum(v)) for k, v in enumerate(sums)] + more)
    for k in range(sent.shape[0]):
        sent[k] = row


def finish(z, gathered, before, residual_in, direction, product, previous, multipliers, residual):
    alpha, _ = scalars(z, gathered, previous[...])
    for i in range(z.blocks):
        for h in range(z.halves):
            part = slice(h * LANES, (h + 1) * LANES)
            multipliers[:, i, part] = before[i, :, part] + alpha * direction[i, :, part]
            residual[:, i, part] = residual_in[i, :, part] - alpha * product[i, :, part]


def call(body, outs, scratch, cost, args, table=True, away=()):
    args = [
        pltpu.with_memory_space_constraint(a, pltpu.HBM) if k in away else a
        for k, a in enumerate(args)
    ]
    specs = [HBM if k in away else VMEM for k in range(len(args))]
    if table:
        specs[0] = SMEM
    shapes = [
        pltpu.SMEM(s, t) if t == jnp.int32 else jax.ShapeDtypeStruct(s, t) for s, t in outs
    ]
    return pl.pallas_call(
        body,
        out_shape=shapes,
        in_specs=specs,
        out_specs=[SMEM if t == jnp.int32 else VMEM for _, t in outs],
        scratch_shapes=scratch,
        compiler_params=pltpu.CompilerParams(vmem_limit_bytes=LIMIT),
        cost_estimate=pl.CostEstimate(flops=cost, bytes_accessed=cost // 16, transcendentals=0),
    )(*args)


def on_device(
    load,
    row_scale,
    diag_blocks,
    off_blocks,
    off_pattern,
    partner,
    corner_coupling,
    corner_index,
    coarse_inverse,
    *,
    mesh,
):
    z = Sizes(load, corner_coupling, coarse_inverse, mesh)
    cols, blocks, width = z.columns, z.blocks, z.width
    field = ((blocks, cols, width), F32)
    other = pltpu.VMEM((blocks + 1, cols, width), F32)
    extra = ((cols, z.extra), F32)
    light, heavy = 4_000_000, 600_000_000

    def shape(rows, kinds):
        return ((rows + (z.extra_chunks if kinds == 1 else 0), cols, LANES), F32)

    def kernel(body, *extra_args):
        return functools.partial(body, z, *extra_args)

    def across(piece, mask_of):
        pairs = [(t, t ^ mask_of(t & 1)) for t in range(z.peers)]
        return lax.ppermute(piece, "sub", pairs)

    def to_near(piece):
        return across(piece, lambda core: 1)

    def exchange(kinds, sources, near):
        *pieces, beside = call(
            kernel(relay, kinds),
            [shape(2 * z.rows(kinds), kinds)] * (len(z.far) + 1), [], light, [table, *sources, near],
        )
        far = [across(piece, lambda core: z.far[z.at(k, core)]) for k, piece in enumerate(pieces)]
        return [*far, to_near(beside)]

    table, loaded, lift, wide, corners, near = call(
        kernel(begin),
        [((z.table,), jnp.int32), field, field, field, ((blocks, 2 * z.corners, width), BF16)]
        + [shape(z.near_rows(2), 2)],
        [
            pltpu.VMEM(load.shape, F32),
            pltpu.VMEM(row_scale.shape, F32),
            pltpu.VMEM(corner_coupling.shape, BF16),
            pltpu.SMEM(partner.shape, jnp.int32),
            pltpu.SMEM(off_pattern.shape, jnp.int32),
            pltpu.SMEM((z.peers,), jnp.int32),
            pltpu.SemaphoreType.DMA((5,)),
        ],
        light,
        [partner, off_pattern, load, row_scale, corner_coupling],
        False, range(5),
    )
    arrived = exchange(2, [loaded, lift], to_near(near))
    weight = (diag_blocks.shape, BF16)
    operator, diag, off = call(
        kernel(prepare), [((z.all_corners, z.all_corners), F32), weight, weight],
        [
            pltpu.VMEM(corner_index.shape, jnp.int32),
            pltpu.VMEM(coarse_inverse.shape, F32),
            pltpu.SemaphoreType.DMA((4,)),
        ],
        heavy, [corner_index, coarse_inverse, diag_blocks, off_blocks], False, range(4),
    )
    half = ((blocks, 2 * cols, width), BF16)
    tile = ((cols, LANES), F32)
    devices = z.groups * z.peers
    fixed = [wide, diag, off, corners]
    multipliers = alpha = None
    for step in range(ITERS):
        early = [field, half, extra, shape(z.near_rows(1), 1)]
        if step == 0:
            residual, part, parts, own_extra, near = call(
                kernel(first_half, step), [field] + early, [other], heavy,
                [table, *fixed, *arrived, loaded],
            )
            direction = residual
            older = []
        else:
            way = direction
            residual, direction, alpha, part, parts, own_extra, near = call(
                kernel(first_half, step), [field, field, tile] + early, [], heavy,
                [table, *fixed, gathered, residual, way, product] + [alpha] * (step > 1),
            )
            older = [alpha, way] + [multipliers] * (step > 1)
        near = to_near(near)
        image, *more = call(
            kernel(second_half, step), [field] + [field] * (step > 0), [], heavy,
            [table, wide, diag, off, parts, part, *older],
        )
        if more:
            (multipliers,) = more
        if step == 0:
            (jump_lift,) = call(
                kernel(build_lift), [((blocks, 2 * z.all_corners, width), BF16)],
                [other, pltpu.VMEM((blocks, z.all_corners, width), F32)], heavy,
                [table, lift, *arrived],
            )
        arrived = exchange(1, [image, own_extra], near)
        product, sent = call(
            kernel(finish_product, step), [field, ((devices, 1, LANES), F32)], [other], heavy,
            [table, operator, image, own_extra, jump_lift, residual, direction, near]
            + [alpha] * (step > 0) + arrived,
        )
        gathered = lax.all_to_all(sent, ("group", "sub"), 0, 0, tiled=True)
    multipliers, residual = call(
        kernel(finish), [(load.shape, F32)] * 2, [], light,
        [gathered, multipliers, residual, direction, product, alpha], False,
    )
    return multipliers, residual


def solution(mesh):
    return jax.shard_map(
        functools.partial(on_device, mesh=dict(mesh.shape)),
        mesh=mesh,
        in_specs=(
            P(None, ("group", "sub"), None),
            P(("group", "sub"), None),
            P(("group", "sub"), None, None),
            P(("group", "sub"), None, None),
            P(("group", "sub"), None),
            P(("group", "sub"), None),
            P(("group", "sub"), None),
            P("group", None),
            P("group", None),
        ),
        out_specs=(P(None, ("group", "sub"), None), P(None, ("group", "sub"), None)),
        check_vma=False,
    )
```

```python
import functools

import jax
import jax.numpy as jnp
from jax import lax
from jax.experimental import pallas as pl
from jax.experimental.pallas import tpu as pltpu
from jax.sharding import PartitionSpec as P

ITERS = 4
HIGH = lax.Precision.HIGHEST
F32 = jnp.float32
BF16 = jnp.bfloat16
VMEM = pl.BlockSpec(memory_space=pltpu.VMEM)
SMEM = pl.BlockSpec(memory_space=pltpu.SMEM)
HBM = pl.BlockSpec(memory_space=pltpu.HBM)
LIMIT = 24 * 1024 * 1024
LANES = 128
RR, DP, RP, PP = range(4)
NN = (((1,), (0,)), ((), ()))
NT = (((1,), (1,)), ((), ()))
TN = (((0,), (0,)), ((), ()))


def dot(a, b, dims):
    return lax.dot_general(a, b, dims, preferred_element_type=F32)


def dot_high(a, b, dims):
    return lax.dot_general(a, b, dims, precision=HIGH, preferred_element_type=F32)


def pad(a):
    return jnp.concatenate([a, jnp.zeros_like(a)], axis=0).astype(BF16)


def split(a):
    high = a.astype(BF16).astype(F32)
    return jnp.concatenate([high, a - high], axis=0).astype(BF16)


def fold(a):
    half = a.shape[0] // 2
    return a[:half] + a[half:]


def lane_ids(shape):
    return lax.broadcasted_iota(jnp.int32, shape, 1)


class Sizes:
    def __init__(self, load, corner_coupling, coarse_inverse, mesh):
        self.columns = load.shape[0]
        self.blocks = load.shape[1]
        self.width = load.shape[2]
        self.corners = corner_coupling.shape[0]
        assert self.corners == self.columns
        self.coarse = coarse_inverse.shape[1]
        self.peers = mesh["sub"]
        self.groups = mesh["group"]
        self.capacity = (self.blocks + self.peers - 2) // (self.peers - 1)
        self.all_corners = self.peers * self.corners
        self.extra_chunks = -(-self.all_corners // LANES)
        self.extra = self.extra_chunks * LANES
        self.halves = self.width // LANES
        evens = range(2, self.peers, 2)
        self.beyond = [m for m in evens if m & (m - 1)]
        self.beside = [m for m in evens if m & (m - 1) == 0]
        self.far = self.beyond + self.beside
        self.handed = [m + 1 for m in self.far]
        self.slots = self.peers * self.capacity
        self.inverse = self.slots
        self.pattern = self.inverse + self.blocks
        self.partner = self.pattern + self.blocks
        self.order = self.partner + self.blocks
        self.count = self.order + self.blocks + 1
        self.table = self.count + 1
        most = len(self.far) * self.capacity
        self.early = min(-(-most * 7 // 8), self.blocks)
        self.middle = max(self.early, min(most, self.blocks))

    def rows(self, kinds):
        return kinds * self.capacity * self.halves

    def near_rows(self, kinds):
        return len(self.handed) * self.rows(kinds)

    def at(self, k, core):
        first = len(self.beyond)
        return k if k < first else first + (k - first + core) % len(self.beside)

    def mine(self, k):
        core = lax.axis_index("sub") & 1
        at = [self.at(k, c) for c in range(2)]
        return tuple(
            jnp.where(core == 0, jnp.int32(a), jnp.int32(b))
            for a, b in [at, [self.far[n] for n in at]]
        )

    def sources(self):
        found = [(1, 0, 0)]
        for k in range(len(self.far)):
            _, m = self.mine(k)
            found += [(m + side, 1 + k, side) for side in range(2)]
        return found


def fill_table(z, partner, pattern, table, counts):
    me = lax.axis_index("sub")
    for entry in range(z.slots):
        table[entry] = z.blocks
    for m in range(z.peers):
        counts[m] = 0
    for i in range(z.blocks):
        mate = partner[0, i]
        source = pattern[0, i]
        m = mate ^ me
        rank = counts[m]
        table[m * z.capacity + rank] = i
        counts[m] = rank + 1
        table[z.inverse + source] = i
        table[z.pattern + i] = source
        table[z.partner + i] = mate
    place = jnp.int32(0)
    for m in z.handed + z.far + [1]:
        for r in range(z.capacity):
            block = table[m * z.capacity + r]
            table[z.order + place] = block
            place = place + (block < z.blocks).astype(jnp.int32)
        if m == z.handed[-1]:
            table[z.count] = place


def fill_piece(z, table, sources, m, piece, row):
    for source in sources:
        for r in range(z.capacity):
            value = source[jnp.minimum(table[m * z.capacity + r], z.blocks - 1)]
            for h in range(z.halves):
                piece[row] = value[:, h * LANES : (h + 1) * LANES]
                row += 1


def fill_near(z, table, sources, near):
    for k, m in enumerate(z.handed):
        fill_piece(z, table, sources, m, near, k * z.rows(len(sources)))


def store_extra(z, tile, piece, row):
    for j in range(z.extra_chunks):
        piece[row + j] = tile[:, j * LANES : (j + 1) * LANES]


def load_extra(z, piece, row):
    return jnp.concatenate([piece[row + j] for j in range(z.extra_chunks)], axis=1)


def relay(z, kinds, table, *rest):
    sources, rest = rest[:kinds], rest[kinds:]
    if kinds == 1:
        extra, rest = rest[0], rest[1:]
    near, pieces, beside = rest[0], rest[1:-1], rest[-1]
    rows = z.rows(kinds)
    fill_piece(z, table, sources, 1, beside, 0)
    if kinds == 1:
        tile = extra[...] + load_extra(z, near, z.near_rows(1))
    for k, piece in enumerate(pieces):
        which, m = z.mine(k)
        fill_piece(z, table, sources, m, piece, 0)
        for row in range(rows):
            piece[rows + row] = near[which * rows + row]
        if kinds == 1:
            store_extra(z, tile, piece, 2 * rows)


def place(z, table, arrived, kind, kinds, target):
    for m, transfer, piece in z.sources():
        row = piece * z.rows(kinds) + z.rows(kind)
        for r in range(z.capacity):
            block = table[m * z.capacity + r]
            for h in range(z.halves):
                target[block, :, h * LANES : (h + 1) * LANES] = arrived[transfer][row]
                row += 1


def begin(z, partner, pattern, load, scale, coupling, table, field, lift, wide, corners, near, *scratch):
    here, scale_here, coupling_here, partner_here, pattern_here, counts, sems = scratch
    copies = [
        pltpu.make_async_copy(a, b, sems.at[k])
        for k, (a, b) in enumerate(
            [
                (partner, partner_here),
                (pattern, pattern_here),
                (load, here),
                (scale, scale_here),
                (coupling, coupling_here),
            ]
        )
    ]
    for copy in copies:
        copy.start()
    copies[0].wait()
    copies[1].wait()
    fill_table(z, partner_here, pattern_here, table, counts)
    for copy in copies[2:]:
        copy.wait()
    for i in range(z.blocks):
        field[i] = here[:, i, :]
        row = jnp.broadcast_to(scale_here[i : i + 1, :], (z.columns, z.width))
        wide[i] = row
        part = coupling_here[:, i * z.width : (i + 1) * z.width].astype(F32)
        lift[i] = row * part
        corners[:, i * z.width : (i + 1) * z.width] = pad(part)
    fill_near(z, table, [field, lift], near)


def split3(a):
    high = a.astype(BF16).astype(F32)
    middle = (a - high).astype(BF16).astype(F32)
    return [high, middle, a - high - middle]


def prepare(z, index_in, inverse_in, diag, off, operator, diag_out, off_out, index, inverse, sems):
    copies = [
        pltpu.make_async_copy(a, b, sems.at[k])
        for k, (a, b) in enumerate(
            [(index_in, index), (inverse_in, inverse), (diag, diag_out), (off, off_out)]
        )
    ]
    for copy in copies:
        copy.start()
    copies[0].wait()
    copies[1].wait()
    rows = lax.broadcasted_iota(jnp.int32, (z.coarse, z.all_corners), 0)
    select = (rows == index[...]).astype(BF16)
    half = sum(dot(part.astype(BF16), select, TN) for part in split3(inverse[...]))
    parts = jnp.concatenate(split3(half), axis=1).astype(BF16)
    full = dot(select, parts, TN)
    operator[...] = sum(full[:, k * z.all_corners : (k + 1) * z.all_corners] for k in range(3))
    copies[2].wait()
    copies[3].wait()


def build_lift(z, table, lift, *rest):
    count = 1 + len(z.far)
    arrived, (jump_lift, other, full) = rest[:count], rest[count:]
    place(z, table, [arrived[-1], *arrived[:-1]], 1, 2, other)
    me = lax.axis_index("sub")
    for i in range(z.blocks):
        full[i] = jnp.zeros((z.all_corners, z.width), F32)
        own = pl.multiple_of(me * z.corners, z.corners)
        theirs = pl.multiple_of(table[z.partner + i] * z.corners, z.corners)
        full[i, pl.ds(own, z.corners), :] = lift[i]
        full[i, pl.ds(theirs, z.corners), :] = -other[i]
        jump_lift[i] = split(full[i])


def extra_sum(z, own, near, *far):
    total = own[...] + load_extra(z, near, z.near_rows(1))
    for piece in far:
        total = total + load_extra(z, piece, 2 * z.rows(1))
    return total


def lane_sum(a):
    return jnp.sum(a, axis=1, keepdims=True)


def to_row(z, values):
    shape = (z.columns, LANES)
    lanes = lane_ids(shape)
    rows = lax.broadcasted_iota(jnp.int32, shape, 0)
    tile = jnp.zeros(shape, F32)
    for first, value in values:
        tile = jnp.where(lanes == first + rows, value, tile)
    return jnp.sum(tile, axis=0, keepdims=True)


def to_tile(z, row, first):
    shape = (z.columns, LANES)
    rows = lax.broadcasted_iota(jnp.int32, shape, 0)
    tile = jnp.where(lane_ids(shape) == first + rows, jnp.broadcast_to(row, shape), 0.0)
    return jnp.broadcast_to(lane_sum(tile), shape)


def scalars(z, gathered, previous):
    zero = jnp.zeros((1, LANES), F32)
    count = gathered.shape[0]
    unroll = 32 if count % 32 == 0 else 1
    total = lax.fori_loop(0, count, lambda k, acc: acc + gathered[k], zero, unroll=unroll)
    norm, way, rest = [to_tile(z, total, k * z.columns) for k in (RR, DP, RP)]
    alpha = norm / way
    turn = 1.0 / norm
    if previous is None:
        placed = to_row(z, [(PP * z.columns, alpha)])

        def squares(k, acc):
            row = gathered[k]
            step = placed * pltpu.roll(row, LANES // 2, 1)
            return acc + row * step * step

        moved = lax.fori_loop(0, count, squares, zero, unroll=unroll)
        moved = to_tile(z, moved, PP * z.columns)
    else:
        ratio = alpha / used_step(previous)
        moved = to_tile(z, total, PP * z.columns) * ratio * ratio
    return alpha, (norm - 2.0 * alpha * rest + moved) * turn


def used_step(previous):
    return jnp.where(previous == 0.0, 1.0, previous)


def across_block(z, tile):
    return jnp.concatenate([tile] * z.halves, axis=1)


def couple(z, i, table, wide, diag, off, parts):
    source = table[z.inverse + i]
    mine = parts[i]
    coupled = dot(mine, diag[i], NT) + dot(mine, diag[i], NN)
    coupled = coupled + dot(parts[table[z.pattern + i]], off[i], NT)
    coupled = coupled + dot(parts[source], off[source], NN)
    return wide[i] * fold(coupled + mine.astype(F32))


def first_half(z, step, table, *rest):
    rest = list(rest)
    take = lambda n: [rest.pop(0) for _ in range(n)]
    wide, diag, off, corners = take(4)
    if step == 0:
        *far, beside, loaded = take(2 + len(z.far))
        residual, image, parts, extra, near_out, other = rest
        direction = residual
        place(z, table, [beside, *far], 0, 2, other)
    else:
        gathered, before, way, product = take(4)
        previous = take(1)[0][...] if step > 1 else None
        residual, direction, step_out, image, parts, extra, near_out = rest
        alpha, beta = scalars(z, gathered, previous)
        step_out[...] = alpha
        alpha, beta = across_block(z, alpha), across_block(z, beta)
    pieces = []
    for i in range(z.blocks):
        if step == 0:
            value = loaded[i] - other[i]
            residual[i] = value
        else:
            value = before[i] - alpha * product[i]
            residual[i] = value
            value = value + beta * way[i]
            direction[i] = value
        mine = pad(wide[i] * value)
        parts[i] = mine
        pieces.append(mine)
    partial = dot(jnp.concatenate(pieces, axis=1), corners[...], NT)
    refs = (table, wide, diag, off, parts)
    for position in range(z.early):
        i = table[z.order + position]
        image[i] = couple(z, i, *refs)

    @pl.when(table[z.count] > z.early)
    def _():
        for position in range(z.early, z.middle):
            i = table[z.order + position]
            image[i] = couple(z, i, *refs)

    fill_near(z, table, [image], near_out)
    sums = fold(partial)
    padded = jnp.concatenate(
        [sums, jnp.zeros((z.columns, z.extra - sums.shape[1]), F32)], axis=1
    )
    tile = pltpu.roll(padded, lax.axis_index("sub") * z.corners, 1)
    extra[...] = tile
    store_extra(z, tile, near_out, z.near_rows(1))


def second_half(z, step, table, wide, diag, off, parts, image_in, *rest):
    if step == 0:
        (image,) = rest
    elif step == 1:
        alpha, way, image, multipliers = rest
    else:
        alpha, way, before, image, multipliers = rest
    refs = (table, wide, diag, off, parts)
    for i in range(z.blocks):
        image[i] = image_in[i]

    @pl.when(table[z.count] <= z.early)
    def _():
        for position in range(z.early, z.middle):
            i = table[z.order + position]
            image[i] = couple(z, i, *refs)

    for position in range(z.middle, z.blocks):
        i = table[z.order + position]
        image[i] = couple(z, i, *refs)
    if step > 0:
        size = across_block(z, alpha[...])
        for i in range(z.blocks):
            value = size * way[i]
            multipliers[i] = value if step == 1 else before[i] + value


def finish_product(z, step, table, operator, image, own_extra, jump_lift, residual, direction, near, *rest):
    *far, beside, product, sent, other = rest
    if step > 0:
        previous, far = far[0], far[1:]
        scale = across_block(z, used_step(previous[...]))
    place(z, table, [beside, *far], 0, 1, other)
    partials = extra_sum(z, own_extra, near, *far)[:, : z.all_corners]
    local = dot_high(partials, operator[...], NN)
    rows = pad(jnp.concatenate([local, local], axis=1))
    zero = jnp.zeros((z.columns, z.width), F32)
    sums = [zero] * (4 if step > 0 else 3)
    top = zero
    for i in range(z.blocks):
        value = image[i] - other[i] + fold(dot(rows, jump_lift[i], NN))
        product[i] = value
        r, d = residual[i], direction[i]
        pairs = [(r, r), (d, value), (r, value)]
        if step > 0:
            scaled = scale * value
            pairs.append((scaled, scaled))
        else:
            top = jnp.maximum(top, jnp.abs(value))
        sums = [s + a * b for s, (a, b) in zip(sums, pairs)]
    more = []
    if step == 0:
        top = jnp.max(top, axis=1, keepdims=True)
        shrink = jnp.where(top > 0.0, 1.0 / top, 0.0)
        squares = zero
        for i in range(z.blocks):
            value = product[i] * shrink
            squares = squares + value * value
        sums.append(squares)
        more.append((PP * z.columns + LANES // 2, top))
    row = to_row(z, [(k * z.columns, lane_sum(v)) for k, v in enumerate(sums)] + more)
    for k in range(sent.shape[0]):
        sent[k] = row


def finish(z, gathered, before, residual_in, direction, product, previous, multipliers, residual):
    alpha, _ = scalars(z, gathered, previous[...])
    for i in range(z.blocks):
        for h in range(z.halves):
            part = slice(h * LANES, (h + 1) * LANES)
            multipliers[:, i, part] = before[i, :, part] + alpha * direction[i, :, part]
            residual[:, i, part] = residual_in[i, :, part] - alpha * product[i, :, part]


def call(body, outs, scratch, cost, args, table=True, away=()):
    args = [
        pltpu.with_memory_space_constraint(a, pltpu.HBM) if k in away else a
        for k, a in enumerate(args)
    ]
    specs = [HBM if k in away else VMEM for k in range(len(args))]
    if table:
        specs[0] = SMEM
    shapes = [
        pltpu.SMEM(s, t) if t == jnp.int32 else jax.ShapeDtypeStruct(s, t) for s, t in outs
    ]
    return pl.pallas_call(
        body,
        out_shape=shapes,
        in_specs=specs,
        out_specs=[SMEM if t == jnp.int32 else VMEM for _, t in outs],
        scratch_shapes=scratch,
        compiler_params=pltpu.CompilerParams(vmem_limit_bytes=LIMIT),
        cost_estimate=pl.CostEstimate(flops=cost, bytes_accessed=cost // 16, transcendentals=0),
    )(*args)


def on_device(
    load,
    row_scale,
    diag_blocks,
    off_blocks,
    off_pattern,
    partner,
    corner_coupling,
    corner_index,
    coarse_inverse,
    *,
    mesh,
):
    z = Sizes(load, corner_coupling, coarse_inverse, mesh)
    cols, blocks, width = z.columns, z.blocks, z.width
    field = ((blocks, cols, width), F32)
    other = pltpu.VMEM((blocks + 1, cols, width), F32)
    extra = ((cols, z.extra), F32)
    light, heavy = 4_000_000, 600_000_000

    def shape(rows, kinds):
        return ((rows + (z.extra_chunks if kinds == 1 else 0), cols, LANES), F32)

    def kernel(body, *extra_args):
        return functools.partial(body, z, *extra_args)

    def across(piece, mask_of):
        pairs = [(t, t ^ mask_of(t & 1)) for t in range(z.peers)]
        return lax.ppermute(piece, "sub", pairs)

    def to_near(piece):
        return across(piece, lambda core: 1)

    def exchange(kinds, sources, near):
        *pieces, beside = call(
            kernel(relay, kinds),
            [shape(2 * z.rows(kinds), kinds)] * (len(z.far) + 1), [], light, [table, *sources, near],
        )
        far = [across(piece, lambda core: z.far[z.at(k, core)]) for k, piece in enumerate(pieces)]
        return [*far, to_near(beside)]

    table, loaded, lift, wide, corners, near = call(
        kernel(begin),
        [((z.table,), jnp.int32), field, field, field, ((2 * z.corners, blocks * width), BF16)]
        + [shape(z.near_rows(2), 2)],
        [
            pltpu.VMEM(load.shape, F32),
            pltpu.VMEM(row_scale.shape, F32),
            pltpu.VMEM(corner_coupling.shape, BF16),
            pltpu.SMEM(partner.shape, jnp.int32),
            pltpu.SMEM(off_pattern.shape, jnp.int32),
            pltpu.SMEM((z.peers,), jnp.int32),
            pltpu.SemaphoreType.DMA((5,)),
        ],
        light,
        [partner, off_pattern, load, row_scale, corner_coupling],
        False, range(5),
    )
    arrived = exchange(2, [loaded, lift], to_near(near))
    weight = (diag_blocks.shape, BF16)
    operator, diag, off = call(
        kernel(prepare), [((z.all_corners, z.all_corners), F32), weight, weight],
        [
            pltpu.VMEM(corner_index.shape, jnp.int32),
            pltpu.VMEM(coarse_inverse.shape, F32),
            pltpu.SemaphoreType.DMA((4,)),
        ],
        heavy, [corner_index, coarse_inverse, diag_blocks, off_blocks], False, range(4),
    )
    half = ((blocks, 2 * cols, width), BF16)
    tile = ((cols, LANES), F32)
    devices = z.groups * z.peers
    fixed = [wide, diag, off, corners]
    multipliers = alpha = None
    for step in range(ITERS):
        early = [field, half, extra, shape(z.near_rows(1), 1)]
        if step == 0:
            residual, part, parts, own_extra, near = call(
                kernel(first_half, step), [field] + early, [other], heavy,
                [table, *fixed, *arrived, loaded],
            )
            direction = residual
            older = []
        else:
            way = direction
            residual, direction, alpha, part, parts, own_extra, near = call(
                kernel(first_half, step), [field, field, tile] + early, [], heavy,
                [table, *fixed, gathered, residual, way, product] + [alpha] * (step > 1),
            )
            older = [alpha, way] + [multipliers] * (step > 1)
        near = to_near(near)
        image, *more = call(
            kernel(second_half, step), [field] + [field] * (step > 0), [], heavy,
            [table, wide, diag, off, parts, part, *older],
        )
        if more:
            (multipliers,) = more
        if step == 0:
            (jump_lift,) = call(
                kernel(build_lift), [((blocks, 2 * z.all_corners, width), BF16)],
                [other, pltpu.VMEM((blocks, z.all_corners, width), F32)], heavy,
                [table, lift, *arrived],
            )
        arrived = exchange(1, [image, own_extra], near)
        product, sent = call(
            kernel(finish_product, step), [field, ((devices, 1, LANES), F32)], [other], heavy,
            [table, operator, image, own_extra, jump_lift, residual, direction, near]
            + [alpha] * (step > 0) + arrived,
        )
        gathered = lax.all_to_all(sent, ("group", "sub"), 0, 0, tiled=True)
    multipliers, residual = call(
        kernel(finish), [(load.shape, F32)] * 2, [], light,
        [gathered, multipliers, residual, direction, product, alpha], False,
    )
    return multipliers, residual


def solution(mesh):
    return jax.shard_map(
        functools.partial(on_device, mesh=dict(mesh.shape)),
        mesh=mesh,
        in_specs=(
            P(None, ("group", "sub"), None),
            P(("group", "sub"), None),
            P(("group", "sub"), None, None),
            P(("group", "sub"), None, None),
            P(("group", "sub"), None),
            P(("group", "sub"), None),
            P(("group", "sub"), None),
            P("group", None),
            P("group", None),
        ),
        out_specs=(P(None, ("group", "sub"), None), P(None, ("group", "sub"), None)),
        check_vma=False,
    )
```
